32 devices in a mesh: dp: 4 (over z), ep: 2 (over core), tp: 4 (over y, x).
Axes of the slice: x: 2, y: 2, z: 4, core: 2. Of those that a mesh axis runs over, the one named last changes fastest.
Arguments:
- activations: bfloat16 [4096, 1536], P(('dp', 'ep', 'tp')), may hold values from -6 to 6
- segments: int32 [8, 512], P(('dp', 'ep')), may hold values from 0 to 3, never falling along the last dimension, each value on 1 to 256 neighbouring positions
- routes: int32 [4096, 8], P(('dp', 'ep', 'tp')), may hold values from 0 to 19, all different within a row; in each aligned block of 128 rows (0 to 127, 128 to 255, ...) at most 52 rows name the same one
- attn_gain: float32 [1536], replicated, may hold values from 0.25 to 1.75
- w_query: bfloat16 [1536, 1536], P(None, 'tp'), may hold values from -0.15625 to 0.15625
- key_value_weight: bfloat16 [1536, 8, 128], P(None, 'tp'), may hold values from -0.15625 to 0.15625
- w_output: bfloat16 [1536, 1536], P('tp'), may hold values from -0.625 to 0.625
- moe_gain: float32 [1536], replicated, may hold values from 0.25 to 1.75
- w_router: bfloat16 [1536, 20], replicated, may hold values from -0.079589844 to 0.079589844
- w_in: bfloat16 [20, 2, 512, 1536], P('ep', None, 'tp'), may hold values from -0.15625 to 0.15625
- w_out: bfloat16 [20, 512, 1536], P('ep', 'tp'), may hold values from -1 to 1
- out_cotangent: bfloat16 [4096, 1536], P(('dp', 'ep', 'tp')), may hold values from -8 to 8
Outputs:
- block_out: bfloat16 [4096, 1536], P(('dp', 'ep', 'tp'))
- grad_input: float32 [4096, 1536], P(('dp', 'ep', 'tp'))
- grad_attn_gain: float32 [1536], replicated
- grad_w_query: float32 [1536, 1536], P(('dp', 'ep'), 'tp')
- grad_w_keyval: float32 [1536, 8, 128], P(('dp', 'ep'), 'tp')
- grad_w_output: float32 [1536, 1536], P('tp', ('dp', 'ep'))
- grad_moe_gain: float32 [1536], replicated
- grad_w_router: float32 [1536, 20], replicated
- grad_w_in: float32 [20, 2, 512, 1536], P('ep', None, 'tp', 'dp')
- grad_w_out: float32 [20, 512, 1536], P('ep', 'tp', 'dp')
The draws below stay inside these ranges and needn't reach their ends.
Inputs may be any that keep to these rules, and one draw needn't show every extreme that they name: `segments`: along each sequence the numbers never fall; no document is longer than 256 positions and some document reaches that length. A token's 8 experts differ. Within the routes of one device's tokens (aligned blocks of 128 rows) no expert is named more than 52 times, a bound that some block reaches.
All inputs are finite; a program needn't handle non-finite values.
Results may differ from the reference program's by a relative error of at most 0.023.
Values may be sent and summed in bfloat16 or wider, within the bound.
A program may use at most 256 MiB of HBM per device.

```python
import math
import jax
import jax.numpy as jnp
import numpy as np
from jax import lax

MODEL_WIDTH = 1536
QUERY_HEADS = 24
KEY_VALUE_HEADS = 8
HEAD_WIDTH = 64
FF = 512
TOP = 8
PACKED_LENGTH = 512
EXPERTS = 20
ROWS = 128
CAP = 52
GROUPS = 8
TOKENS = 4096
DOCS = 4
N_TP = 4


def spiked(values, rng, source, target, parts, factor):
    owner, partner = [(jnp.arange(values.shape[dim]) // (values.shape[dim] // parts)).reshape([-1 if axis == dim else 1 for axis in range(values.ndim)]) for dim in (source, target)]
    chosen = jax.random.permutation(rng, parts)[partner]
    strong = (owner == chosen) | (owner == (partner + parts // 2) % parts)
    return jnp.where(strong, factor * values, values)


def levels(key, extent, split, low, high):
    def one(axis_at, parts):
        heights = jax.random.uniform(jax.random.fold_in(jax.random.fold_in(key, 6), axis_at), (parts,), jnp.float32, low / len(split), high / len(split))
        return jnp.repeat(jnp.exp(heights), extent[axis_at] // parts).reshape((-1,) + (1,) * (len(extent) - axis_at - 1))

    gain = one(*split[0])
    for cut in split[1:]:
        gain = gain * one(*cut)
    return gain


def length_profile(count, total, bound, lean):
    portions = [(1 << 20) // math.isqrt(standing ** lean) + 1 for standing in range(2, count + 1)]
    rest, counts = total - bound - (count - 1), [1] * (count - 1)
    while rest > 0:
        candidates = [i for i in range(count - 1) if counts[i] < bound]
        whole, left = sum([portions[i] for i in candidates]), rest
        for i in candidates:
            more = min(bound - counts[i], max(1, left * portions[i] // whole), rest)
            counts[i] = counts[i] + more
            rest = rest - more
    return np.array([bound] + counts)


def uneven_parts(key, number_of, total, most, lean):
    if number_of == 2:
        one = jax.random.randint(key, (), max(1, total - most), min(most, total - 1) + 1)
        return jnp.stack([one, total - one])
    tallies = jnp.asarray(length_profile(number_of, total, most, lean), jnp.int32)
    couples = (number_of - 1) // 2
    source_of, sink = tallies[1:1 + 2 * couples:2], tallies[2:2 + 2 * couples:2]
    room = jnp.minimum(source_of - 1, most - sink)
    passed = jax.random.randint(jax.random.fold_in(key, 1), (couples,), 0, 1 << 20) % (room + 1)
    tallies = tallies.at[1:1 + 2 * couples:2].set(source_of - passed).at[2:2 + 2 * couples:2].set(sink + passed)
    return tallies[jax.random.permutation(jax.random.fold_in(key, 2), number_of)]


def shared_out(stream_key, own, number, rows, number_of, top, most, skew):
    sequence = jax.random.permutation(stream_key, number_of)
    packed, usual = portions_of(number_of, rows * top, most, skew, True), portions_of(number_of, rows * top, most, skew, False)
    places = jnp.arange(number_of)

    def named(tallies, rotation):
        used = int((tallies > 0).sum())
        fixed = max(1, used // 4)
        passed = fixed + (places - fixed + rotation * (used - fixed)) % max(1, number_of - fixed)
        return jnp.zeros((number_of,), jnp.int32).at[sequence[jnp.where(places < fixed, places, passed)]].set(jnp.asarray(tallies, jnp.int32))

    tallies = jnp.where(number % 4 == 0, named(packed, number // 4), named(usual, number - number // 4 - 1))
    mixed = jax.random.permutation(jax.random.fold_in(own, 3), number_of)
    donor, taker = mixed[0:number_of // 2 * 2:2], mixed[1:number_of // 2 * 2:2]
    margin = jnp.minimum(tallies[donor] - 1, most - tallies[taker]) // 2
    margin = jnp.where((donor == sequence[0]) | (taker == sequence[0]) | (tallies[taker] == 0), 0, jnp.maximum(margin, 0))
    passed = jax.random.randint(jax.random.fold_in(own, 4), (number_of // 2,), 0, 1 << 20) % (margin + 1)
    tallies = tallies.at[donor].add(-passed).at[taker].add(passed)
    items = jnp.searchsorted(jnp.cumsum(tallies), jnp.arange(rows * top), side="right").astype(jnp.int32)
    table = items.reshape(top, rows).T
    table = table[jax.random.permutation(jax.random.fold_in(own, 1), rows)]
    rotation = jax.random.randint(jax.random.fold_in(own, 2), (rows, 1), 0, top)
    return jnp.take_along_axis(table, (jnp.arange(top)[None, :] + rotation) % top, axis=1)


def portions_of(count, total, most, slope, full):
    loads = [(1 << 20) // math.isqrt(grade ** slope) + 1 for grade in range(1, count + 1)]
    largest = most if full else min(most, max(-(-total // count), total * loads[0] // sum(loads)))
    least = 1 if total - largest >= count - 1 else 0
    counts, surplus = [largest] + [least] * (count - 1), total - largest - least * (count - 1)
    while surplus > 0:
        movable = [i for i in range(1, count) if counts[i] < largest] or [i for i in range(1, count) if counts[i] < most]
        pool, remaining = sum([loads[i] for i in movable]), surplus
        for i in movable:
            addition = min(most - counts[i], max(1, remaining * loads[i] // pool), surplus)
            counts[i] = counts[i] + addition
            surplus = surplus - addition
    return np.array(counts)


def noise(key, dims, scale, reach, shards=(), held_as=jnp.bfloat16):
    entries = scale * jax.random.normal(key, dims, jnp.float32)
    if shards:
        entries = entries * levels(key, dims, shards, -0.22, 0.18)
    return jnp.clip(entries, -reach, reach).astype(held_as)


def bell_draw_with(key, extent, scale, most, split, heavy, kind=jnp.bfloat16):
    result = scale * jax.random.normal(key, extent, jnp.float32)
    if split:
        result = result * levels(key, extent, split, -0.22, 0.18)
    return jnp.clip(spiked(result, jax.random.fold_in(key, 3), *heavy), -most, most).astype(kind)


def setup_inputs(seed: int = 0) -> dict:
    seeds = jax.random.split(jax.random.key(seed), 13)
    activations = noise(seeds[0], (TOKENS, MODEL_WIDTH), 1.0, 6.0, ((0, 32),))
    segments = jax.vmap(lambda own: jnp.searchsorted(jnp.cumsum(uneven_parts(own, DOCS, PACKED_LENGTH, PACKED_LENGTH // 2, 2)), jnp.arange(PACKED_LENGTH), side="right"))(jax.random.split(seeds[1], GROUPS)).reshape((GROUPS, PACKED_LENGTH)).astype(jnp.int32)
    routes_keys = jax.random.split(jax.random.fold_in(seeds[2], 1), TOKENS // ROWS)
    routes_turns = jax.random.permutation(jax.random.fold_in(seeds[2], 3), TOKENS // ROWS)
    routes = jax.vmap(lambda own, number: shared_out(jax.random.fold_in(seeds[2], 2), own, number, ROWS, EXPERTS, TOP, CAP, 1))(routes_keys, routes_turns).reshape((TOKENS, TOP))
    attn_gain = jnp.clip(1.0 + 0.15 * jax.random.normal(seeds[3], (MODEL_WIDTH,), jnp.float32), 0.25, 1.75)
    w_query = noise(seeds[4], (MODEL_WIDTH, QUERY_HEADS * HEAD_WIDTH), MODEL_WIDTH ** -0.5, 0.15625, ((1, 4),))
    key_value_weight = noise(seeds[5], (MODEL_WIDTH, KEY_VALUE_HEADS, 2 * HEAD_WIDTH), MODEL_WIDTH ** -0.5, 0.15625, ((1, 4),))
    w_output = noise(seeds[6], (QUERY_HEADS * HEAD_WIDTH, MODEL_WIDTH), (QUERY_HEADS * HEAD_WIDTH // 16) ** -0.5, 0.625, ((0, 4),))
    moe_gain = jnp.clip(1.0 + 0.15 * jax.random.normal(seeds[7], (MODEL_WIDTH,), jnp.float32), 0.25, 1.75)
    w_router = noise(seeds[8], (MODEL_WIDTH, EXPERTS), 0.0128, 0.079589844)
    w_in = noise(seeds[9], (EXPERTS, 2, FF, MODEL_WIDTH), MODEL_WIDTH ** -0.5, 0.15625, ((0, 2), (2, 4)))
    w_out = noise(seeds[10], (EXPERTS, FF, MODEL_WIDTH), (FF // 16) ** -0.5, 1.0, ((0, 2), (1, 4)))
    out_cotangent = bell_draw_with(seeds[11], (TOKENS, MODEL_WIDTH), 1.0, 8.0, ((0, 32),), (0, 1, 32, 2.75))
    return {"activations": activations, "segments": segments, "routes": routes, "attn_gain": attn_gain, "w_query": w_query, "key_value_weight": key_value_weight, "w_output": w_output, "moe_gain": moe_gain, "w_router": w_router, "w_in": w_in, "w_out": w_out, "out_cotangent": out_cotangent}


eps_norm = 1e-05
rope_base = 10000.0
neg_fill = -1000000000.0
highest = lax.Precision.HIGHEST

@jax.custom_vjp
def low(v):
    return lax.optimization_barrier(v.astype(jnp.bfloat16)).astype(jnp.float32)

@jax.custom_vjp
def low_back(v):
    return v

def low_keep(v):
    return (low(v), None)

def low_pass(kept, grad):
    return (grad,)

def back_keep(v):
    return (v, None)

def back_low(kept, grad):
    return (low(grad),)
low.defvjp(low_keep, low_pass)
low_back.defvjp(back_keep, back_low)

def rope_tables(length, head_size):
    half_size = head_size // 2
    frequency = jnp.exp(jnp.arange(half_size, dtype=jnp.float32) * (-2.0 * math.log(rope_base) / head_size))
    angles = jnp.arange(length, dtype=jnp.float32)[:, None] * frequency[None, :]
    return (jnp.cos(angles)[:, None, :], jnp.sin(angles)[:, None, :])

def apply_rotation(tensor, cosine_rows, sine_rows):
    half_size = tensor.shape[-1] // 2
    first = tensor[..., :half_size]
    second = tensor[..., half_size:]
    return jnp.concatenate([first * cosine_rows - second * sine_rows, second * cosine_rows + first * sine_rows], axis=-1)

def normalize(matrix):
    return matrix * lax.rsqrt(lax.optimization_barrier(jnp.mean(matrix * matrix, axis=-1, keepdims=True)) + eps_norm)

def slot_tables(route_ids):
    blocks = route_ids.reshape(N_TP, ROWS * TOP)
    hot_table = (blocks[:, :, None] == jnp.arange(EXPERTS, dtype=jnp.int32)[None, None, :]).astype(jnp.int32)
    earlier = jnp.cumsum(hot_table, axis=1) - hot_table
    position = lax.optimization_barrier(jnp.sum(earlier * hot_table, axis=2))
    block_base = (jnp.arange(N_TP, dtype=jnp.int32) * CAP)[:, None]
    slot_of_route = (blocks * (N_TP * CAP) + block_base + position).reshape(PACKED_LENGTH * TOP).astype(jnp.int32)
    token_of_route = jnp.arange(PACKED_LENGTH * TOP, dtype=jnp.int32) // TOP
    token_of_slot = jnp.full((EXPERTS * N_TP * CAP,), PACKED_LENGTH, jnp.int32).at[slot_of_route].set(token_of_route)
    return (slot_of_route, token_of_slot)

def sequence_block(x_seq, doc_ids, route_ids, weights):
    attn_gain, w_query, key_value_weight, w_output, moe_gain, w_router, w_in, w_out = weights
    heads_per_group = QUERY_HEADS // KEY_VALUE_HEADS
    hat_one = normalize(x_seq)
    normed_one = low(hat_one * attn_gain)
    query_before_rotation = low_back(jnp.dot(normed_one, w_query, precision=highest))
    keyval_pre = low_back(jnp.einsum('sd,dhe->she', normed_one, key_value_weight, precision=highest))
    cosine_rows, sine_rows = rope_tables(PACKED_LENGTH, HEAD_WIDTH)
    query_vectors = low(apply_rotation(query_before_rotation.reshape(PACKED_LENGTH, QUERY_HEADS, HEAD_WIDTH), cosine_rows, sine_rows)).reshape(PACKED_LENGTH, KEY_VALUE_HEADS, heads_per_group, HEAD_WIDTH)
    keys_rot = low(apply_rotation(keyval_pre[:, :, :HEAD_WIDTH], cosine_rows, sine_rows))
    values = low(keyval_pre[:, :, HEAD_WIDTH:])
    positions = jnp.arange(PACKED_LENGTH)
    allowed = (doc_ids[:, None] == doc_ids[None, :]) & (positions[None, :] <= positions[:, None])
    scores = low_back(jnp.einsum('qhgd,khd->hgqk', query_vectors, keys_rot, precision=highest) * (1.0 / math.sqrt(HEAD_WIDTH)))
    probs = jax.nn.softmax(jnp.where(allowed, scores, neg_fill), axis=-1)
    attended = jnp.einsum('hgqk,khd->qhgd', low(probs), values, precision=highest).reshape(PACKED_LENGTH, QUERY_HEADS * HEAD_WIDTH)
    attended = low_back(low(attended))
    x_mid = x_seq + low_back(jnp.dot(attended, w_output, precision=highest))
    hat_two = normalize(x_mid)
    normed_two = low(hat_two * moe_gain)
    logits = low_back(jnp.dot(normed_two, w_router, precision=highest))
    gate_weights = jax.nn.softmax(jnp.take_along_axis(logits, route_ids, axis=1), axis=-1)
    slot_of_route, token_of_slot = slot_tables(route_ids)
    padded_rows = jnp.concatenate([normed_two, jnp.zeros((1, MODEL_WIDTH), jnp.float32)], axis=0)
    rows_in = padded_rows[token_of_slot].reshape(EXPERTS, N_TP * CAP, MODEL_WIDTH)

    def expert_apply(inputs):
        expert_rows, expert_in, expert_out = inputs
        gate_up = low_back(jnp.einsum('sd,jfd->sjf', expert_rows, expert_in, precision=highest))
        active = low(jax.nn.silu(gate_up[:, 0]) * gate_up[:, 1])
        shares = jnp.einsum('snf,nfd->snd', active.reshape(-1, N_TP, FF // N_TP), expert_out.reshape(N_TP, FF // N_TP, MODEL_WIDTH), precision=highest)
        return lax.optimization_barrier(jnp.sum(low_back(low(shares)), axis=1))
    outputs = lax.map(jax.checkpoint(expert_apply), (rows_in, w_in, w_out))
    route_rows = outputs.reshape(-1, MODEL_WIDTH)[slot_of_route].reshape(PACKED_LENGTH, TOP, MODEL_WIDTH)
    return x_mid + lax.optimization_barrier(jnp.sum(gate_weights[:, :, None] * route_rows, axis=1))

def reference(activations, segments, routes, attn_gain, w_query, key_value_weight, w_output, moe_gain, w_router, w_in, w_out, out_cotangent):
    params = (attn_gain.astype(jnp.float32), w_query.astype(jnp.float32), key_value_weight.astype(jnp.float32), w_output.astype(jnp.float32), moe_gain.astype(jnp.float32), w_router.astype(jnp.float32), w_in.astype(jnp.float32), w_out.astype(jnp.float32))
    route_groups = routes.reshape(GROUPS, PACKED_LENGTH, TOP)

    def layer(inputs, weights):

        def one_sequence(pieces):
            return sequence_block(pieces[0], pieces[1], pieces[2], weights)
        stacked = lax.map(jax.checkpoint(one_sequence), (inputs.reshape(GROUPS, PACKED_LENGTH, MODEL_WIDTH), segments, route_groups))
        return stacked.reshape(TOKENS, MODEL_WIDTH)
    layer_out, pullback = jax.vjp(layer, activations.astype(jnp.float32), params)
    grad_input, grads = pullback(out_cotangent.astype(jnp.float32))
    return (layer_out.astype(jnp.bfloat16), grad_input, grads[0], grads[1], grads[2], grads[3], grads[4], grads[5], grads[6], grads[7])
```

```python
import functools
import math

import jax
import jax.numpy as jnp
from jax import lax
from jax.experimental import pallas as pl
from jax.experimental.pallas import tpu as pltpu
from jax.sharding import PartitionSpec as P

eps_norm = 1e-05
rope_base = 10000.0
neg_fill = -1000000000.0
MESH = pl.DeviceIdType.MESH
bf16 = jnp.bfloat16
f32 = jnp.float32


def greet(partners):
    barrier = pltpu.get_barrier_semaphore()
    for partner in partners:
        pl.semaphore_signal(barrier, inc=1, device_id=partner, device_id_type=MESH)
    pl.semaphore_wait(barrier, len(partners))


def rows_at(start, count):
    return pl.ds(pl.multiple_of(start, count), count)


def gather_kernel(with_ep, block_ref, whole_ref, local_sem, send_sem, recv_sem):
    rows = block_ref.shape[0]
    half = rows // 2
    t, e = lax.axis_index("tp"), lax.axis_index("ep")
    near, far = {"tp": t ^ 1}, {"tp": t ^ 2}
    twin = {"ep": 1 - e}
    greet((near, far, twin) if with_ep else (near, far))
    tp = lax.axis_size("tp")
    base = e * (tp * rows) if with_ep else 0

    def place(tt, part, count):
        return whole_ref.at[rows_at(base + tt * rows + part * half, count)]

    def send(src, dst, k, device):
        copy = pltpu.make_async_remote_copy(
            src, dst, send_sem.at[k], recv_sem.at[k], device_id=device, device_id_type=MESH
        )
        copy.start()
        return copy

    def own(part):
        return block_ref.at[pl.ds(part * half, half)]

    local = pltpu.make_async_copy(block_ref, place(t, 0, rows), local_sem)
    near_a = send(own(0), place(t, 0, half), 0, near)
    far_b = send(own(1), place(t, 1, half), 1, far)
    near_b = send(own(1), place(t, 1, half), 2, near)
    far_a = send(own(0), place(t, 0, half), 3, far)
    local.start()
    copies = [near_a, far_b, near_b, far_a]
    if with_ep:
        twin_own = send(block_ref, place(t, 0, rows), 6, twin)
        copies.append(twin_own)
    near_a.wait_recv()
    on_a = send(place(t ^ 1, 0, half), place(t ^ 1, 0, half), 4, far)
    far_b.wait_recv()
    on_b = send(place(t ^ 2, 1, half), place(t ^ 2, 1, half), 5, near)
    near_b.wait_recv()
    far_a.wait_recv()
    if with_ep:
        twin_near = send(place(t ^ 1, 0, rows), place(t ^ 1, 0, rows), 7, twin)
        twin_far = send(place(t ^ 2, 0, rows), place(t ^ 2, 0, rows), 8, twin)
    on_a.wait_recv()
    on_b.wait_recv()
    if with_ep:
        twin_diag = send(place(t ^ 3, 0, rows), place(t ^ 3, 0, rows), 9, twin)
        for copy in (twin_own, twin_near, twin_far, twin_diag):
            copy.wait_recv()
        copies += [twin_near, twin_far, twin_diag]
    local.wait()
    for copy in copies + [on_a, on_b]:
        copy.wait_send()


def gather(block, with_ep, collective_id):
    rows, width = block.shape
    count = lax.axis_size("tp") * (lax.axis_size("ep") if with_ep else 1)
    return pl.pallas_call(
        functools.partial(gather_kernel, with_ep),
        out_shape=jax.ShapeDtypeStruct((count * rows, width), block.dtype),
        in_specs=[pl.BlockSpec(memory_space=pl.ANY)],
        out_specs=pl.BlockSpec(memory_space=pl.ANY),
        scratch_shapes=[
            pltpu.SemaphoreType.DMA,
            pltpu.SemaphoreType.DMA((10,)),
            pltpu.SemaphoreType.DMA((10,)),
        ],
        name="gather_plane" if with_ep else "gather_tp",
        cost_estimate=pl.CostEstimate(flops=0, bytes_accessed=40 * 10**6, transcendentals=0),
        compiler_params=pltpu.CompilerParams(
            collective_id=collective_id, has_side_effects=True, vmem_limit_bytes=16 * 2**20
        ),
    )(block)


def scatter_kernel(with_ep, part_ref, sum_ref, mine, twins, arrived, passed, local_sem, send_sem, recv_sem):
    rows = sum_ref.shape[0]
    half = rows // 2
    t, e = lax.axis_index("tp"), lax.axis_index("ep")
    tp = lax.axis_size("tp")
    near, far = {"tp": t ^ 1}, {"tp": t ^ 2}
    twin = {"ep": 1 - e}
    greet((near, far, twin) if with_ep else (near, far))
    base = e * (tp * rows) if with_ep else 0
    other = (1 - e) * (tp * rows)

    def send(src, dst, k, device):
        copy = pltpu.make_async_remote_copy(
            src, dst, send_sem.at[k], recv_sem.at[k], device_id=device, device_id_type=MESH
        )
        copy.start()
        return copy

    order = (3, 1, 2, 0)
    locals_, twin_copies = {}, {}
    for k in order:
        if with_ep:
            twin_copies[k] = send(
                part_ref.at[rows_at(other + (t ^ k) * rows, rows)], twins.at[k], k, twin
            )
        locals_[k] = pltpu.make_async_copy(
            part_ref.at[rows_at(base + (t ^ k) * rows, rows)], mine.at[k], local_sem.at[k]
        )
        locals_[k].start()

    def ready(k):
        locals_[k].wait()
        if with_ep:
            twin_copies[k].wait_recv()
            mine[k] = (mine[k].astype(f32) + twins[k].astype(f32)).astype(mine.dtype)

    first, second = pl.ds(0, half), pl.ds(half, half)
    ready(3)
    a_on = send(mine.at[3, first], arrived.at[0, 0], 4, near)
    b_on = send(mine.at[3, second], arrived.at[1, 0], 5, far)
    ready(1)
    a_own = send(mine.at[1, first], arrived.at[0, 1], 6, near)
    ready(2)
    b_own = send(mine.at[2, second], arrived.at[1, 1], 7, far)
    ready(0)
    a_on.wait_recv()
    mine[2, first] = (mine[2, first].astype(f32) + arrived[0, 0].astype(f32)).astype(mine.dtype)
    a_last = send(mine.at[2, first], passed.at[0], 8, far)
    b_on.wait_recv()
    mine[1, second] = (mine[1, second].astype(f32) + arrived[1, 0].astype(f32)).astype(mine.dtype)
    b_last = send(mine.at[1, second], passed.at[1], 9, near)
    a_own.wait_recv()
    b_own.wait_recv()
    a_last.wait_recv()
    sum_ref[first] = (
        mine[0, first].astype(f32) + arrived[0, 1].astype(f32) + passed[0].astype(f32)
    ).astype(sum_ref.dtype)
    b_last.wait_recv()
    sum_ref[second] = (
        mine[0, second].astype(f32) + arrived[1, 1].astype(f32) + passed[1].astype(f32)
    ).astype(sum_ref.dtype)
    copies = [a_on, b_on, a_own, b_own, a_last, b_last]
    if with_ep:
        copies += list(twin_copies.values())
    for copy in copies:
        copy.wait_send()


def scatter_sum(parts, with_ep, collective_id):
    count = lax.axis_size("tp") * (lax.axis_size("ep") if with_ep else 1)
    rows, width = parts.shape[0] // count, parts.shape[1]
    return pl.pallas_call(
        functools.partial(scatter_kernel, with_ep),
        out_shape=jax.ShapeDtypeStruct((rows, width), f32),
        in_specs=[pl.BlockSpec(memory_space=pl.ANY)],
        out_specs=pl.BlockSpec(memory_space=pltpu.VMEM),
        scratch_shapes=[
            pltpu.VMEM((4, rows, width), bf16),
            pltpu.VMEM((4, rows, width) if with_ep else (4, 16, 128), bf16),
            pltpu.VMEM((2, 2, rows // 2, width), bf16),
            pltpu.VMEM((2, rows // 2, width), bf16),
            pltpu.SemaphoreType.DMA((4,)),
            pltpu.SemaphoreType.DMA((10,)),
            pltpu.SemaphoreType.DMA((10,)),
        ],
        name="scatter_plane" if with_ep else "scatter_tp",
        cost_estimate=pl.CostEstimate(flops=0, bytes_accessed=40 * 10**6, transcendentals=0),
        compiler_params=pltpu.CompilerParams(
            collective_id=collective_id, has_side_effects=True, vmem_limit_bytes=24 * 2**20
        ),
    )(parts)


def halved_over_dp(blocks):
    dp = lax.axis_size("dp")
    d = lax.axis_index("dp")
    if dp & (dp - 1):
        return lax.psum_scatter(blocks, "dp", scatter_dimension=0, tiled=False).astype(f32)
    step = 1
    while step < dp:
        bit = (d // step) % 2
        pairs = blocks.reshape(-1, 2, *blocks.shape[1:])
        kept = lax.dynamic_index_in_dim(pairs, bit, 1, keepdims=False)
        given = lax.dynamic_index_in_dim(pairs, 1 - bit, 1, keepdims=False)
        got = lax.ppermute(given, "dp", [(i, i ^ step) for i in range(dp)])
        total = kept.astype(f32) + got.astype(f32)
        step *= 2
        blocks = total if step == dp else total.astype(bf16)
    return blocks[0]


def rope_tables(length, head_size):
    half_size = head_size // 2
    frequency = jnp.exp(
        jnp.arange(half_size, dtype=f32) * (-2.0 * math.log(rope_base) / head_size)
    )
    angles = jnp.arange(length, dtype=f32)[:, None] * frequency[None, :]
    return (jnp.cos(angles)[:, None, :], jnp.sin(angles)[:, None, :])


def apply_rotation(tensor, cosine_rows, sine_rows):
    half_size = tensor.shape[-1] // 2
    first = tensor[..., :half_size]
    second = tensor[..., half_size:]
    return jnp.concatenate(
        [first * cosine_rows - second * sine_rows, second * cosine_rows + first * sine_rows],
        axis=-1,
    )


def normalize(matrix):
    factor = lax.rsqrt(jnp.mean(matrix * matrix, axis=-1, keepdims=True) + eps_norm)
    return (matrix * factor, factor)


def norm_back(grad_normed, normed_hat, factor, gain):
    grad_hat = grad_normed * gain
    grad_inner = jnp.mean(grad_hat * normed_hat, axis=-1, keepdims=True)
    return (
        factor * (grad_hat - normed_hat * grad_inner),
        jnp.sum(grad_normed * normed_hat, axis=0),
    )


def dot(a, b, dims):
    return lax.dot_general(a, b, ((dims[:1], dims[1:]), ((), ())), preferred_element_type=f32)


def per_device(
    activations,
    segments,
    routes,
    attn_gain,
    w_query,
    key_value_weight,
    w_output,
    moe_gain,
    w_router,
    w_in,
    w_out,
    out_cotangent,
):
    row_count, width = activations.shape
    tp_count = lax.axis_size("tp")
    ep_count = lax.axis_size("ep")
    dp_count = lax.axis_size("dp")
    e_index = lax.axis_index("ep")
    seq_len = row_count * tp_count
    head_size = key_value_weight.shape[2] // 2
    kv_heads = key_value_weight.shape[1]
    q_heads = w_query.shape[1] // head_size
    heads_per_group = q_heads // kv_heads
    top_count = routes.shape[1]
    expert_count = w_router.shape[1]
    local_experts = w_in.shape[0]
    hidden = w_in.shape[2]
    score_scale = 1.0 / math.sqrt(head_size)

    routes_low = jnp.pad(routes.astype(bf16), ((0, 0), (0, 128 - top_count)), constant_values=255)
    plane_grad = lax.all_gather(
        jnp.concatenate([out_cotangent, routes_low], axis=1), ("ep", "tp"), axis=0, tiled=True
    )
    grad_rows = plane_grad[:, :width]
    plane_routes = plane_grad[:, width : width + top_count].astype(jnp.int32)

    cosine_rows, sine_rows = rope_tables(seq_len, head_size)
    x_float = activations.astype(f32)
    hat_one, factor_one = normalize(x_float)
    full_x = gather(activations, False, 0)
    full_rows = (normalize(full_x.astype(f32))[0] * attn_gain).astype(bf16)
    query_before_rotation = jnp.dot(full_rows, w_query, preferred_element_type=f32).reshape(
        seq_len, q_heads, head_size
    )
    keyval_pre = jnp.einsum("sd,dhe->she", full_rows, key_value_weight, preferred_element_type=f32)
    query_vectors = (
        apply_rotation(query_before_rotation, cosine_rows, sine_rows)
        .astype(bf16)
        .reshape(seq_len, kv_heads, heads_per_group, head_size)
    )
    keys_rot = apply_rotation(keyval_pre[:, :, :head_size], cosine_rows, sine_rows).astype(bf16)
    values = keyval_pre[:, :, head_size:].astype(bf16)
    positions = jnp.arange(seq_len)
    doc_ids = segments[0]
    allowed = (doc_ids[:, None] == doc_ids[None, :]) & (positions[None, :] <= positions[:, None])

    def masked_scores():
        raw_scores = (
            jnp.einsum("qhgd,khd->hgqk", query_vectors, keys_rot, preferred_element_type=f32)
            * score_scale
        )
        return jnp.where(allowed, raw_scores, neg_fill)

    scores = masked_scores()
    peak_score = jnp.max(scores, axis=-1, keepdims=True)
    log_total = peak_score + jnp.log(jnp.sum(jnp.exp(scores - peak_score), axis=-1, keepdims=True))
    probs_low = jnp.exp(scores - log_total).astype(bf16)
    attended = jnp.einsum("hgqk,khd->qhgd", probs_low, values, preferred_element_type=f32)
    attended = attended.reshape(seq_len, q_heads * head_size).astype(bf16)
    x_mid = x_float + scatter_sum(
        jnp.dot(attended, w_output, preferred_element_type=f32).astype(bf16), False, 1
    )
    hat_two, factor_two = normalize(x_mid)
    normed_two = (hat_two * moe_gain).astype(bf16)
    rows_two = gather(normed_two, True, 2)

    logits = jnp.dot(rows_two, w_router, preferred_element_type=f32)
    experts = jnp.arange(expert_count, dtype=jnp.int32)
    used = jnp.any(plane_routes[:, :, None] == experts[None, None, :], axis=1)
    peak = jnp.max(jnp.where(used, logits, -jnp.inf), axis=-1, keepdims=True)
    weight = jnp.where(used, jnp.exp(jnp.where(used, logits - peak, 0.0)), 0.0)
    gates = weight / jnp.sum(weight, axis=-1, keepdims=True)
    local_gates = lax.dynamic_slice_in_dim(gates, e_index * local_experts, local_experts, 1)

    group = 2 if local_experts % 2 == 0 else 1
    tokens = rows_two.shape[0]
    mixed_all, grad_all, gate_terms, weight_grads = [], [], [], []
    for start in range(0, local_experts, group):
        now = slice(start, start + group)
        into = w_in[now].reshape(group * 2 * hidden, width)
        out_of = w_out[now].reshape(group * hidden, width)
        gate_up = dot(rows_two, into, (1, 1)).reshape(tokens, group, 2, hidden)
        gate_pre, up_pre = gate_up[:, :, 0], gate_up[:, :, 1]
        back = dot(grad_rows, out_of, (1, 1)).reshape(tokens, group, hidden)
        g = local_gates[:, now][:, :, None]
        sig = jax.nn.sigmoid(gate_pre)
        silu = gate_pre * sig
        active = silu * up_pre
        gate_terms.append(jnp.sum(active * back, axis=-1))
        mixed = (g * active).astype(bf16).reshape(tokens, group * hidden)
        grad_active = g * back
        grad_gate = grad_active * up_pre * sig * (1.0 + gate_pre * (1.0 - sig))
        grad_up = grad_active * silu
        grad_gate_up = (
            jnp.stack([grad_gate, grad_up], axis=2)
            .astype(bf16)
            .reshape(tokens, group * 2 * hidden)
        )
        mixed_all.append(mixed)
        grad_all.append(grad_gate_up)
        columns = width // dp_count
        grad_in = jnp.einsum(
            "tk,tcd->ckd",
            grad_gate_up,
            rows_two.reshape(tokens, dp_count, columns),
            preferred_element_type=f32,
        ).astype(bf16)
        grad_out = jnp.einsum(
            "tk,tcd->ckd",
            mixed,
            grad_rows.reshape(tokens, dp_count, columns),
            preferred_element_type=f32,
        ).astype(bf16)
        weight_grads.append(halved_over_dp(jnp.concatenate([grad_in, grad_out], axis=1)))
    mixed_all = jnp.concatenate(mixed_all, axis=1)
    grad_all = jnp.concatenate(grad_all, axis=1)
    local_terms = jnp.concatenate(gate_terms, axis=1)

    local_inner = jnp.sum(local_gates * local_terms, axis=-1, keepdims=True)
    all_terms = lax.dynamic_update_slice_in_dim(
        jnp.zeros_like(gates), local_terms, e_index * local_experts, 1
    )
    grad_logits = gates * (all_terms - local_inner)
    logits_high = grad_logits.astype(bf16)
    logits_rest = (grad_logits - logits_high.astype(f32)).astype(bf16)
    grad_rows_two = (
        dot(grad_all, w_in.reshape(-1, width), (1, 0))
        + dot(logits_high, w_router, (1, 1))
        + dot(logits_rest, w_router, (1, 1))
    )
    grad_w_router = dot(rows_two, logits_high, (0, 0)) + dot(rows_two, logits_rest, (0, 0))

    grad_normed_two = scatter_sum(grad_rows_two.astype(bf16), True, 3)
    grad_out = out_cotangent.astype(f32)
    grad_from_moe, grad_moe_gain = norm_back(grad_normed_two, hat_two, factor_two, moe_gain)
    grad_mid = grad_out + grad_from_moe
    grad_full = gather(grad_mid.astype(bf16), False, 4)
    expert_mix = scatter_sum(dot(mixed_all, w_out.reshape(-1, width), (1, 0)).astype(bf16), True, 5)
    block_out = (x_mid + expert_mix).astype(bf16)

    grad_attended = dot(grad_full, w_output, (1, 1)).astype(bf16)
    grad_w_output = dot(grad_full, attended, (0, 0)).astype(bf16)
    grad_heads = grad_attended.reshape(seq_len, kv_heads, heads_per_group, head_size)
    probs = jnp.exp(masked_scores() - log_total)
    grad_probs = jnp.einsum("qhgd,khd->hgqk", grad_heads, values, preferred_element_type=f32)
    row_inner = jnp.sum(probs * grad_probs, axis=-1, keepdims=True)
    grad_scores = (probs * (grad_probs - row_inner)).astype(bf16)
    grad_queries = (
        jnp.einsum("hgqk,khd->qhgd", grad_scores, keys_rot, preferred_element_type=f32)
        * score_scale
    )
    grad_keys = (
        jnp.einsum("hgqk,qhgd->khd", grad_scores, query_vectors, preferred_element_type=f32)
        * score_scale
    )
    grad_values = jnp.einsum(
        "hgqk,qhgd->khd", probs.astype(bf16), grad_heads, preferred_element_type=f32
    )
    grad_query_pre = apply_rotation(
        grad_queries.reshape(seq_len, q_heads, head_size), cosine_rows, -sine_rows
    )
    grad_query_pre = grad_query_pre.reshape(seq_len, q_heads * head_size).astype(bf16)
    grad_key_pre = apply_rotation(grad_keys, cosine_rows, -sine_rows)
    grad_keyval_pre = jnp.concatenate([grad_key_pre, grad_values], axis=-1).astype(bf16)
    grad_keyval_flat = grad_keyval_pre.reshape(seq_len, kv_heads * 2 * head_size)
    keyval_flat = key_value_weight.reshape(width, kv_heads * 2 * head_size)
    from_heads = dot(grad_query_pre, w_query, (1, 1)) + dot(grad_keyval_flat, keyval_flat, (1, 1))
    grad_normed_one = scatter_sum(from_heads.astype(bf16), False, 6)
    grad_w_query = dot(full_rows, grad_query_pre, (0, 0)).astype(bf16)
    grad_w_keyval = dot(full_rows, grad_keyval_flat, (0, 0)).astype(bf16)
    grad_from_attn, grad_attn_gain = norm_back(grad_normed_one, hat_one, factor_one, attn_gain)
    grad_input = grad_mid + grad_from_attn

    def over_dp_ep(matrix):
        blocks = matrix.reshape(dp_count, ep_count, -1, matrix.shape[1])
        kept = lax.dynamic_index_in_dim(blocks, e_index, 1, keepdims=False)
        given = lax.dynamic_index_in_dim(blocks, 1 - e_index, 1, keepdims=False)
        got = lax.ppermute(given, "ep", [(0, 1), (1, 0)])
        return halved_over_dp((kept.astype(f32) + got.astype(f32)).astype(bf16))

    grad_w_output = over_dp_ep(grad_w_output).T
    both = over_dp_ep(jnp.concatenate([grad_w_query, grad_w_keyval], axis=1))
    grad_w_query = both[:, : q_heads * head_size]
    grad_w_keyval = both[:, q_heads * head_size :].reshape(-1, kv_heads, 2 * head_size)

    summed = jnp.stack(weight_grads)
    grad_w_in = summed[:, : group * 2 * hidden].reshape(local_experts, 2, hidden, -1)
    grad_w_out = summed[:, group * 2 * hidden :].reshape(local_experts, hidden, -1)
    grad_attn_gain, grad_moe_gain, grad_w_router = lax.psum(
        (grad_attn_gain, grad_moe_gain, grad_w_router), ("dp", "ep", "tp")
    )
    return (
        block_out,
        grad_input,
        grad_attn_gain,
        grad_w_query,
        grad_w_keyval,
        grad_w_output,
        grad_moe_gain,
        grad_w_router,
        grad_w_in,
        grad_w_out,
    )


def solution(mesh):
    return jax.shard_map(
        per_device,
        mesh=mesh,
        in_specs=(
            P(("dp", "ep", "tp"), None),
            P(("dp", "ep"), None),
            P(("dp", "ep", "tp"), None),
            P(),
            P(None, "tp"),
            P(None, "tp", None),
            P("tp", None),
            P(),
            P(),
            P("ep", None, "tp", None),
            P("ep", "tp", None),
            P(("dp", "ep", "tp"), None),
        ),
        out_specs=(
            P(("dp", "ep", "tp"), None),
            P(("dp", "ep", "tp"), None),
            P(),
            P(("dp", "ep"), "tp"),
            P(("dp", "ep"), "tp", None),
            P("tp", ("dp", "ep")),
            P(),
            P(),
            P("ep", None, "tp", "dp"),
            P("ep", "tp", "dp"),
        ),
        check_vma=False,
    )
```

```python
import functools
import math

import jax
import jax.numpy as jnp
from jax import lax
from jax.experimental import pallas as pl
from jax.experimental.pallas import tpu as pltpu
from jax.sharding import PartitionSpec as P

eps_norm = 1e-05
rope_base = 10000.0
neg_fill = -1000000000.0
MESH = pl.DeviceIdType.MESH
bf16 = jnp.bfloat16
f32 = jnp.float32


def greet(partners):
    barrier = pltpu.get_barrier_semaphore()
    for partner in partners:
        pl.semaphore_signal(barrier, inc=1, device_id=partner, device_id_type=MESH)
    pl.semaphore_wait(barrier, len(partners))


def rows_at(start, count):
    return pl.ds(pl.multiple_of(start, count), count)


def gather_kernel(with_ep, block_ref, *refs):
    whole_ref, local_sem, send_sem, recv_sem = refs[-4:]
    rows = block_ref.shape[0]
    half = rows // 2
    t, e = lax.axis_index("tp"), lax.axis_index("ep")
    near, far = {"tp": t ^ 1}, {"tp": t ^ 2}
    twin = {"ep": 1 - e}
    greet((near, far, twin) if with_ep else (near, far))
    tp = lax.axis_size("tp")
    base = e * (tp * rows) if with_ep else 0

    def place(tt, part, count):
        return whole_ref.at[rows_at(base + tt * rows + part * half, count)]

    def send(src, dst, k, device):
        copy = pltpu.make_async_remote_copy(
            src, dst, send_sem.at[k], recv_sem.at[k], device_id=device, device_id_type=MESH
        )
        copy.start()
        return copy

    def own(part):
        return block_ref.at[pl.ds(part * half, half)]

    local = pltpu.make_async_copy(block_ref, place(t, 0, rows), local_sem)
    near_a = send(own(0), place(t, 0, half), 0, near)
    far_b = send(own(1), place(t, 1, half), 1, far)
    near_b = send(own(1), place(t, 1, half), 2, near)
    far_a = send(own(0), place(t, 0, half), 3, far)
    local.start()
    copies = [near_a, far_b, near_b, far_a]
    if with_ep:
        twin_own = send(block_ref, place(t, 0, rows), 6, twin)
        copies.append(twin_own)
    near_a.wait_recv()
    on_a = send(place(t ^ 1, 0, half), place(t ^ 1, 0, half), 4, far)
    far_b.wait_recv()
    on_b = send(place(t ^ 2, 1, half), place(t ^ 2, 1, half), 5, near)
    near_b.wait_recv()
    far_a.wait_recv()
    if with_ep:
        twin_near = send(place(t ^ 1, 0, rows), place(t ^ 1, 0, rows), 7, twin)
        twin_far = send(place(t ^ 2, 0, rows), place(t ^ 2, 0, rows), 8, twin)
    on_a.wait_recv()
    on_b.wait_recv()
    if with_ep:
        twin_diag = send(place(t ^ 3, 0, rows), place(t ^ 3, 0, rows), 9, twin)
        for copy in (twin_own, twin_near, twin_far, twin_diag):
            copy.wait_recv()
        copies += [twin_near, twin_far, twin_diag]
    local.wait()
    for copy in copies + [on_a, on_b]:
        copy.wait_send()


def gather(block, with_ep, collective_id, after=()):
    rows, width = block.shape
    count = lax.axis_size("tp") * (lax.axis_size("ep") if with_ep else 1)
    return pl.pallas_call(
        functools.partial(gather_kernel, with_ep),
        out_shape=jax.ShapeDtypeStruct((count * rows, width), block.dtype),
        in_specs=[pl.BlockSpec(memory_space=pl.ANY)] * (1 + len(after)),
        out_specs=pl.BlockSpec(memory_space=pl.ANY),
        scratch_shapes=[
            pltpu.SemaphoreType.DMA,
            pltpu.SemaphoreType.DMA((10,)),
            pltpu.SemaphoreType.DMA((10,)),
        ],
        name="gather_plane" if with_ep else "gather_tp",
        cost_estimate=pl.CostEstimate(flops=0, bytes_accessed=10**6, transcendentals=0),
        compiler_params=pltpu.CompilerParams(
            collective_id=collective_id, has_side_effects=True, vmem_limit_bytes=16 * 2**20
        ),
    )(block, *after)


def scatter_kernel(with_ep, part_ref, *refs):
    sum_ref, mine, twins, arrived, passed, local_sem, send_sem, recv_sem = refs[-8:]
    rows = sum_ref.shape[0]
    half = rows // 2
    t, e = lax.axis_index("tp"), lax.axis_index("ep")
    tp = lax.axis_size("tp")
    near, far = {"tp": t ^ 1}, {"tp": t ^ 2}
    twin = {"ep": 1 - e}
    greet((near, far, twin) if with_ep else (near, far))
    base = e * (tp * rows) if with_ep else 0
    other = (1 - e) * (tp * rows)

    def send(src, dst, k, device):
        copy = pltpu.make_async_remote_copy(
            src, dst, send_sem.at[k], recv_sem.at[k], device_id=device, device_id_type=MESH
        )
        copy.start()
        return copy

    order = (3, 1, 2, 0)
    locals_, twin_copies = {}, {}
    for k in order:
        if with_ep:
            twin_copies[k] = send(
                part_ref.at[rows_at(other + (t ^ k) * rows, rows)], twins.at[k], k, twin
            )
        locals_[k] = pltpu.make_async_copy(
            part_ref.at[rows_at(base + (t ^ k) * rows, rows)], mine.at[k], local_sem.at[k]
        )
        locals_[k].start()

    def ready(k):
        locals_[k].wait()
        if with_ep:
            twin_copies[k].wait_recv()
            mine[k] = (mine[k].astype(f32) + twins[k].astype(f32)).astype(mine.dtype)

    first, second = pl.ds(0, half), pl.ds(half, half)
    ready(3)
    a_on = send(mine.at[3, first], arrived.at[0, 0], 4, near)
    b_on = send(mine.at[3, second], arrived.at[1, 0], 5, far)
    ready(1)
    a_own = send(mine.at[1, first], arrived.at[0, 1], 6, near)
    ready(2)
    b_own = send(mine.at[2, second], arrived.at[1, 1], 7, far)
    ready(0)
    a_on.wait_recv()
    mine[2, first] = (mine[2, first].astype(f32) + arrived[0, 0].astype(f32)).astype(mine.dtype)
    a_last = send(mine.at[2, first], passed.at[0], 8, far)
    b_on.wait_recv()
    mine[1, second] = (mine[1, second].astype(f32) + arrived[1, 0].astype(f32)).astype(mine.dtype)
    b_last = send(mine.at[1, second], passed.at[1], 9, near)
    a_own.wait_recv()
    b_own.wait_recv()
    a_last.wait_recv()
    sum_ref[first] = (
        mine[0, first].astype(f32) + arrived[0, 1].astype(f32) + passed[0].astype(f32)
    ).astype(sum_ref.dtype)
    b_last.wait_recv()
    sum_ref[second] = (
        mine[0, second].astype(f32) + arrived[1, 1].astype(f32) + passed[1].astype(f32)
    ).astype(sum_ref.dtype)
    copies = [a_on, b_on, a_own, b_own, a_last, b_last]
    if with_ep:
        copies += list(twin_copies.values())
    for copy in copies:
        copy.wait_send()


def scatter_sum(parts, with_ep, collective_id, after=()):
    count = lax.axis_size("tp") * (lax.axis_size("ep") if with_ep else 1)
    rows, width = parts.shape[0] // count, parts.shape[1]
    return pl.pallas_call(
        functools.partial(scatter_kernel, with_ep),
        out_shape=jax.ShapeDtypeStruct((rows, width), f32),
        in_specs=[pl.BlockSpec(memory_space=pl.ANY)] * (1 + len(after)),
        out_specs=pl.BlockSpec(memory_space=pltpu.VMEM),
        scratch_shapes=[
            pltpu.VMEM((4, rows, width), bf16),
            pltpu.VMEM((4, rows, width) if with_ep else (4, 16, 128), bf16),
            pltpu.VMEM((2, 2, rows // 2, width), bf16),
            pltpu.VMEM((2, rows // 2, width), bf16),
            pltpu.SemaphoreType.DMA((4,)),
            pltpu.SemaphoreType.DMA((10,)),
            pltpu.SemaphoreType.DMA((10,)),
        ],
        name="scatter_plane" if with_ep else "scatter_tp",
        cost_estimate=pl.CostEstimate(flops=0, bytes_accessed=10**6, transcendentals=0),
        compiler_params=pltpu.CompilerParams(
            collective_id=collective_id, has_side_effects=True, vmem_limit_bytes=24 * 2**20
        ),
    )(parts, *after)


def halve(blocks, step):
    dp = lax.axis_size("dp")
    bit = (lax.axis_index("dp") // step) % 2
    pairs = blocks.reshape(-1, 2, *blocks.shape[1:])
    kept = lax.dynamic_index_in_dim(pairs, bit, 1, keepdims=False)
    given = lax.dynamic_index_in_dim(pairs, 1 - bit, 1, keepdims=False)
    got = lax.ppermute(given, "dp", [(i, i ^ step) for i in range(dp)])
    total = kept.astype(f32) + got.astype(f32)
    return total if 2 * step == dp else total.astype(bf16)


def halved_over_dp(blocks):
    dp = lax.axis_size("dp")
    if dp & (dp - 1):
        return [lax.psum_scatter(blocks, "dp", scatter_dimension=0, tiled=False).astype(f32)]
    stages, step = [], 1
    while step < dp:
        blocks = halve(blocks, step)
        stages.append(blocks)
        step *= 2
    stages[-1] = stages[-1][0]
    return stages


def rows_back_kernel(count, gates_ref, terms_ref, in_ref, router_ref, *refs):
    back_refs, (rows_ref, logits_ref) = refs[:count], refs[-2:]
    gates, terms = gates_ref[...], terms_ref[...]
    logits = gates * (terms - jnp.sum(gates * terms, axis=0, keepdims=True))
    high = logits.astype(bf16)
    rows = logits.shape[0]
    logits_ref[:rows] = high
    logits_ref[rows:] = (logits - high.astype(f32)).astype(bf16)
    total = dot(logits_ref[...], router_ref[...], (0, 0))
    units = back_refs[0].shape[0]
    for k, back_ref in enumerate(back_refs):
        total += dot(back_ref[...], in_ref[k * units : (k + 1) * units], (0, 0))
    rows_ref[...] = total.astype(bf16)


def rows_back(gates, terms, backs, w_in, router_rows, carried=()):
    count, tokens = gates.shape
    width = w_in.shape[1]
    tile = 256 if tokens % 256 == 0 else tokens

    def whole(array):
        return pl.BlockSpec(array.shape, lambda i: (0, 0), pipeline_mode=pl.Buffered(1))

    def some(rows):
        return pl.BlockSpec((rows, tile), lambda i: (0, i))

    def body(*refs):
        ins = 4 + len(backs)
        outs = refs[ins + len(carried) :]
        rows_back_kernel(len(backs), *refs[:ins], *outs[:2])

    return pl.pallas_call(
        body,
        grid=(tokens // tile,),
        out_shape=[
            jax.ShapeDtypeStruct((tokens, width), bf16),
            jax.ShapeDtypeStruct((2 * count, tokens), bf16),
            *(jax.ShapeDtypeStruct(c.shape, c.dtype) for c in carried),
        ],
        in_specs=[
            some(count),
            some(count),
            whole(w_in),
            whole(router_rows),
            *(some(back.shape[0]) for back in backs),
            *([pl.BlockSpec(memory_space=pl.ANY)] * len(carried)),
        ],
        out_specs=[
            pl.BlockSpec((tile, width), lambda i: (i, 0)),
            some(2 * count),
            *([pl.BlockSpec(memory_space=pl.ANY)] * len(carried)),
        ],
        input_output_aliases={4 + len(backs) + k: 2 + k for k in range(len(carried))},
        name="rows_back",
        cost_estimate=pl.CostEstimate(flops=10**6, bytes_accessed=10**6, transcendentals=0),
        compiler_params=pltpu.CompilerParams(vmem_limit_bytes=32 * 2**20),
    )(gates, terms, w_in, router_rows, *backs, *carried)


def swapped(matrix, half):
    lane = lax.broadcasted_iota(jnp.int32, matrix.shape, 1)
    width = matrix.shape[1]
    return jnp.where(
        lane % (2 * half) < half,
        pltpu.roll(matrix, width - half, 1),
        pltpu.roll(matrix, half, 1),
    )


def rotated(matrix, tables, half, back):
    cosine, sine = tables
    times = matrix.shape[1] // cosine.shape[1]
    cosine, sine = (jnp.concatenate([t] * times, axis=1) for t in (cosine, sine))
    return matrix * cosine + swapped(matrix, half) * (-sine if back else sine)


def mask_into(bias_ref, column_ref, row_ref):
    shape = bias_ref.shape
    key = lax.broadcasted_iota(jnp.int32, shape, 0)
    query = lax.broadcasted_iota(jnp.int32, shape, 1)
    allowed = (column_ref[:, :1] == row_ref[:1]) & (key <= query)
    bias_ref[...] = jnp.where(allowed, 0.0, neg_fill)


def head_cuts(head, kv_heads, q_heads, size):
    group = head // (q_heads // kv_heads)
    return (
        slice(head * size, (head + 1) * size),
        slice(2 * group * size, (2 * group + 1) * size),
        slice((2 * group + 1) * size, (2 * group + 2) * size),
    )


def attention_kernel(
    size, scale, x_ref, gain_ref, query_ref, keyval_ref, out_ref, column_ref, row_ref, cos_ref, sin_ref,
    kcos_ref, ksin_ref, part_ref, rows_ref, q_ref, kv_ref, total_ref, attended_ref, bias_ref, turned_ref,
):
    x = x_ref[...].astype(f32)
    factor = lax.rsqrt(jnp.mean(x * x, axis=-1, keepdims=True) + eps_norm)
    rows_ref[...] = (x * factor * gain_ref[:1]).astype(bf16)
    rows = rows_ref[...]
    q = jnp.dot(rows, query_ref[...], preferred_element_type=f32)
    q_ref[...] = rotated(q, (cos_ref[...], sin_ref[...]), size // 2, False).astype(bf16)
    kv = jnp.dot(rows, keyval_ref[...], preferred_element_type=f32)
    kv_ref[...] = rotated(kv, (kcos_ref[...], ksin_ref[...]), size // 2, False).astype(bf16)
    mask_into(bias_ref, column_ref, row_ref)
    length = x.shape[0]
    tile = length // 2
    q_heads, kv_heads = q_ref.shape[1] // size, kv_ref.shape[1] // (2 * size)
    total_ref[...] = jnp.zeros_like(total_ref)
    for block in range(2):
        now, past = slice(block * tile, (block + 1) * tile), slice(0, (block + 1) * tile)
        for head in range(q_heads):
            at, key_at, value_at = head_cuts(head, kv_heads, q_heads, size)
            scores = dot(kv_ref[past, key_at], q_ref[now, at], (1, 1)) * scale + bias_ref[past, now]
            peak = jnp.max(scores, axis=0, keepdims=True)
            weight = jnp.exp(scores - peak)
            total = jnp.sum(weight, axis=0, keepdims=True)
            probs = (weight * (1.0 / total)).astype(bf16)
            total_ref[head : head + 1, now] = peak + jnp.log(total)
            turned_ref[at, now] = dot(kv_ref[past, value_at], probs, (0, 0))
    attended_ref[...] = turned_ref[...].T.astype(bf16)
    part_ref[...] = jnp.dot(
        attended_ref[...], out_ref[...], preferred_element_type=f32
    ).astype(bf16)


def attention_back_kernel(
    size, scale, grad_ref, out_ref, q_ref, kv_ref, total_ref, query_ref, keyval_ref, column_ref, row_ref,
    cos_ref, sin_ref, kcos_ref, ksin_ref, *refs,
):
    part_ref, pre_ref, bias_ref, turned_ref, kv_grad_ref, heads_ref = refs[-6:]
    mask_into(bias_ref, column_ref, row_ref)
    heads_ref[...] = dot(grad_ref[...], out_ref[...], (1, 1)).astype(bf16)
    length = q_ref.shape[0]
    tile = length // 2
    q_heads, kv_heads = q_ref.shape[1] // size, kv_ref.shape[1] // (2 * size)
    kv_grad_ref[...] = jnp.zeros_like(kv_grad_ref)
    for block in range(2):
        now, past = slice(block * tile, (block + 1) * tile), slice(0, (block + 1) * tile)
        for head in range(q_heads):
            at, key_at, value_at = head_cuts(head, kv_heads, q_heads, size)
            keys, query, grad = kv_ref[past, key_at], q_ref[now, at], heads_ref[now, at]
            scores = dot(keys, query, (1, 1)) * scale + bias_ref[past, now]
            probs = jnp.exp(scores - total_ref[head : head + 1, now])
            grad_probs = dot(kv_ref[past, value_at], grad, (1, 1))
            inner = jnp.sum(probs * grad_probs, axis=0, keepdims=True)
            grad_scores = (probs * (grad_probs - inner)).astype(bf16)
            turned_ref[at, now] = dot(keys, grad_scores, (0, 0)) * scale
            kv_grad_ref[past, key_at] += dot(grad_scores, query, (1, 0)) * scale
            kv_grad_ref[past, value_at] += dot(probs.astype(bf16), grad, (1, 0))
    width = q_ref.shape[1]
    pre_ref[:, :width] = rotated(turned_ref[...].T, (cos_ref[...], sin_ref[...]), size // 2, True).astype(bf16)
    pre_ref[:, width:] = rotated(
        kv_grad_ref[...], (kcos_ref[...], ksin_ref[...]), size // 2, True
    ).astype(bf16)
    part_ref[...] = (
        dot(pre_ref[:, :width], query_ref[...], (1, 1))
        + dot(pre_ref[:, width:], keyval_ref[...], (1, 1))
    ).astype(bf16)


def local_call(body, name, out_shape, scratch, args, after=(), limit=48):
    spec = pl.BlockSpec(memory_space=pltpu.VMEM)
    return pl.pallas_call(
        body,
        out_shape=out_shape,
        in_specs=[spec] * len(args) + [pl.BlockSpec(memory_space=pl.ANY)] * len(after),
        out_specs=jax.tree.map(lambda _: spec, out_shape),
        scratch_shapes=scratch,
        name=name,
        cost_estimate=pl.CostEstimate(flops=10**6, bytes_accessed=10**6, transcendentals=0),
        compiler_params=pltpu.CompilerParams(vmem_limit_bytes=limit * 2**20),
    )(*args, *after)


def held(array, after):
    def body(array_ref, _, out_ref):
        out_ref[...] = array_ref[...]

    return local_call(
        body, "held", jax.ShapeDtypeStruct(array.shape, array.dtype), [], (array,), (after,), limit=4
    )


def attention_weights_kernel(rows_ref, pre_ref, grad_ref, attended_ref, *outs):
    width, pre = rows_ref.shape[1], pre_ref.shape[1]
    parts = outs[0].shape[0] if len(outs) == 2 else 4
    d, e = lax.axis_index("dp"), lax.axis_index("ep")
    step = width // parts
    for c in range(parts):
        cut = slice(c * step, (c + 1) * step)
        first = dot(rows_ref[:, cut], pre_ref[...], (0, 0)).astype(bf16)
        second = dot(grad_ref[:, cut], attended_ref[...], (0, 0)).astype(bf16)
        if len(outs) == 1:
            outs[0][cut, :pre] = first
            outs[0][cut, pre:] = second
            continue
        for half in range(2):
            some = slice(half * (step // 2), (half + 1) * (step // 2))
            for mine in range(2):

                @pl.when((half == e) == (mine == 1))
                def _():
                    out_ref = outs[0] if mine else outs[1]
                    out_ref[d ^ c, :, :pre] = first[some]
                    out_ref[d ^ c, :, pre:] = second[some]


def mixed_rows(mixed, w_out, after=()):
    count = len(mixed)
    units, tokens = mixed[0].shape
    width = w_out.shape[1]
    tile = 256 if tokens % 256 == 0 else tokens

    def body(out_ref, *refs):
        total = dot(refs[0][...], out_ref[:units], (0, 0))
        for k in range(1, count):
            total += dot(refs[k][...], out_ref[k * units : (k + 1) * units], (0, 0))
        refs[-1][...] = total.astype(bf16)

    return pl.pallas_call(
        body,
        grid=(tokens // tile,),
        out_shape=jax.ShapeDtypeStruct((tokens, width), bf16),
        in_specs=[pl.BlockSpec(w_out.shape, lambda i: (0, 0), pipeline_mode=pl.Buffered(1))]
        + [pl.BlockSpec((units, tile), lambda i: (0, i))] * count
        + [pl.BlockSpec(memory_space=pl.ANY)] * len(after),
        out_specs=pl.BlockSpec((tile, width), lambda i: (i, 0)),
        name="mixed_rows",
        cost_estimate=pl.CostEstimate(flops=10**6, bytes_accessed=10**6, transcendentals=0),
        compiler_params=pltpu.CompilerParams(vmem_limit_bytes=24 * 2**20),
    )(w_out, *mixed, *after)


def add_blocks(kept, at, got, after=(), carried=()):
    count, rows, columns = got.shape
    tile = 128 if rows % 128 == 0 else rows
    half = jax.ShapeDtypeStruct((count // 2, rows, columns), bf16)
    half_spec = pl.BlockSpec((count // 2, tile, columns), lambda i: (0, i, 0))
    whole_spec = pl.BlockSpec((count, tile, columns), lambda i: (0, i, 0))
    elsewhere = [pl.BlockSpec(memory_space=pl.ANY)]

    def body(kept_ref, got_ref, *refs):
        outs = refs[len(after) + len(carried) :]
        for i in range(count):
            outs[i % 2][i // 2] = (kept_ref[0, i].astype(f32) + got_ref[i].astype(f32)).astype(bf16)

    return pl.pallas_call(
        body,
        grid=(rows // tile,),
        out_shape=[half, half] + [jax.ShapeDtypeStruct(c.shape, c.dtype) for c in carried],
        in_specs=[
            pl.BlockSpec((1, count, tile, columns), lambda i: (at, 0, i, 0)),
            whole_spec,
            *(elsewhere * (len(carried) + len(after))),
        ],
        out_specs=[half_spec, half_spec] + elsewhere * len(carried),
        input_output_aliases={2 + k: 2 + k for k in range(len(carried))},
        name="add_blocks",
        cost_estimate=pl.CostEstimate(flops=10**6, bytes_accessed=10**6, transcendentals=0),
        compiler_params=pltpu.CompilerParams(vmem_limit_bytes=16 * 2**20),
    )(kept, got, *carried, *after)


def place_pair(number, kept, got, grads, shapes, after=()):
    (experts_all, _, hidden, columns), _ = shapes
    pair = kept.shape[1] // (3 * hidden)

    def body(kept_ref, got_ref, *refs):
        into_ref, out_ref = refs[-2:]
        into = kept_ref[0, : 2 * pair * hidden].astype(f32) + got_ref[
            0, : 2 * pair * hidden
        ].astype(f32)
        into_ref[...] = into.reshape(pair, 2, hidden, columns)
        out = kept_ref[0, 2 * pair * hidden :].astype(f32) + got_ref[
            0, 2 * pair * hidden :
        ].astype(f32)
        out_ref[...] = out.reshape(pair, hidden, columns)

    block = pl.BlockSpec(kept.shape, lambda i: (0, 0, 0))
    return pl.pallas_call(
        body,
        grid=(1,),
        out_shape=[jax.ShapeDtypeStruct(shape, f32) for shape in shapes],
        in_specs=[block, block] + [pl.BlockSpec(memory_space=pl.ANY)] * (len(grads) + len(after)),
        out_specs=[
            pl.BlockSpec((pair, 2, hidden, columns), lambda i: (number, 0, 0, 0)),
            pl.BlockSpec((pair, hidden, columns), lambda i: (number, 0, 0)),
        ],
        input_output_aliases={2: 0, 3: 1} if grads else {},
        name="place_pair",
        cost_estimate=pl.CostEstimate(flops=10**6, bytes_accessed=10**6, transcendentals=0),
        compiler_params=pltpu.CompilerParams(vmem_limit_bytes=16 * 2**20),
    )(kept, got, *grads, *after)


def exchanged(blocks, step):
    return lax.ppermute(blocks, "dp", [(i, i ^ step) for i in range(lax.axis_size("dp"))])


def summed_everywhere(value):
    for axis in ("ep", "tp", "dp"):
        size, step = lax.axis_size(axis), 1
        if size & (size - 1):
            value = lax.psum(value, axis)
            continue
        while step < size:
            value = value + lax.ppermute(value, axis, [(i, i ^ step) for i in range(size)])
            step *= 2
    return value


def dot(a, b, dims):
    return lax.dot_general(a, b, ((dims[:1], dims[1:]), ((), ())), preferred_element_type=f32)


def experts_kernel(first, local_experts, *refs):
    if first == 0:
        rows_ref, grad_ref, router_ref, in_ref, out_ref = refs[:5]
        gates_ref, terms_ref, back_ref, mixed_ref, keep_ref, *give_refs = refs[5:]
    else:
        rows_ref, grad_ref, gates_ref, in_ref, out_ref = refs[:5]
        terms_in, terms_ref, back_ref, mixed_ref, keep_ref, *give_refs = refs[7:]
    tokens, width = rows_ref.shape
    pair, _, hidden, _ = in_ref.shape
    tile = 256 if tokens % 256 == 0 else tokens
    number = pl.program_id(0) + first

    if first == 0:
        logits = jnp.dot(rows_ref[...], router_ref[...], preferred_element_type=f32)
        used = grad_ref[:, width:].astype(f32) > 0.5
        peak = jnp.max(jnp.where(used, logits, -jnp.inf), axis=-1, keepdims=True)
        weight = jnp.where(used, jnp.exp(jnp.where(used, logits - peak, 0.0)), 0.0)
        gates = weight / jnp.sum(weight, axis=-1, keepdims=True)
        gates_ref[...] = gates.T[: gates_ref.shape[0]]
    if first == 0:
        terms_ref[...] = jnp.zeros_like(terms_ref)
    else:

        @pl.when(pl.program_id(0) == 0)
        def _():
            terms_ref[...] = terms_in[...]

    into = in_ref[...].reshape(pair * 2 * hidden, width)
    out_of = out_ref[...].reshape(pair * hidden, width)
    base = lax.axis_index("ep") * local_experts + number * pair

    @pl.loop(0, tokens // tile)
    def _(j):
        now = pl.ds(pl.multiple_of(j * tile, tile), tile)
        gate_up = dot(into, rows_ref[now, :], (1, 1))
        down = dot(out_of, grad_ref[now, :width], (1, 1))
        for k in range(pair):
            gate = gate_up[2 * k * hidden : (2 * k + 1) * hidden]
            up = gate_up[(2 * k + 1) * hidden : (2 * k + 2) * hidden]
            back = down[k * hidden : (k + 1) * hidden]
            g = gates_ref[pl.ds(base + k, 1), now]
            sig = 1.0 / (1.0 + jnp.exp(-gate))
            silu = gate * sig
            active = silu * up
            terms_ref[pl.ds(base + k, 1), now] = jnp.sum(active * back, axis=0, keepdims=True)
            mixed_ref[k * hidden : (k + 1) * hidden, now] = (g * active).astype(bf16)
            grad_active = g * back
            back_ref[2 * k * hidden : (2 * k + 1) * hidden, now] = (
                grad_active * up * (sig * (1.0 + gate * (1.0 - sig)))
            ).astype(bf16)
            back_ref[(2 * k + 1) * hidden : (2 * k + 2) * hidden, now] = (
                grad_active * silu
            ).astype(bf16)

    columns = keep_ref.shape[3]
    blocks = width // columns
    ins = pair * 2 * hidden
    for at in range(0, pair * 3 * hidden, pair * hidden):
        if at < ins:
            total = jnp.dot(
                back_ref[at : at + pair * hidden], rows_ref[...], preferred_element_type=f32
            )
        else:
            total = jnp.dot(mixed_ref[...], grad_ref[:, :width], preferred_element_type=f32)
        total = total.astype(bf16)
        if blocks == 1:
            keep_ref[0, 0, at : at + pair * hidden] = total
            continue
        for c in range(blocks):
            apart = c ^ lax.axis_index("dp")
            part = total[:, c * columns : (c + 1) * columns]

            @pl.when(apart % 2 == 0)
            def _():
                keep_ref[0, apart // 2, at : at + pair * hidden] = part

            @pl.when(apart % 2 == 1)
            def _():
                give_refs[0][0, apart // 2, at : at + pair * hidden] = part


def experts(first, count, blocks, rows_two, plane_grad, gates_or_router, w_in, w_out, earlier=()):
    local_experts, _, hidden, width = w_in.shape
    tokens = rows_two.shape[0]
    pair = 2 if local_experts % 2 == 0 else 1
    pairs = local_experts // pair
    gate_rows = -(-local_experts * lax.axis_size("ep") // 8) * 8

    spread = (max(blocks // 2, 1), pair * 3 * hidden, width // blocks)
    given = 1 if blocks > 1 else 0

    def whole(array):
        return pl.BlockSpec(array.shape, lambda i: (0,) * array.ndim, pipeline_mode=pl.Buffered(1))

    in_specs = [
        whole(rows_two),
        whole(plane_grad),
        whole(gates_or_router),
        pl.BlockSpec((pair, 2, hidden, width), lambda i: (i + first, 0, 0, 0)),
        pl.BlockSpec((pair, hidden, width), lambda i: (i + first, 0, 0)),
    ]
    if earlier:
        in_specs += [pl.BlockSpec(memory_space=pl.ANY)] * 2 + [whole(earlier[2])]
    out_shape = [
        jax.ShapeDtypeStruct((gate_rows, tokens), f32),
        jax.ShapeDtypeStruct((local_experts * 2 * hidden, tokens), bf16),
        jax.ShapeDtypeStruct((local_experts * hidden, tokens), bf16),
        jax.ShapeDtypeStruct((count, *spread), bf16),
    ] + [jax.ShapeDtypeStruct((count, *spread), bf16)] * given
    out_specs = [
        pl.BlockSpec((gate_rows, tokens), lambda i: (0, 0)),
        pl.BlockSpec((pair * 2 * hidden, tokens), lambda i: (i + first, 0)),
        pl.BlockSpec((pair * hidden, tokens), lambda i: (i + first, 0)),
        pl.BlockSpec((1, *spread), lambda i: (i, 0, 0, 0)),
    ] + [pl.BlockSpec((1, *spread), lambda i: (i, 0, 0, 0))] * given
    aliases = {}
    if first == 0:
        out_shape.insert(0, jax.ShapeDtypeStruct((gate_rows, tokens), f32))
        out_specs.insert(0, pl.BlockSpec((gate_rows, tokens), lambda i: (0, 0)))
    else:
        aliases = {5: 1, 6: 2}
    return pl.pallas_call(
        functools.partial(experts_kernel, first, local_experts),
        grid=(count,),
        out_shape=out_shape,
        in_specs=in_specs,
        out_specs=out_specs,
        input_output_aliases=aliases,
        name=f"experts_{first}",
        cost_estimate=pl.CostEstimate(
            flops=10**6, bytes_accessed=10**6, transcendentals=0
        ),
        compiler_params=pltpu.CompilerParams(vmem_limit_bytes=44 * 2**20),
    )(rows_two, plane_grad, gates_or_router, w_in, w_out, *earlier)


def rope_tables(length, head_size):
    half_size = head_size // 2
    frequency = jnp.exp(
        jnp.arange(half_size, dtype=f32) * (-2.0 * math.log(rope_base) / head_size)
    )
    angles = jnp.arange(length, dtype=f32)[:, None] * frequency[None, :]
    cosine, sine = jnp.cos(angles), jnp.sin(angles)
    one_cos = jnp.concatenate([cosine, cosine], axis=1)
    one_sin = jnp.concatenate([-sine, sine], axis=1)
    return (
        jnp.concatenate([one_cos, one_cos], axis=1),
        jnp.concatenate([one_sin, one_sin], axis=1),
        jnp.concatenate([one_cos, jnp.ones_like(one_cos)], axis=1),
        jnp.concatenate([one_sin, jnp.zeros_like(one_sin)], axis=1),
    )


def normalize(matrix):
    factor = lax.rsqrt(jnp.mean(matrix * matrix, axis=-1, keepdims=True) + eps_norm)
    return (matrix * factor, factor)


def norm_back(grad_normed, normed_hat, factor, gain):
    grad_hat = grad_normed * gain
    grad_inner = jnp.mean(grad_hat * normed_hat, axis=-1, keepdims=True)
    return (
        factor * (grad_hat - normed_hat * grad_inner),
        jnp.sum(grad_normed * normed_hat, axis=0),
    )


def per_device(
    activations,
    segments,
    routes,
    attn_gain,
    w_query,
    key_value_weight,
    w_output,
    moe_gain,
    w_router,
    w_in,
    w_out,
    out_cotangent,
):
    row_count, width = activations.shape
    tp_count = lax.axis_size("tp")
    ep_count = lax.axis_size("ep")
    dp_count = lax.axis_size("dp")
    e_index = lax.axis_index("ep")
    seq_len = row_count * tp_count
    head_size = key_value_weight.shape[2] // 2
    kv_heads = key_value_weight.shape[1]
    q_heads = w_query.shape[1] // head_size
    heads_per_group = q_heads // kv_heads
    top_count = routes.shape[1]
    expert_count = w_router.shape[1]
    local_experts = w_in.shape[0]
    hidden = w_in.shape[2]
    score_scale = 1.0 / math.sqrt(head_size)

    lanes = jnp.arange(128, dtype=jnp.int32)
    used = jnp.any(routes[:, :, None] == lanes[None, None, :], axis=1).astype(bf16)
    plane_grad = lax.all_gather(
        jnp.concatenate([out_cotangent, used], axis=1), ("ep", "tp"), axis=0, tiled=True
    )

    tables = rope_tables(seq_len, head_size)
    x_float = activations.astype(f32)
    hat_one, factor_one = normalize(x_float)
    full_x = gather(activations, False, 0)
    keyval_flat = key_value_weight.reshape(width, kv_heads * 2 * head_size)
    doc_column = jnp.broadcast_to(segments[0].astype(f32)[:, None], (seq_len, 128))
    doc_row = jnp.broadcast_to(segments.astype(f32), (8, seq_len))
    q_width, kv_width = q_heads * head_size, 2 * kv_heads * head_size
    attn_part, full_rows, query_rows, keyval_rows, log_total, attended = local_call(
        functools.partial(attention_kernel, head_size, score_scale),
        "attention",
        [
            jax.ShapeDtypeStruct((seq_len, width), bf16),
            jax.ShapeDtypeStruct((seq_len, width), bf16),
            jax.ShapeDtypeStruct((seq_len, q_width), bf16),
            jax.ShapeDtypeStruct((seq_len, kv_width), bf16),
            jax.ShapeDtypeStruct((-(-q_heads // 8) * 8, seq_len), f32),
            jax.ShapeDtypeStruct((seq_len, q_width), bf16),
        ],
        [pltpu.VMEM((seq_len, seq_len), f32), pltpu.VMEM((q_width, seq_len), f32)],
        (
            full_x,
            jnp.broadcast_to(attn_gain, (8, width)),
            w_query,
            keyval_flat,
            w_output,
            doc_column,
            doc_row,
            *tables,
        ),
    )
    x_mid = x_float + scatter_sum(attn_part, False, 1)
    hat_two, factor_two = normalize(x_mid)
    normed_two = (hat_two * moe_gain).astype(bf16)
    rows_two = gather(normed_two, True, 2)

    pair = 2 if local_experts % 2 == 0 else 1
    pairs = local_experts // pair
    columns = width // dp_count
    in_order = columns % 128 == 0 and dp_count > 1 and dp_count & (dp_count - 1) == 0
    blocks = dp_count if in_order else 1
    gates = jnp.pad(w_router, ((0, 0), (0, 128 - expert_count)))
    keeps, gives, earlier = [], [], ()
    for start, count in ((0, 1), (1, pairs - 1)):
        results = experts(start, count, blocks, rows_two, plane_grad, gates, w_in, w_out, earlier)
        if start == 0:
            gates, *results = results
        terms, back, mixed, keep, *give = results
        earlier = (back, mixed, terms)
        keeps += [(keep, k) for k in range(count)]
        gives += [part[k] for part in give for k in range(count)]

    arrived, halved = {}, {}

    def first(*numbers):
        for number in numbers:
            if in_order and number < pairs:
                arrived[number] = exchanged(gives[number], 1)

    def waiting(*numbers):
        return [number for number in numbers if in_order and number < pairs]

    def go_on(number, after=(), release=()):
        if not in_order or number >= pairs:
            return ()
        (keep, k), got, step, deps = keeps[number], arrived[number], 2, []
        release = waiting(*release)
        while step < dp_count:
            keep, give, *freed = add_blocks(keep, k, got, after, [gives[n] for n in release])
            keep, k = keep[None], 0
            for n, block in zip(release, freed):
                gives[n] = block
            first(*release)
            release = ()
            deps.append(give)
            got = exchanged(give, step)
            step *= 2
        halved[number] = (keep[0], got)
        return tuple(deps)

    def come(*numbers):
        return tuple(halved[number][1] for number in waiting(*numbers))

    first(*range(pairs))

    gate_rows = gates.shape[0]
    router_rows = jnp.pad(w_router.T, ((0, gate_rows - expert_count), (0, 0)))
    grad_rows_two, grad_logits = rows_back(
        gates,
        terms,
        [back],
        w_in.reshape(-1, width),
        jnp.concatenate([router_rows] * 2),
    )
    grad_w_router = dot(grad_logits, rows_two, (1, 0))
    grad_w_router = grad_w_router[:expert_count] + grad_w_router[gate_rows : gate_rows + expert_count]

    grad_normed_two = scatter_sum(grad_rows_two, True, 3, go_on(0))
    grad_out = out_cotangent.astype(f32)
    grad_from_moe, grad_moe_gain = norm_back(grad_normed_two, hat_two, factor_two, moe_gain)
    grad_mid = grad_out + grad_from_moe
    grad_full = gather(grad_mid.astype(bf16), False, 4, go_on(1, (grad_normed_two,)))

    heads_part, grad_pre = local_call(
        functools.partial(attention_back_kernel, head_size, score_scale),
        "attention_back",
        [
            jax.ShapeDtypeStruct((seq_len, width), bf16),
            jax.ShapeDtypeStruct((seq_len, q_width + kv_width), bf16),
        ],
        [
            pltpu.VMEM((seq_len, seq_len), f32),
            pltpu.VMEM((q_width, seq_len), f32),
            pltpu.VMEM((seq_len, kv_width), f32),
            pltpu.VMEM((seq_len, q_width), bf16),
        ],
        (
            grad_full,
            w_output,
            query_rows,
            keyval_rows,
            log_total,
            w_query,
            keyval_flat,
            doc_column,
            doc_row,
            *tables,
        ),
    )
    all_width = 2 * q_width + kv_width
    block = (dp_count, width // (dp_count * ep_count), all_width)
    attn_weights = local_call(
        attention_weights_kernel,
        "attention_weights",
        [jax.ShapeDtypeStruct(block, bf16)] * 2
        if in_order
        else [jax.ShapeDtypeStruct((width, all_width), bf16)],
        [],
        (full_rows, grad_pre, grad_full, attended),
    )
    grad_normed_one = scatter_sum(
        heads_part, False, 6, go_on(2, (grad_full,)) + come(0)
    )
    grad_from_attn, grad_attn_gain = norm_back(grad_normed_one, hat_one, factor_one, attn_gain)
    grad_input = grad_mid + grad_from_attn

    attn_given = ()
    if in_order:
        keep, give = attn_weights
        got = lax.ppermute(give, "ep", [(0, 1), (1, 0)])
        keep, give = add_blocks(keep[None], 0, got, (grad_normed_one,))
        got = exchanged(give, 1)
        attn_given = (give,)
    else:
        halves = attn_weights[0].reshape(dp_count, ep_count, -1, all_width)
        kept = lax.dynamic_index_in_dim(halves, e_index, 1, keepdims=False)
        given = lax.dynamic_index_in_dim(halves, 1 - e_index, 1, keepdims=False)
        got = lax.ppermute(given, "ep", [(0, 1), (1, 0)])
        attn_sum = halved_over_dp((kept.astype(f32) + got.astype(f32)).astype(bf16))[-1]
    expert_part = mixed_rows(
        [mixed], w_out.reshape(-1, width), go_on(3, (grad_normed_one,)) + (grad_normed_one,) + come(1) + attn_given
    )
    expert_mix = scatter_sum(expert_part, True, 5, come(2))
    block_out = (x_mid + expert_mix).astype(bf16)

    if in_order:
        step = 2
        while step < dp_count:
            keep, give = add_blocks(keep[None], 0, got, (expert_mix,))
            got = exchanged(give, step)
            step *= 2
        attn_sum = keep[0].astype(f32) + got[0].astype(f32)
    grad_w_query = attn_sum[:, :q_width]
    grad_w_keyval = attn_sum[:, q_width : q_width + kv_width].reshape(-1, kv_heads, 2 * head_size)
    grad_w_output = attn_sum[:, q_width + kv_width :].T


    shapes = [(local_experts, 2, hidden, columns), (local_experts, hidden, columns)]
    if in_order:
        for number in range(4, pairs):
            if number not in arrived:
                first(number)
            go_on(number, (expert_mix,))
        grads = ()
        for number in range(pairs):
            grads = place_pair(number, *halved[number], grads, shapes)
        grad_w_in, grad_w_out = grads
    else:
        summed = []
        for keep, k in keeps:
            parts = jnp.moveaxis(keep[k].reshape(-1, dp_count, columns), 1, 0)
            summed.append(halved_over_dp(parts)[-1])
        summed = jnp.stack(summed)
        ins = pair * 2 * hidden
        grad_w_in = summed[:, :ins].reshape(shapes[0])
        grad_w_out = summed[:, ins:].reshape(shapes[1])
    small = summed_everywhere(
        held(jnp.concatenate([grad_w_router, grad_moe_gain[None], grad_attn_gain[None]]), expert_mix)
    )
    grad_w_router = small[:expert_count].T
    grad_moe_gain, grad_attn_gain = small[expert_count], small[expert_count + 1]
    return (
        block_out,
        grad_input,
        grad_attn_gain,
        grad_w_query,
        grad_w_keyval,
        grad_w_output,
        grad_moe_gain,
        grad_w_router,
        grad_w_in,
        grad_w_out,
    )


def solution(mesh):
    return jax.shard_map(
        per_device,
        mesh=mesh,
        in_specs=(
            P(("dp", "ep", "tp"), None),
            P(("dp", "ep"), None),
            P(("dp", "ep", "tp"), None),
            P(),
            P(None, "tp"),
            P(None, "tp", None),
            P("tp", None),
            P(),
            P(),
            P("ep", None, "tp", None),
            P("ep", "tp", None),
            P(("dp", "ep", "tp"), None),
        ),
        out_specs=(
            P(("dp", "ep", "tp"), None),
            P(("dp", "ep", "tp"), None),
            P(),
            P(("dp", "ep"), "tp"),
            P(("dp", "ep"), "tp", None),
            P("tp", ("dp", "ep")),
            P(),
            P(),
            P("ep", None, "tp", "dp"),
            P("ep", "tp", "dp"),
        ),
        check_vma=False,
    )
```

```python
import functools
import math

import jax
import jax.numpy as jnp
from jax import lax
from jax.experimental import pallas as pl
from jax.experimental.pallas import tpu as pltpu
from jax.sharding import PartitionSpec as P

eps_norm = 1e-05
rope_base = 10000.0
neg_fill = -1000000000.0
MESH = pl.DeviceIdType.MESH
bf16 = jnp.bfloat16
f32 = jnp.float32


def greet(partners):
    barrier = pltpu.get_barrier_semaphore()
    for partner in partners:
        pl.semaphore_signal(barrier, inc=1, device_id=partner, device_id_type=MESH)
    pl.semaphore_wait(barrier, len(partners))


def rows_at(start, count):
    return pl.ds(pl.multiple_of(start, count), count)


def gather_kernel(with_ep, block_ref, *refs):
    whole_ref, local_sem, send_sem, recv_sem = refs[-4:]
    rows = block_ref.shape[0]
    half = rows // 2
    t, e = lax.axis_index("tp"), lax.axis_index("ep")
    near, far = {"tp": t ^ 1}, {"tp": t ^ 2}
    twin = {"ep": 1 - e}
    greet((near, far, twin) if with_ep else (near, far))
    tp = lax.axis_size("tp")
    base = e * (tp * rows) if with_ep else 0

    def place(tt, part, count):
        return whole_ref.at[rows_at(base + tt * rows + part * half, count)]

    def send(src, dst, k, device):
        copy = pltpu.make_async_remote_copy(
            src, dst, send_sem.at[k], recv_sem.at[k], device_id=device, device_id_type=MESH
        )
        copy.start()
        return copy

    def own(part):
        return block_ref.at[pl.ds(part * half, half)]

    local = pltpu.make_async_copy(block_ref, place(t, 0, rows), local_sem)
    near_a = send(own(0), place(t, 0, half), 0, near)
    far_b = send(own(1), place(t, 1, half), 1, far)
    near_b = send(own(1), place(t, 1, half), 2, near)
    far_a = send(own(0), place(t, 0, half), 3, far)
    local.start()
    copies = [near_a, far_b, near_b, far_a]
    if with_ep:
        twin_own = send(block_ref, place(t, 0, rows), 6, twin)
        copies.append(twin_own)
    near_a.wait_recv()
    on_a = send(place(t ^ 1, 0, half), place(t ^ 1, 0, half), 4, far)
    far_b.wait_recv()
    on_b = send(place(t ^ 2, 1, half), place(t ^ 2, 1, half), 5, near)
    near_b.wait_recv()
    far_a.wait_recv()
    if with_ep:
        twin_near = send(place(t ^ 1, 0, rows), place(t ^ 1, 0, rows), 7, twin)
        twin_far = send(place(t ^ 2, 0, rows), place(t ^ 2, 0, rows), 8, twin)
    on_a.wait_recv()
    on_b.wait_recv()
    if with_ep:
        twin_diag = send(place(t ^ 3, 0, rows), place(t ^ 3, 0, rows), 9, twin)
        for copy in (twin_own, twin_near, twin_far, twin_diag):
            copy.wait_recv()
        copies += [twin_near, twin_far, twin_diag]
    local.wait()
    for copy in copies + [on_a, on_b]:
        copy.wait_send()


def gather(block, with_ep, collective_id, after=()):
    rows, width = block.shape
    count = lax.axis_size("tp") * (lax.axis_size("ep") if with_ep else 1)
    return pl.pallas_call(
        functools.partial(gather_kernel, with_ep),
        out_shape=jax.ShapeDtypeStruct((count * rows, width), block.dtype),
        in_specs=[pl.BlockSpec(memory_space=pl.ANY)] * (1 + len(after)),
        out_specs=pl.BlockSpec(memory_space=pl.ANY),
        scratch_shapes=[
            pltpu.SemaphoreType.DMA,
            pltpu.SemaphoreType.DMA((10,)),
            pltpu.SemaphoreType.DMA((10,)),
        ],
        name="gather_plane" if with_ep else "gather_tp",
        cost_estimate=pl.CostEstimate(flops=0, bytes_accessed=10**6, transcendentals=0),
        compiler_params=pltpu.CompilerParams(
            collective_id=collective_id, has_side_effects=True, vmem_limit_bytes=16 * 2**20
        ),
    )(block, *after)


def scatter_kernel(with_ep, part_ref, *refs):
    sum_ref, mine, twins, arrived, passed, local_sem, send_sem, recv_sem = refs[-8:]
    rows = sum_ref.shape[0]
    half = rows // 2
    t, e = lax.axis_index("tp"), lax.axis_index("ep")
    tp = lax.axis_size("tp")
    near, far = {"tp": t ^ 1}, {"tp": t ^ 2}
    twin = {"ep": 1 - e}
    greet((near, far, twin) if with_ep else (near, far))
    base = e * (tp * rows) if with_ep else 0
    other = (1 - e) * (tp * rows)

    def send(src, dst, k, device):
        copy = pltpu.make_async_remote_copy(
            src, dst, send_sem.at[k], recv_sem.at[k], device_id=device, device_id_type=MESH
        )
        copy.start()
        return copy

    order = (3, 1, 2, 0)
    locals_, twin_copies = {}, {}
    for k in order:
        if with_ep:
            twin_copies[k] = send(
                part_ref.at[rows_at(other + (t ^ k) * rows, rows)], twins.at[k], k, twin
            )
        locals_[k] = pltpu.make_async_copy(
            part_ref.at[rows_at(base + (t ^ k) * rows, rows)], mine.at[k], local_sem.at[k]
        )
        locals_[k].start()

    def ready(k):
        locals_[k].wait()
        if with_ep:
            twin_copies[k].wait_recv()
            mine[k] = (mine[k].astype(f32) + twins[k].astype(f32)).astype(mine.dtype)

    first, second = pl.ds(0, half), pl.ds(half, half)
    ready(3)
    a_on = send(mine.at[3, first], arrived.at[0, 0], 4, near)
    b_on = send(mine.at[3, second], arrived.at[1, 0], 5, far)
    ready(1)
    a_own = send(mine.at[1, first], arrived.at[0, 1], 6, near)
    ready(2)
    b_own = send(mine.at[2, second], arrived.at[1, 1], 7, far)
    ready(0)
    a_on.wait_recv()
    mine[2, first] = (mine[2, first].astype(f32) + arrived[0, 0].astype(f32)).astype(mine.dtype)
    a_last = send(mine.at[2, first], passed.at[0], 8, far)
    b_on.wait_recv()
    mine[1, second] = (mine[1, second].astype(f32) + arrived[1, 0].astype(f32)).astype(mine.dtype)
    b_last = send(mine.at[1, second], passed.at[1], 9, near)
    a_own.wait_recv()
    b_own.wait_recv()
    a_last.wait_recv()
    sum_ref[first] = (
        mine[0, first].astype(f32) + arrived[0, 1].astype(f32) + passed[0].astype(f32)
    ).astype(sum_ref.dtype)
    b_last.wait_recv()
    sum_ref[second] = (
        mine[0, second].astype(f32) + arrived[1, 1].astype(f32) + passed[1].astype(f32)
    ).astype(sum_ref.dtype)
    copies = [a_on, b_on, a_own, b_own, a_last, b_last]
    if with_ep:
        copies += list(twin_copies.values())
    for copy in copies:
        copy.wait_send()


def scatter_sum(parts, with_ep, collective_id, after=()):
    count = lax.axis_size("tp") * (lax.axis_size("ep") if with_ep else 1)
    rows, width = parts.shape[0] // count, parts.shape[1]
    return pl.pallas_call(
        functools.partial(scatter_kernel, with_ep),
        out_shape=jax.ShapeDtypeStruct((rows, width), f32),
        in_specs=[pl.BlockSpec(memory_space=pl.ANY)] * (1 + len(after)),
        out_specs=pl.BlockSpec(memory_space=pltpu.VMEM),
        scratch_shapes=[
            pltpu.VMEM((4, rows, width), bf16),
            pltpu.VMEM((4, rows, width) if with_ep else (4, 16, 128), bf16),
            pltpu.VMEM((2, 2, rows // 2, width), bf16),
            pltpu.VMEM((2, rows // 2, width), bf16),
            pltpu.SemaphoreType.DMA((4,)),
            pltpu.SemaphoreType.DMA((10,)),
            pltpu.SemaphoreType.DMA((10,)),
        ],
        name="scatter_plane" if with_ep else "scatter_tp",
        cost_estimate=pl.CostEstimate(flops=0, bytes_accessed=10**6, transcendentals=0),
        compiler_params=pltpu.CompilerParams(
            collective_id=collective_id, has_side_effects=True, vmem_limit_bytes=24 * 2**20
        ),
    )(parts, *after)


def halve(blocks, step):
    dp = lax.axis_size("dp")
    bit = (lax.axis_index("dp") // step) % 2
    pairs = blocks.reshape(-1, 2, *blocks.shape[1:])
    kept = lax.dynamic_index_in_dim(pairs, bit, 1, keepdims=False)
    given = lax.dynamic_index_in_dim(pairs, 1 - bit, 1, keepdims=False)
    got = lax.ppermute(given, "dp", [(i, i ^ step) for i in range(dp)])
    total = kept.astype(f32) + got.astype(f32)
    return total if 2 * step == dp else total.astype(bf16)


def halved_over_dp(blocks):
    dp = lax.axis_size("dp")
    if dp & (dp - 1):
        return lax.psum_scatter(blocks, "dp", scatter_dimension=0, tiled=False).astype(f32)
    step = 1
    while step < dp:
        blocks = halve(blocks, step)
        step *= 2
    return blocks[0].astype(f32)


def swapped(matrix, half):
    lane = lax.broadcasted_iota(jnp.int32, matrix.shape, 1)
    width = matrix.shape[1]
    return jnp.where(
        lane % (2 * half) < half,
        pltpu.roll(matrix, width - half, 1),
        pltpu.roll(matrix, half, 1),
    )


def rotated(matrix, tables, half, back):
    cosine, sine = tables
    times = matrix.shape[1] // cosine.shape[1]
    cosine, sine = (jnp.concatenate([t] * times, axis=1) for t in (cosine, sine))
    return matrix * cosine + swapped(matrix, half) * (-sine if back else sine)


def mask_into(bias_ref, row_ref):
    shape = bias_ref.shape
    key = lax.broadcasted_iota(jnp.int32, shape, 0)
    query = lax.broadcasted_iota(jnp.int32, shape, 1)
    column = jnp.broadcast_to(row_ref[:1], (128, shape[0])).T
    allowed = (column[:, :1] == row_ref[:1]) & (key <= query)
    bias_ref[...] = jnp.where(allowed, 0.0, neg_fill)


def head_cuts(head, kv_heads, q_heads, size):
    group = head // (q_heads // kv_heads)
    return (
        slice(head * size, (head + 1) * size),
        slice(2 * group * size, (2 * group + 1) * size),
        slice((2 * group + 1) * size, (2 * group + 2) * size),
    )


def attention_steps(
    size, scale, x_ref, gain_ref, query_ref, keyval_ref, tables, rows_ref, q_ref, kv_ref, total_ref, attended_ref,
    bias_ref, turned_ref,
):
    cos_ref, sin_ref, kcos_ref, ksin_ref = tables
    x = x_ref[...].astype(f32)
    factor = lax.rsqrt(jnp.mean(x * x, axis=-1, keepdims=True) + eps_norm)
    rows_ref[...] = (x * factor * gain_ref[:1]).astype(bf16)
    rows = rows_ref[...]
    q = jnp.dot(rows, query_ref[...], preferred_element_type=f32)
    q_ref[...] = rotated(q, (cos_ref[...], sin_ref[...]), size // 2, False).astype(bf16)
    kv = jnp.dot(rows, keyval_ref[...], preferred_element_type=f32)
    kv_ref[...] = rotated(kv, (kcos_ref[...], ksin_ref[...]), size // 2, False).astype(bf16)
    length = x.shape[0]
    tile = length // 2
    q_heads, kv_heads = q_ref.shape[1] // size, kv_ref.shape[1] // (2 * size)
    total_ref[...] = jnp.zeros_like(total_ref)
    for block in range(2):
        now, past = slice(block * tile, (block + 1) * tile), slice(0, (block + 1) * tile)
        for head in range(q_heads):
            at, key_at, value_at = head_cuts(head, kv_heads, q_heads, size)
            scores = dot(kv_ref[past, key_at], q_ref[now, at], (1, 1)) * scale + bias_ref[past, now]
            peak = jnp.max(scores, axis=0, keepdims=True)
            weight = jnp.exp(scores - peak)
            total = jnp.sum(weight, axis=0, keepdims=True)
            probs = (weight * (1.0 / total)).astype(bf16)
            total_ref[head : head + 1, now] = peak + jnp.log(total)
            turned_ref[at, now] = dot(kv_ref[past, value_at], probs, (0, 0))
    attended_ref[...] = turned_ref[...].T.astype(bf16)


def front_kernel(
    size, scale, x_ref, gain_ref, query_ref, keyval_ref, out_ref, row_ref, cos_ref, sin_ref,
    kcos_ref, ksin_ref, rows_out, q_out, kv_out, attended_out, total_ref, mid_ref, plane_ref, rows_ref, q_ref,
    kv_ref, attended_ref, x_whole, bias_ref, turned_ref, mine, arrived, passed, out_sem, x_s, x_r, h_s, h_r, p_s,
    p_r,
):
    t, e = lax.axis_index("tp"), lax.axis_index("ep")
    near, far, twin = {"tp": t ^ 1}, {"tp": t ^ 2}, {"ep": 1 - e}
    rows = x_ref.shape[0]
    half = rows // 2
    first, second = pl.ds(0, half), pl.ds(half, half)
    greet((near, far, twin))

    def link(send_sem, recv_sem):
        def send(src, dst, k, device):
            copy = pltpu.make_async_remote_copy(
                src, dst, send_sem.at[k], recv_sem.at[k], device_id=device, device_id_type=MESH
            )
            copy.start()
            return copy

        return send

    unsent = []

    def spread(send, whole, base, between, with_twin):
        def place(tt, part, count):
            return whole.at[rows_at(base + tt * rows + part * half, count)]

        def on(tt, part, count, k, device):
            copy = send(place(tt, part, count), place(tt, part, count), k, device)
            unsent.append(copy)
            return copy

        near_a, far_b = on(t, 0, half, 0, near), on(t, 1, half, 1, far)
        near_b, far_a = on(t, 1, half, 2, near), on(t, 0, half, 3, far)
        twins = [on(t, 0, rows, 6, twin)] if with_twin else []
        between()
        near_a.wait_recv()
        on_a = on(t ^ 1, 0, half, 4, far)
        far_b.wait_recv()
        on_b = on(t ^ 2, 1, half, 5, near)
        near_b.wait_recv()
        far_a.wait_recv()
        if with_twin:
            twins += [on(t ^ k, 0, rows, 6 + k, twin) for k in (1, 2)]
        on_a.wait_recv()
        on_b.wait_recv()
        if with_twin:
            twins.append(on(t ^ 3, 0, rows, 9, twin))
        for copy in twins:
            copy.wait_recv()

    x_whole[rows_at(t * rows, rows)] = x_ref[...]
    spread(link(x_s, x_r), x_whole, 0, lambda: mask_into(bias_ref, row_ref), False)
    attention_steps(
        size, scale, x_whole, gain_ref, query_ref, keyval_ref, (cos_ref, sin_ref, kcos_ref, ksin_ref),
        rows_ref, q_ref, kv_ref, total_ref, attended_ref, bias_ref, turned_ref,
    )
    late = ((rows_ref, rows_out), (q_ref, q_out), (kv_ref, kv_out), (attended_ref, attended_out))
    leaving = [pltpu.make_async_copy(a, b, out_sem.at[k]) for k, (a, b) in enumerate(late)]
    send = link(h_s, h_r)

    def bring(k):
        block = attended_ref[rows_at((t ^ k) * rows, rows)]
        mine[k] = jnp.dot(block, out_ref[...], preferred_element_type=f32).astype(bf16)

    def added(k, cut, *others):
        total = mine[k, cut].astype(f32)
        for other in others:
            total += other.astype(f32)
        return total

    bring(3)
    a_on = send(mine.at[3, first], arrived.at[0, 0], 0, near)
    b_on = send(mine.at[3, second], arrived.at[1, 0], 1, far)
    bring(1)
    a_own = send(mine.at[1, first], arrived.at[0, 1], 2, near)
    bring(2)
    b_own = send(mine.at[2, second], arrived.at[1, 1], 3, far)
    bring(0)
    for copy in leaving:
        copy.start()
    a_on.wait_recv()
    mine[2, first] = added(2, first, arrived[0, 0]).astype(bf16)
    a_last = send(mine.at[2, first], passed.at[0], 4, far)
    b_on.wait_recv()
    mine[1, second] = added(1, second, arrived[1, 0]).astype(bf16)
    b_last = send(mine.at[1, second], passed.at[1], 5, near)
    a_own.wait_recv()
    b_own.wait_recv()
    a_last.wait_recv()
    mid_ref[first] = x_ref[first].astype(f32) + added(0, first, arrived[0, 1], passed[0])
    b_last.wait_recv()
    mid_ref[second] = x_ref[second].astype(f32) + added(0, second, arrived[1, 1], passed[1])
    unsent.extend((a_on, b_on, a_own, b_own, a_last, b_last))
    x_mid = mid_ref[...]
    factor = lax.rsqrt(jnp.mean(x_mid * x_mid, axis=-1, keepdims=True) + eps_norm)
    base = e * (lax.axis_size("tp") * rows)
    plane_ref[rows_at(base + t * rows, rows)] = (x_mid * factor * gain_ref[1:2]).astype(bf16)
    spread(link(p_s, p_r), plane_ref, base, lambda: None, True)
    for copy in leaving:
        copy.wait()
    for copy in unsent:
        copy.wait_send()


def front(size, scale, x, gains, w_query, keyval, w_output, row, tables, collective_id):
    rows, width = x.shape
    length = row.shape[1]
    q_width, kv_width = w_query.shape[1], keyval.shape[1]
    shape, dma = jax.ShapeDtypeStruct, pltpu.SemaphoreType.DMA
    spec = pl.BlockSpec(memory_space=pltpu.VMEM)
    late = [
        shape((length, width), bf16),
        shape((length, q_width), bf16),
        shape((length, kv_width), bf16),
        shape((length, q_width), bf16),
    ]
    outs = late + [
        shape((-(-q_width // (8 * size)) * 8, length), f32),
        shape((rows, width), f32),
        shape((2 * length, width), bf16),
    ]
    return pl.pallas_call(
        functools.partial(front_kernel, size, scale),
        out_shape=outs,
        in_specs=[spec] * 10,
        out_specs=[pl.BlockSpec(memory_space=pl.ANY)] * 4 + [spec] * 3,
        scratch_shapes=[
            *(pltpu.VMEM(part.shape, part.dtype) for part in late),
            pltpu.VMEM((length, width), bf16),
            pltpu.VMEM((length, length), f32),
            pltpu.VMEM((q_width, length), f32),
            pltpu.VMEM((4, rows, width), bf16),
            pltpu.VMEM((2, 2, rows // 2, width), bf16),
            pltpu.VMEM((2, rows // 2, width), bf16),
            dma((4,)),
            *([dma((6,))] * 4),
            *([dma((10,))] * 2),
        ],
        name="front",
        cost_estimate=pl.CostEstimate(flops=10**9, bytes_accessed=10**6, transcendentals=0),
        compiler_params=pltpu.CompilerParams(
            collective_id=collective_id, has_side_effects=True, vmem_limit_bytes=58 * 2**20
        ),
    )(x, gains, w_query, keyval, w_output, row, *tables)


def attention_back_steps(
    size, scale, grad_ref, out_ref, q_ref, kv_ref, total_ref, tables, pre_ref, bias_ref, turned_ref,
    kv_grad_ref, heads_ref,
):
    heads_ref[...] = dot(grad_ref[...], out_ref[...], (1, 1)).astype(bf16)
    length = q_ref.shape[0]
    tile = length // 2
    q_heads, kv_heads = q_ref.shape[1] // size, kv_ref.shape[1] // (2 * size)
    for block in range(2):
        now, past = slice(block * tile, (block + 1) * tile), slice(0, (block + 1) * tile)
        for head in range(q_heads):
            at, key_at, value_at = head_cuts(head, kv_heads, q_heads, size)
            keys, query, grad = kv_ref[past, key_at], q_ref[now, at], heads_ref[now, at]
            scores = dot(keys, query, (1, 1)) * scale + bias_ref[past, now]
            probs = jnp.exp(scores - total_ref[head : head + 1, now])
            grad_probs = dot(kv_ref[past, value_at], grad, (1, 1))
            inner = jnp.sum(probs * grad_probs, axis=0, keepdims=True)
            grad_scores = (probs * (grad_probs - inner)).astype(bf16)
            turned_ref[at, now] = dot(keys, grad_scores, (0, 0)) * scale
            kv_grad_ref[past, key_at] += dot(grad_scores, query, (1, 0)) * scale
            kv_grad_ref[past, value_at] += dot(probs.astype(bf16), grad, (1, 0))
    width = q_ref.shape[1]
    cos_ref, sin_ref, kcos_ref, ksin_ref = tables
    pre_ref[:, :width] = rotated(
        turned_ref[...].T, (cos_ref[...], sin_ref[...]), size // 2, True
    ).astype(bf16)
    pre_ref[:, width:] = rotated(
        kv_grad_ref[...], (kcos_ref[...], ksin_ref[...]), size // 2, True
    ).astype(bf16)


def attention_back_kernel(
    size, scale, grad_ref, out_ref, q_ref, kv_ref, total_ref, query_ref, keyval_ref, row_ref,
    cos_ref, sin_ref, kcos_ref, ksin_ref, *refs,
):
    part_ref, pre_ref, bias_ref, turned_ref, kv_grad_ref, heads_ref = refs[-6:]
    mask_into(bias_ref, row_ref)
    kv_grad_ref[...] = jnp.zeros_like(kv_grad_ref)
    attention_back_steps(
        size, scale, grad_ref, out_ref, q_ref, kv_ref, total_ref, (cos_ref, sin_ref, kcos_ref, ksin_ref),
        pre_ref, bias_ref, turned_ref, kv_grad_ref, heads_ref,
    )
    width = q_ref.shape[1]
    part_ref[...] = (
        dot(pre_ref[:, :width], query_ref[...], (1, 1))
        + dot(pre_ref[:, width:], keyval_ref[...], (1, 1))
    ).astype(bf16)


def local_call(body, name, out_shape, scratch, args, after=(), limit=48):
    spec = pl.BlockSpec(memory_space=pltpu.VMEM)
    return pl.pallas_call(
        body,
        out_shape=out_shape,
        in_specs=[spec] * len(args) + [pl.BlockSpec(memory_space=pl.ANY)] * len(after),
        out_specs=jax.tree.map(lambda _: spec, out_shape),
        scratch_shapes=scratch,
        name=name,
        cost_estimate=pl.CostEstimate(flops=10**6, bytes_accessed=10**6, transcendentals=0),
        compiler_params=pltpu.CompilerParams(vmem_limit_bytes=limit * 2**20),
    )(*args, *after)


def attention_weights_kernel(rows_ref, pre_ref, grad_ref, attended_ref, *outs):
    width, pre = rows_ref.shape[1], pre_ref.shape[1]
    parts = outs[0].shape[0] if len(outs) == 2 else 4
    d, e = lax.axis_index("dp"), lax.axis_index("ep")
    step = width // parts
    for c in range(parts):
        cut = slice(c * step, (c + 1) * step)
        first = dot(rows_ref[:, cut], pre_ref[...], (0, 0)).astype(bf16)
        second = dot(grad_ref[:, cut], attended_ref[...], (0, 0)).astype(bf16)
        if len(outs) == 1:
            outs[0][cut, :pre] = first
            outs[0][cut, pre:] = second
            continue
        for half in range(2):
            some = slice(half * (step // 2), (half + 1) * (step // 2))
            for mine in range(2):

                @pl.when((half == e) == (mine == 1))
                def _():
                    out_ref = outs[0] if mine else outs[1]
                    out_ref[d ^ c, :, :pre] = first[some]
                    out_ref[d ^ c, :, pre:] = second[some]


def exchanged(blocks, step):
    return lax.ppermute(blocks, "dp", [(i, i ^ step) for i in range(lax.axis_size("dp"))])


def summed_everywhere(value):
    for axis in ("ep", "tp", "dp"):
        size, step = lax.axis_size(axis), 1
        if size & (size - 1):
            value = lax.psum(value, axis)
            continue
        while step < size:
            value = value + lax.ppermute(value, axis, [(i, i ^ step) for i in range(size)])
            step *= 2
    return value


def dot(a, b, dims):
    return lax.dot_general(a, b, ((dims[:1], dims[1:]), ((), ())), preferred_element_type=f32)


def experts_kernel(first, local_experts, is_last, held, *refs):
    if first == 0:
        rows_ref, grad_ref, router_ref, in_ref, out_ref = refs[:5]
        gates_ref, terms_ref, back_ref, mixed_ref, keep_ref, *give_refs = refs[5:]
    else:
        rows_ref, grad_ref, gates_ref, in_ref, out_ref = refs[:5]
        terms_in = refs[7]
        outs = refs[8 + held :]
        if is_last:
            logits_ref, router_grad_ref, *outs = outs
        terms_ref, back_ref, mixed_ref, keep_ref, *give_refs = outs
    tokens, width = rows_ref.shape
    pair, _, hidden, _ = in_ref.shape
    tile = 256 if tokens % 256 == 0 else tokens
    number = pl.program_id(0) + first

    if first == 0:
        logits = jnp.dot(rows_ref[...], router_ref[...], preferred_element_type=f32)
        used = grad_ref[:, width:].astype(f32) > 0.5
        peak = jnp.max(jnp.where(used, logits, -jnp.inf), axis=-1, keepdims=True)
        weight = jnp.where(used, jnp.exp(jnp.where(used, logits - peak, 0.0)), 0.0)
        gates = weight / jnp.sum(weight, axis=-1, keepdims=True)
        gates_ref[...] = gates.T[: gates_ref.shape[0]]
    if first == 0:
        terms_ref[...] = jnp.zeros_like(terms_ref)
    else:

        @pl.when(pl.program_id(0) == 0)
        def _():
            terms_ref[...] = terms_in[...]

    into = in_ref[...].reshape(pair * 2 * hidden, width)
    out_of = out_ref[...].reshape(pair * hidden, width)
    base = lax.axis_index("ep") * local_experts + number * pair

    @pl.loop(0, tokens // tile)
    def _(j):
        now = pl.ds(pl.multiple_of(j * tile, tile), tile)
        gate_up = dot(into, rows_ref[now, :], (1, 1))
        down = dot(out_of, grad_ref[now, :width], (1, 1))
        for k in range(pair):
            gate = gate_up[2 * k * hidden : (2 * k + 1) * hidden]
            up = gate_up[(2 * k + 1) * hidden : (2 * k + 2) * hidden]
            back = down[k * hidden : (k + 1) * hidden]
            g = gates_ref[pl.ds(base + k, 1), now]
            sig = 1.0 / (1.0 + jnp.exp(-gate))
            silu = gate * sig
            active = silu * up
            terms_ref[pl.ds(base + k, 1), now] = jnp.sum(active * back, axis=0, keepdims=True)
            mixed_ref[k * hidden : (k + 1) * hidden, now] = (g * active).astype(bf16)
            grad_active = g * back
            back_ref[2 * k * hidden : (2 * k + 1) * hidden, now] = (
                grad_active * up * (sig * (1.0 + gate * (1.0 - sig)))
            ).astype(bf16)
            back_ref[(2 * k + 1) * hidden : (2 * k + 2) * hidden, now] = (
                grad_active * silu
            ).astype(bf16)

    columns = keep_ref.shape[3]
    blocks = width // columns
    ins = pair * 2 * hidden
    for at in range(0, pair * 3 * hidden, pair * hidden):
        if at < ins:
            total = jnp.dot(
                back_ref[at : at + pair * hidden], rows_ref[...], preferred_element_type=f32
            )
        else:
            total = jnp.dot(mixed_ref[...], grad_ref[:, :width], preferred_element_type=f32)
        total = total.astype(bf16)
        if blocks == 1:
            keep_ref[0, 0, at : at + pair * hidden] = total
            continue
        for c in range(blocks):
            apart = c ^ lax.axis_index("dp")
            part = total[:, c * columns : (c + 1) * columns]

            @pl.when(apart % 2 == 0)
            def _():
                keep_ref[0, apart // 2, at : at + pair * hidden] = part

            @pl.when(apart % 2 == 1)
            def _():
                give_refs[0][0, apart // 2, at : at + pair * hidden] = part

    if is_last:

        @pl.when(pl.program_id(0) == pl.num_programs(0) - 1)
        def _():
            gates, terms = gates_ref[...], terms_ref[...]
            logits = gates * (terms - jnp.sum(gates * terms, axis=0, keepdims=True))
            high = logits.astype(bf16)
            rows = logits.shape[0]
            logits_ref[:rows] = high
            logits_ref[rows:] = (logits - high.astype(f32)).astype(bf16)
            both = jnp.dot(logits_ref[...], rows_ref[...], preferred_element_type=f32)
            router_grad_ref[...] = both[:rows] + both[rows:]


def experts(
    first, count, blocks, rows_two, plane_grad, gates_or_router, w_in, w_out, earlier=(), after=()
):
    local_experts, _, hidden, width = w_in.shape
    tokens = rows_two.shape[0]
    pair = 2 if local_experts % 2 == 0 else 1
    pairs = local_experts // pair
    gate_rows = -(-local_experts * lax.axis_size("ep") // 8) * 8
    is_last = first + count == pairs
    spread = (max(blocks // 2, 1), pair * 3 * hidden, width // blocks)
    given = 1 if blocks > 1 else 0

    def whole(array):
        return pl.BlockSpec(array.shape, lambda i: (0,) * array.ndim, pipeline_mode=pl.Buffered(1))

    in_specs = [
        whole(rows_two),
        whole(plane_grad),
        whole(gates_or_router),
        pl.BlockSpec((pair, 2, hidden, width), lambda i: (i + first, 0, 0, 0)),
        pl.BlockSpec((pair, hidden, width), lambda i: (i + first, 0, 0)),
    ]
    if earlier:
        in_specs += [pl.BlockSpec(memory_space=pl.ANY)] * 2 + [whole(earlier[2])]
    in_specs += [pl.BlockSpec(memory_space=pl.ANY)] * len(after)
    out_shape = [
        jax.ShapeDtypeStruct((gate_rows, tokens), f32),
        jax.ShapeDtypeStruct((local_experts * 2 * hidden, tokens), bf16),
        jax.ShapeDtypeStruct((local_experts * hidden, tokens), bf16),
        jax.ShapeDtypeStruct((count, *spread), bf16),
    ] + [jax.ShapeDtypeStruct((count, *spread), bf16)] * given
    out_specs = [
        pl.BlockSpec((gate_rows, tokens), lambda i: (0, 0)),
        pl.BlockSpec((pair * 2 * hidden, tokens), lambda i: (i + first, 0)),
        pl.BlockSpec((pair * hidden, tokens), lambda i: (i + first, 0)),
        pl.BlockSpec((1, *spread), lambda i: (i, 0, 0, 0)),
    ] + [pl.BlockSpec((1, *spread), lambda i: (i, 0, 0, 0))] * given
    aliases = {}
    if first == 0:
        out_shape.insert(0, jax.ShapeDtypeStruct((gate_rows, tokens), f32))
        out_specs.insert(0, pl.BlockSpec((gate_rows, tokens), lambda i: (0, 0)))
    else:
        aliases = {5: 1 + 2 * is_last, 6: 2 + 2 * is_last}
    if is_last:
        out_shape = [
            jax.ShapeDtypeStruct((2 * gate_rows, tokens), bf16),
            jax.ShapeDtypeStruct((gate_rows, width), f32),
        ] + out_shape
        out_specs = [
            pl.BlockSpec((2 * gate_rows, tokens), lambda i: (0, 0)),
            pl.BlockSpec((gate_rows, width), lambda i: (0, 0)),
        ] + out_specs
    return pl.pallas_call(
        functools.partial(experts_kernel, first, local_experts, is_last, len(after)),
        grid=(count,),
        out_shape=out_shape,
        in_specs=in_specs,
        out_specs=out_specs,
        input_output_aliases=aliases,
        name=f"experts_{first}",
        cost_estimate=pl.CostEstimate(
            flops=10**6, bytes_accessed=10**6, transcendentals=0
        ),
        compiler_params=pltpu.CompilerParams(vmem_limit_bytes=44 * 2**20),
    )(rows_two, plane_grad, gates_or_router, w_in, w_out, *earlier, *after)


def rope_tables(length, head_size):
    half_size = head_size // 2
    frequency = jnp.exp(
        jnp.arange(half_size, dtype=f32) * (-2.0 * math.log(rope_base) / head_size)
    )
    angles = jnp.arange(length, dtype=f32)[:, None] * frequency[None, :]
    cosine, sine = jnp.cos(angles), jnp.sin(angles)
    one_cos = jnp.concatenate([cosine, cosine], axis=1)
    one_sin = jnp.concatenate([-sine, sine], axis=1)
    return (
        jnp.concatenate([one_cos, one_cos], axis=1),
        jnp.concatenate([one_sin, one_sin], axis=1),
        jnp.concatenate([one_cos, jnp.ones_like(one_cos)], axis=1),
        jnp.concatenate([one_sin, jnp.zeros_like(one_sin)], axis=1),
    )


def normalize(matrix):
    factor = lax.rsqrt(jnp.mean(matrix * matrix, axis=-1, keepdims=True) + eps_norm)
    return (matrix * factor, factor)


def norm_back(grad_normed, normed_hat, factor, gain):
    grad_hat = grad_normed * gain
    grad_inner = jnp.mean(grad_hat * normed_hat, axis=-1, keepdims=True)
    return (
        factor * (grad_hat - normed_hat * grad_inner),
        jnp.sum(grad_normed * normed_hat, axis=0),
    )


tail_late = [
    "got_a", "got_b", "w_output", "q", "kv", "w_query", "keyval", "rows", "attended",
]
tail_first = [
    "back", "w_up",
]
tail_last = [
    "mixed", "w_down",
]
tail_held = [
    "keep_a", "keep_b", "keep_c", "keep_rest", "give_c", "give_rest",
]
tail_near = [
    "x_mid", "grad", "x", "gains", "router", "router_rows", "logits", "total", "row", "cosine", "sine",
    "kcosine", "ksine",
]
tail_out = [
    "kept", "got", "attn_kept", "attn_got", "block_out", "grad_input", "small",
]
tail_scratch = [
    "backs", "ups", "stage", "came1", "give2", "mine", "twins", "arrived", "passed", "outbox", "sums", "bias",
    "turned", "kv_grad", "heads", "pre", "own_w", "twin_w", "twin_came", "w_came", "w_give", "quarters",
    "small_came",
]
tail_sems = [
    "late_sem", "part_sem", "stage_sem", "z1_s", "z1_r", "z2_s", "z2_r", "p_s", "p_r", "g_s", "g_r", "o_s",
    "o_r", "h_s", "h_r", "w_s", "w_r", "s_s", "s_r",
]


def tail_kernel(size, scale, *refs):
    names = tail_near + tail_late + tail_first + tail_last + tail_held + tail_out + ["l_" + n for n in tail_late]
    names = names + tail_scratch + tail_sems
    r = dict(zip(names, refs, strict=True))
    d, e, t = lax.axis_index("dp"), lax.axis_index("ep"), lax.axis_index("tp")
    near, far, twin = {"tp": t ^ 1}, {"tp": t ^ 2}, {"ep": 1 - e}
    next_z, far_z = {"dp": d ^ 1}, {"dp": d ^ 2}
    rows, width = r["x_mid"].shape
    half = rows // 2
    first, second = pl.ds(0, half), pl.ds(half, half)
    pairs = r["kept"].shape[0]
    greet((near, far, twin, next_z, far_z))

    loads = {}
    for k, name in enumerate(tail_late):
        loads[name] = pltpu.make_async_copy(r[name], r["l_" + name], r["late_sem"].at[k])

    def late(name):
        if name in loads:
            loads.pop(name).wait()
        return r["l_" + name]

    def link(name):
        send_sem, recv_sem = r[name + "_s"], r[name + "_r"]

        def send(src, dst, k, device):
            copy = pltpu.make_async_remote_copy(
                src, dst, send_sem.at[k], recv_sem.at[k], device_id=device, device_id_type=MESH
            )
            copy.start()
            return copy

        return send

    unsent = []

    z1, z2 = link("z1"), link("z2")
    over1, over2, stages = {}, {}, {}

    units = r["kept"].shape[1]
    pieces = [(n, pl.ds(0, units)) for n in range(pairs - 1)]
    pieces += [(pairs - 1, pl.ds(at, units // 2)) for at in (0, units // 2)]

    def start1(k):
        n, cut = pieces[k]
        over1[k] = [
            z1(
                (r["give_c"].at[0] if n == 2 else r["give_rest"].at[n - 3]).at[side, cut],
                r["came1"].at[n - 2, side, cut],
                2 * (k - 2) + side,
                next_z,
            )
            for side in (1, 0)
        ]

    def prepare(k):
        n, cut = pieces[k]
        kept = r[("keep_a", "keep_b", "keep_c")[n]].at[0] if n < 3 else r["keep_rest"].at[n - 3]
        stages[k] = pltpu.make_async_copy(kept.at[:, cut], r["stage"].at[:, cut], r["stage_sem"])
        stages[k].start()

    def add1(k):
        n, cut = pieces[k]
        if n < 2:
            came = late(("got_a", "got_b")[n])
        else:
            for copy in over1[k]:
                copy.wait_recv()
            unsent.extend(over1[k])
            came = r["came1"].at[n - 2]
        stages[k].wait()
        r["give2"][n, cut] = (
            r["stage"][1, cut].astype(f32) + came[1, cut].astype(f32)
        ).astype(bf16)
        over2[k] = z2(r["give2"].at[n, cut], r["got"].at[n, cut], k, far_z)
        r["kept"][n, cut] = (r["stage"][0, cut].astype(f32) + came[0, cut].astype(f32)).astype(bf16)
        if k + 1 < len(pieces):
            prepare(k + 1)

    def added(to, index, *others):
        total = to[index].astype(f32)
        for other in others:
            total += other.astype(f32)
        return total

    def scatter(send, bring, number, between):
        mine, arrived, passed = r["mine"], r["arrived"].at[number], r["passed"].at[number]
        bring(3)
        a_on = send(mine.at[3, first], arrived.at[0, 0], 4, near)
        b_on = send(mine.at[3, second], arrived.at[1, 0], 5, far)
        bring(1)
        a_own = send(mine.at[1, first], arrived.at[0, 1], 6, near)
        bring(2)
        b_own = send(mine.at[2, second], arrived.at[1, 1], 7, far)
        bring(0)
        between()
        a_on.wait_recv()
        mine[2, first] = added(mine, (2, first), arrived[0, 0]).astype(bf16)
        a_last = send(mine.at[2, first], passed.at[0], 8, far)
        b_on.wait_recv()
        mine[1, second] = added(mine, (1, second), arrived[1, 0]).astype(bf16)
        b_last = send(mine.at[1, second], passed.at[1], 9, near)
        a_own.wait_recv()
        b_own.wait_recv()
        a_last.wait_recv()
        r["sums"][first] = added(mine, (0, first), arrived[0, 1], passed[0])
        b_last.wait_recv()
        r["sums"][second] = added(mine, (0, second), arrived[1, 1], passed[1])
        for copy in (a_on, b_on, a_own, b_own, a_last, b_last):
            copy.wait_send()

    def nothing():
        pass

    plane = rows * lax.axis_size("tp")

    def scatter_all(send, make, number, between):
        order = (3, 1, 2, 0)
        twins_sent = {}

        def compute(k):
            block = rows_at((1 - e) * plane + (t ^ k) * rows, rows)
            r["outbox"][k] = make(block)
            twins_sent[k] = send(r["outbox"].at[k], r["twins"].at[number // 2, k], k, twin)
            r["mine"][k] = make(rows_at(e * plane + (t ^ k) * rows, rows))

        def bring(k):
            at = order.index(k)
            if at + 1 < 4:
                compute(order[at + 1])
            twins_sent[k].wait_recv()
            r["mine"][k] = added(r["mine"], k, r["twins"][number // 2, k]).astype(bf16)

        compute(order[0])
        scatter(send, bring, number, between)
        for copy in twins_sent.values():
            copy.wait_send()

    start1(2)
    backs, ups = r["backs"], r["ups"]
    for copy in list(loads.values())[:2]:
        copy.start()
    prepare(0)
    firsts = [
        pltpu.make_async_copy(r[n], place, r["part_sem"].at[k])
        for k, (n, place) in enumerate((("back", backs), ("w_up", ups)))
    ]
    for copy in firsts + list(loads.values())[2:]:
        copy.start()
    add1(0)
    add1(1)
    for copy in firsts:
        copy.wait()

    def rows_back(block):
        return (
            dot(backs[:, block], ups[...], (0, 0))
            + dot(r["logits"][:, block], r["router_rows"][...], (0, 0))
        ).astype(bf16)

    scatter_all(link("p"), rows_back, 0, nothing)

    def norm_back_in(grad_normed, values, gain):
        factor = lax.rsqrt(jnp.mean(values * values, axis=-1, keepdims=True) + eps_norm)
        hat = values * factor
        grad_hat = grad_normed * gain
        inner = jnp.mean(grad_hat * hat, axis=-1, keepdims=True)
        return (
            factor * (grad_hat - hat * inner),
            jnp.sum(grad_normed * hat, axis=0, keepdims=True),
        )

    small, lanes = r["quarters"], width // 4
    experts_all = r["router"].shape[0] - 4

    def small_put(values, at):
        for k in range(4):
            small[k, at] = values[:, k * lanes : (k + 1) * lanes]

    small_put(r["router"][...], slice(0, experts_all + 4))
    back, gain_grad = norm_back_in(r["sums"][...], r["x_mid"][...], r["gains"][1:2])
    small_put(gain_grad, slice(experts_all, experts_all + 1))
    grad_mid = r["grad"][...].astype(f32) + back
    r["grad_input"][...] = grad_mid

    length = r["l_q"].shape[0]
    whole = ups.at[:length]

    def place(tt, part, count):
        return ups.at[rows_at(tt * rows + part * half, count)]

    ups[rows_at(t * rows, rows), :] = grad_mid.astype(bf16)
    g = link("g")
    near_a = g(place(t, 0, half), place(t, 0, half), 0, near)
    far_b = g(place(t, 1, half), place(t, 1, half), 1, far)
    near_b = g(place(t, 1, half), place(t, 1, half), 2, near)
    far_a = g(place(t, 0, half), place(t, 0, half), 3, far)
    mixed = backs.at[: r["mixed"].shape[0]]
    w_down = ups.at[length : length + r["w_down"].shape[0]]
    lasts = [
        pltpu.make_async_copy(r[n], place_, r["part_sem"].at[2 + k])
        for k, (n, place_) in enumerate((("mixed", mixed), ("w_down", w_down)))
    ]
    for copy in lasts:
        copy.start()
    mask_into(r["bias"], r["row"])
    r["kv_grad"][...] = jnp.zeros_like(r["kv_grad"])
    near_a.wait_recv()
    on_a = g(place(t ^ 1, 0, half), place(t ^ 1, 0, half), 4, far)
    far_b.wait_recv()
    on_b = g(place(t ^ 2, 1, half), place(t ^ 2, 1, half), 5, near)
    for copy in (near_b, far_a, on_a, on_b):
        copy.wait_recv()
    unsent.extend((near_a, far_b, near_b, far_a, on_a, on_b))

    attention_back_steps(
        size,
        scale,
        whole,
        late("w_output"),
        late("q"),
        late("kv"),
        r["total"],
        [r[n] for n in ("cosine", "sine", "kcosine", "ksine")],
        *(r[n] for n in ("pre", "bias", "turned", "kv_grad", "heads")),
    )
    start1(3)
    q_width = r["l_q"].shape[1]
    w_query, keyval = late("w_query"), late("keyval")

    def bring_heads(k):
        block = rows_at((t ^ k) * rows, rows)
        r["mine"][k] = (
            dot(r["pre"][block, :q_width], w_query[...], (1, 1))
            + dot(r["pre"][block, q_width:], keyval[...], (1, 1))
        ).astype(bf16)

    w = link("w")
    twin_w = []

    def weights():
        attention_weights_kernel(
            late("rows"), r["pre"], whole, late("attended"), r["own_w"], r["twin_w"]
        )
        twin_w.append(w(r["twin_w"], r["twin_came"], 0, twin))
        add1(2)

    scatter(link("h"), bring_heads, 1, weights)
    back, gain_grad = norm_back_in(r["sums"][...], r["x"][...].astype(f32), r["gains"][:1])
    small_put(gain_grad, slice(experts_all + 1, experts_all + 2))
    r["grad_input"][...] = r["grad_input"][...] + back

    twin_w[0].wait_recv()
    own_w = r["own_w"]
    w_copies = list(twin_w)
    for k in (1, 3):
        own_w[k] = added(own_w, k, r["twin_came"][k]).astype(bf16)
        w_copies.append(w(own_w.at[k], r["w_came"].at[k // 2], 1 + k // 2, next_z))
    for k in (0, 2):
        own_w[k] = added(own_w, k, r["twin_came"][k]).astype(bf16)

    s = link("s")
    low, high = t % 2, t // 2 % 2
    two = [pl.ds((low ^ k) * 2, 2) for k in range(2)]
    one = [pl.ds(low * 2 + (high ^ k), 1) for k in range(2)]
    own, every = one[0], pl.ds(0, 4)
    small_plan = [
        (twin, every, every),
        (near, two[1], two[0]),
        (far, one[1], own),
        (next_z, own, own),
        (far_z, own, own),
        (far, own, one[1]),
        (near, two[0], two[1]),
    ]
    small_sent = {}

    def small_send(k):
        device, cut, _ = small_plan[k]
        small_sent[k] = s(small.at[cut], r["small_came"].at[k, cut], k, device)

    def small_add(k):
        kept = small_plan[k][2]
        small_sent[k].wait()
        came = r["small_came"][k, kept]
        small[kept] = small[kept] + came if k < 5 else came

    small_send(0)

    for copy in lasts:
        copy.wait()

    def mixed_rows(block):
        return dot(mixed[:, block], w_down[...], (0, 0)).astype(bf16)

    def third_sum():
        add1(3)
        start1(4)
        small_add(0)
        small_send(1)

    scatter_all(link("o"), mixed_rows, 2, third_sum)
    r["block_out"][...] = (r["x_mid"][...] + r["sums"][...]).astype(bf16)

    small_add(1)
    small_send(2)
    small_add(2)
    small_send(3)
    for copy in w_copies[1:]:
        copy.wait_recv()
    r["w_give"][...] = added(own_w, 2, r["w_came"][1]).astype(bf16)
    w_copies.append(w(r["w_give"], r["attn_got"], 3, far_z))
    r["attn_kept"][...] = added(own_w, 0, r["w_came"][0]).astype(bf16)
    start1(5)
    small_add(3)
    small_send(4)
    add1(4)
    small_add(4)
    small_send(5)
    add1(5)
    small_add(5)
    small_send(6)
    small_add(6)
    for k in range(4):
        r["small"][:, k * lanes : (k + 1) * lanes] = small[k]
    w_copies[-1].wait_recv()
    for k in range(len(pieces)):
        over2[k].wait()
    for copy in unsent + w_copies:
        copy.wait_send()


def tail(size, scale, named, collective_id):
    width = named["x_mid"].shape[1]
    rows = named["x_mid"].shape[0]
    length = named["q"].shape[0]
    q_width, kv_width = named["q"].shape[1], named["kv"].shape[1]
    _, count, units, columns = named["keep_a"].shape
    pairs = 3 + named["keep_rest"].shape[0]
    block = (width // 8, 2 * q_width + kv_width)
    shape = jax.ShapeDtypeStruct
    outs = dict(
        kept=shape((pairs, units, columns), bf16),
        got=shape((pairs, units, columns), bf16),
        attn_kept=shape(block, bf16),
        attn_got=shape(block, bf16),
        block_out=shape((rows, width), bf16),
        grad_input=shape((rows, width), f32),
        small=shape(named["router"].shape, f32),
    )
    scratch = dict(
        stage=((count, units, columns), bf16),
        came1=((pairs - 2, count, units, columns), bf16),
        give2=((pairs, units, columns), bf16),
        mine=((4, rows, width), bf16),
        twins=((2, 4, rows, width), bf16),
        arrived=((3, 2, 2, rows // 2, width), bf16),
        passed=((3, 2, rows // 2, width), bf16),
        outbox=((4, rows, width), bf16),
        sums=((rows, width), f32),
        backs=(named["back"].shape, bf16),
        ups=(named["w_up"].shape, bf16),
        bias=((length, length), f32),
        turned=((q_width, length), f32),
        kv_grad=((length, kv_width), f32),
        heads=((length, q_width), bf16),
        pre=((length, q_width + kv_width), bf16),
        own_w=((4, *block), bf16),
        twin_w=((4, *block), bf16),
        twin_came=((4, *block), bf16),
        w_came=((2, *block), bf16),
        w_give=(block, bf16),
        quarters=((4, named["router"].shape[0], width // 4), f32),
        small_came=((7, 4, named["router"].shape[0], width // 4), f32),
    )
    sems = dict(late_sem=len(tail_late), part_sem=4, z1=2 * (pairs - 1), z2=pairs + 1, p=10, g=6, o=10, h=10, w=4, s=7)
    dma = pltpu.SemaphoreType.DMA
    scratch_shapes = (
        [pltpu.VMEM(named[n].shape, named[n].dtype) for n in tail_late]
        + [pltpu.VMEM(*scratch[n]) for n in tail_scratch]
        + [dma((sems["late_sem"],)), dma((4,)), dma]
        + [dma((sems[n[:-2]],)) for n in tail_sems[3:]]
    )
    elsewhere, here = pl.BlockSpec(memory_space=pl.ANY), pl.BlockSpec(memory_space=pltpu.VMEM)
    ins = tail_near + tail_late + tail_first + tail_last + tail_held
    results = pl.pallas_call(
        functools.partial(tail_kernel, size, scale),
        out_shape=[outs[n] for n in tail_out],
        in_specs=[here] * len(tail_near) + [elsewhere] * (len(ins) - len(tail_near)),
        out_specs=[elsewhere if n in ("got", "attn_got") else here for n in tail_out],
        scratch_shapes=scratch_shapes,
        name="tail",
        cost_estimate=pl.CostEstimate(flops=10**9, bytes_accessed=10**6, transcendentals=0),
        compiler_params=pltpu.CompilerParams(
            collective_id=collective_id, has_side_effects=True, vmem_limit_bytes=60 * 2**20
        ),
    )(*(named[n] for n in ins))
    return dict(zip(tail_out, results))


def place_pairs(kept, got, shapes):
    (_, _, hidden, columns), _ = shapes
    pairs, units, _ = kept.shape
    pair = units // (3 * hidden)
    ins = 2 * pair * hidden

    def body(kept_ref, got_ref, into_ref, out_ref):
        total = kept_ref[0].astype(f32) + got_ref[0].astype(f32)
        into_ref[...] = total[:ins].reshape(pair, 2, hidden, columns)
        out_ref[...] = total[ins:].reshape(pair, hidden, columns)

    block = pl.BlockSpec((1, units, columns), lambda i: (i, 0, 0))
    return pl.pallas_call(
        body,
        grid=(pairs,),
        out_shape=[jax.ShapeDtypeStruct(s, f32) for s in shapes],
        in_specs=[block, block],
        out_specs=[
            pl.BlockSpec((pair, 2, hidden, columns), lambda i: (i, 0, 0, 0)),
            pl.BlockSpec((pair, hidden, columns), lambda i: (i, 0, 0)),
        ],
        name="place_pairs",
        compiler_params=pltpu.CompilerParams(vmem_limit_bytes=24 * 2**20),
    )(kept, got)


def per_device(
    activations,
    segments,
    routes,
    attn_gain,
    w_query,
    key_value_weight,
    w_output,
    moe_gain,
    w_router,
    w_in,
    w_out,
    out_cotangent,
):
    row_count, width = activations.shape
    tp_count = lax.axis_size("tp")
    ep_count = lax.axis_size("ep")
    dp_count = lax.axis_size("dp")
    e_index = lax.axis_index("ep")
    seq_len = row_count * tp_count
    head_size = key_value_weight.shape[2] // 2
    kv_heads = key_value_weight.shape[1]
    q_heads = w_query.shape[1] // head_size
    heads_per_group = q_heads // kv_heads
    top_count = routes.shape[1]
    expert_count = w_router.shape[1]
    local_experts = w_in.shape[0]
    hidden = w_in.shape[2]
    score_scale = 1.0 / math.sqrt(head_size)

    lanes = jnp.arange(128, dtype=jnp.int32)
    used = jnp.any(routes[:, :, None] == lanes[None, None, :], axis=1).astype(bf16)
    plane_grad = lax.all_gather(
        jnp.concatenate([out_cotangent, used], axis=1), ("ep", "tp"), axis=0, tiled=True
    )

    tables = rope_tables(seq_len, head_size)
    keyval_flat = key_value_weight.reshape(width, kv_heads * 2 * head_size)
    doc_row = segments.astype(f32)
    q_width, kv_width = q_heads * head_size, 2 * kv_heads * head_size
    gains = jnp.concatenate([attn_gain[None], moe_gain[None], jnp.zeros((6, width), f32)])
    full_rows, query_rows, keyval_rows, attended, log_total, x_mid, rows_two = front(
        head_size,
        score_scale,
        activations,
        gains,
        w_query,
        keyval_flat,
        w_output,
        doc_row,
        tables,
        0,
    )

    pair = 2 if local_experts % 2 == 0 else 1
    pairs = local_experts // pair
    columns = width // dp_count
    in_order = dp_count == 4 and ep_count == 2 and tp_count == 4 and columns % 128 == 0 and pairs == 5
    blocks = dp_count if in_order else 1
    gates = jnp.pad(w_router, ((0, 0), (0, 128 - expert_count)))
    keeps, gives, came, earlier = [], [], [], ()
    calls = ((0, 1), (1, 1), (2, 1), (3, pairs - 3)) if in_order else ((0, 1), (1, pairs - 1))
    for start, count in calls:
        after = (came[0],) if start == 3 else ()
        results = experts(
            start, count, blocks, rows_two, plane_grad, gates, w_in, w_out, earlier, after
        )
        if start == 0:
            gates, *results = results
        if start + count == pairs:
            logits, grad_w_router, *results = results
        terms, back, mixed, keep, *give = results
        earlier = (back, mixed, terms)
        keeps.append(keep)
        gives += give
        if in_order and start < 2:
            came.append(exchanged(give[0][0], 1))

    gate_rows = gates.shape[0]
    router_rows = jnp.pad(w_router.T, ((0, gate_rows - expert_count), (0, 0)))
    router_rows = jnp.concatenate([router_rows] * 2)
    all_width = 2 * q_width + kv_width
    shapes = [(local_experts, 2, hidden, columns), (local_experts, hidden, columns)]
    if in_order:
        done = tail(
            head_size,
            score_scale,
            dict(
                back=back,
                w_up=w_in.reshape(-1, width),
                logits=logits,
                router_rows=router_rows,
                keep_a=keeps[0],
                keep_b=keeps[1],
                keep_c=keeps[2],
                give_c=gives[2],
                keep_rest=keeps[3],
                give_rest=gives[3],
                got_a=came[0],
                got_b=came[1],
                x_mid=x_mid,
                grad=out_cotangent,
                x=activations,
                gains=gains,
                router=grad_w_router,
                total=log_total,
                row=doc_row,
                cosine=tables[0],
                sine=tables[1],
                kcosine=tables[2],
                ksine=tables[3],
                w_output=w_output,
                q=query_rows,
                kv=keyval_rows,
                w_query=w_query,
                keyval=keyval_flat,
                rows=full_rows,
                attended=attended,
                mixed=mixed,
                w_down=w_out.reshape(-1, width),
            ),
            3,
        )
        block_out, grad_input, small = (done[n] for n in ("block_out", "grad_input", "small"))
        grad_w_in, grad_w_out = place_pairs(done["kept"], done["got"], shapes)
        attn_sum = done["attn_kept"].astype(f32) + done["attn_got"].astype(f32)
    else:
        grad_rows_two = dot(back, w_in.reshape(-1, width), (0, 0)) + dot(logits, router_rows, (0, 0))
        grad_normed_two = scatter_sum(grad_rows_two.astype(bf16), True, 3)
        hat_two, factor_two = normalize(x_mid)
        grad_from_moe, grad_moe_gain = norm_back(grad_normed_two, hat_two, factor_two, moe_gain)
        grad_mid = out_cotangent.astype(f32) + grad_from_moe
        grad_full = gather(grad_mid.astype(bf16), False, 4)

        heads_part, grad_pre = local_call(
            functools.partial(attention_back_kernel, head_size, score_scale),
            "attention_back",
            [
                jax.ShapeDtypeStruct((seq_len, width), bf16),
                jax.ShapeDtypeStruct((seq_len, q_width + kv_width), bf16),
            ],
            [
                pltpu.VMEM((seq_len, seq_len), f32),
                pltpu.VMEM((q_width, seq_len), f32),
                pltpu.VMEM((seq_len, kv_width), f32),
                pltpu.VMEM((seq_len, q_width), bf16),
            ],
            (
                grad_full,
                w_output,
                query_rows,
                keyval_rows,
                log_total,
                w_query,
                keyval_flat,
                        doc_row,
                *tables,
            ),
        )
        attn_weights = local_call(
            attention_weights_kernel,
            "attention_weights",
            [jax.ShapeDtypeStruct((width, all_width), bf16)],
            [],
            (full_rows, grad_pre, grad_full, attended),
        )
        grad_normed_one = scatter_sum(heads_part, False, 6)
        hat_one, factor_one = normalize(activations.astype(f32))
        grad_from_attn, grad_attn_gain = norm_back(grad_normed_one, hat_one, factor_one, attn_gain)
        grad_input = grad_mid + grad_from_attn

        expert_part = dot(mixed, w_out.reshape(-1, width), (0, 0)).astype(bf16)
        block_out = (x_mid + scatter_sum(expert_part, True, 5)).astype(bf16)

        halves = attn_weights[0].reshape(dp_count, ep_count, -1, all_width)
        kept = lax.dynamic_index_in_dim(halves, e_index, 1, keepdims=False)
        given = lax.dynamic_index_in_dim(halves, 1 - e_index, 1, keepdims=False)
        got = lax.ppermute(given, "ep", [(0, 1), (1, 0)])
        attn_sum = halved_over_dp((kept.astype(f32) + got.astype(f32)).astype(bf16))
        summed = []
        for keep in keeps:
            for k in range(keep.shape[0]):
                parts = jnp.moveaxis(keep[k].reshape(-1, dp_count, columns), 1, 0)
                summed.append(halved_over_dp(parts))
        summed = jnp.stack(summed)
        ins = pair * 2 * hidden
        grad_w_in = summed[:, :ins].reshape(shapes[0])
        grad_w_out = summed[:, ins:].reshape(shapes[1])
        small = summed_everywhere(
            jnp.concatenate(
                [grad_w_router[:expert_count], grad_moe_gain[None], grad_attn_gain[None]]
            )
        )
    grad_w_query = attn_sum[:, :q_width]
    grad_w_keyval = attn_sum[:, q_width : q_width + kv_width].reshape(-1, kv_heads, 2 * head_size)
    grad_w_output = attn_sum[:, q_width + kv_width :].T
    grad_w_router = small[:expert_count].T
    grad_moe_gain, grad_attn_gain = small[expert_count], small[expert_count + 1]
    return (
        block_out,
        grad_input,
        grad_attn_gain,
        grad_w_query,
        grad_w_keyval,
        grad_w_output,
        grad_moe_gain,
        grad_w_router,
        grad_w_in,
        grad_w_out,
    )


def solution(mesh):
    return jax.shard_map(
        per_device,
        mesh=mesh,
        in_specs=(
            P(("dp", "ep", "tp"), None),
            P(("dp", "ep"), None),
            P(("dp", "ep", "tp"), None),
            P(),
            P(None, "tp"),
            P(None, "tp", None),
            P("tp", None),
            P(),
            P(),
            P("ep", None, "tp", None),
            P("ep", "tp", None),
            P(("dp", "ep", "tp"), None),
        ),
        out_specs=(
            P(("dp", "ep", "tp"), None),
            P(("dp", "ep", "tp"), None),
            P(),
            P(("dp", "ep"), "tp"),
            P(("dp", "ep"), "tp", None),
            P("tp", ("dp", "ep")),
            P(),
            P(),
            P("ep", None, "tp", "dp"),
            P("ep", "tp", "dp"),
        ),
        check_vma=False,
    )
```

```python
import functools
import math
import types

import jax
import jax.numpy as jnp
from jax import lax
from jax.experimental import pallas as pl
from jax.experimental.pallas import tpu as pltpu
from jax.sharding import PartitionSpec as P

eps_norm = 1e-05
rope_base = 10000.0
neg_fill = -1000000000.0
MESH = pl.DeviceIdType.MESH
bf16 = jnp.bfloat16
f32 = jnp.float32


def greet(partners):
    barrier = pltpu.get_barrier_semaphore()
    for partner in partners:
        pl.semaphore_signal(barrier, inc=1, device_id=partner, device_id_type=MESH)
    pl.semaphore_wait(barrier, len(partners))


def rows_at(start, count):
    return pl.ds(pl.multiple_of(start, count), count)


def gather_kernel(with_ep, block_ref, *refs):
    whole_ref, local_sem, send_sem, recv_sem = refs[-4:]
    rows = block_ref.shape[0]
    half = rows // 2
    t, e = lax.axis_index("tp"), lax.axis_index("ep")
    near, far = {"tp": t ^ 1}, {"tp": t ^ 2}
    twin = {"ep": 1 - e}
    greet((near, far, twin) if with_ep else (near, far))
    tp = lax.axis_size("tp")
    base = e * (tp * rows) if with_ep else 0

    def place(tt, part, count):
        return whole_ref.at[rows_at(base + tt * rows + part * half, count)]

    def send(src, dst, k, device):
        copy = pltpu.make_async_remote_copy(
            src, dst, send_sem.at[k], recv_sem.at[k], device_id=device, device_id_type=MESH
        )
        copy.start()
        return copy

    def own(part):
        return block_ref.at[pl.ds(part * half, half)]

    local = pltpu.make_async_copy(block_ref, place(t, 0, rows), local_sem)
    near_a = send(own(0), place(t, 0, half), 0, near)
    far_b = send(own(1), place(t, 1, half), 1, far)
    near_b = send(own(1), place(t, 1, half), 2, near)
    far_a = send(own(0), place(t, 0, half), 3, far)
    local.start()
    copies = [near_a, far_b, near_b, far_a]
    if with_ep:
        twin_own = send(block_ref, place(t, 0, rows), 6, twin)
        copies.append(twin_own)
    near_a.wait_recv()
    on_a = send(place(t ^ 1, 0, half), place(t ^ 1, 0, half), 4, far)
    far_b.wait_recv()
    on_b = send(place(t ^ 2, 1, half), place(t ^ 2, 1, half), 5, near)
    near_b.wait_recv()
    far_a.wait_recv()
    if with_ep:
        twin_near = send(place(t ^ 1, 0, rows), place(t ^ 1, 0, rows), 7, twin)
        twin_far = send(place(t ^ 2, 0, rows), place(t ^ 2, 0, rows), 8, twin)
    on_a.wait_recv()
    on_b.wait_recv()
    if with_ep:
        twin_diag = send(place(t ^ 3, 0, rows), place(t ^ 3, 0, rows), 9, twin)
        for copy in (twin_own, twin_near, twin_far, twin_diag):
            copy.wait_recv()
        copies += [twin_near, twin_far, twin_diag]
    local.wait()
    for copy in copies + [on_a, on_b]:
        copy.wait_send()


def gather(block, with_ep, collective_id, after=()):
    rows, width = block.shape
    count = lax.axis_size("tp") * (lax.axis_size("ep") if with_ep else 1)
    return pl.pallas_call(
        functools.partial(gather_kernel, with_ep),
        out_shape=jax.ShapeDtypeStruct((count * rows, width), block.dtype),
        in_specs=[pl.BlockSpec(memory_space=pl.ANY)] * (1 + len(after)),
        out_specs=pl.BlockSpec(memory_space=pl.ANY),
        scratch_shapes=[
            pltpu.SemaphoreType.DMA,
            pltpu.SemaphoreType.DMA((10,)),
            pltpu.SemaphoreType.DMA((10,)),
        ],
        name="gather_plane" if with_ep else "gather_tp",
        cost_estimate=pl.CostEstimate(flops=0, bytes_accessed=10**6, transcendentals=0),
        compiler_params=pltpu.CompilerParams(
            collective_id=collective_id, has_side_effects=True, vmem_limit_bytes=16 * 2**20
        ),
    )(block, *after)


def scatter_kernel(with_ep, part_ref, *refs):
    sum_ref, mine, twins, arrived, passed, local_sem, send_sem, recv_sem = refs[-8:]
    rows = sum_ref.shape[0]
    half = rows // 2
    t, e = lax.axis_index("tp"), lax.axis_index("ep")
    tp = lax.axis_size("tp")
    near, far = {"tp": t ^ 1}, {"tp": t ^ 2}
    twin = {"ep": 1 - e}
    greet((near, far, twin) if with_ep else (near, far))
    base = e * (tp * rows) if with_ep else 0
    other = (1 - e) * (tp * rows)

    def send(src, dst, k, device):
        copy = pltpu.make_async_remote_copy(
            src, dst, send_sem.at[k], recv_sem.at[k], device_id=device, device_id_type=MESH
        )
        copy.start()
        return copy

    order = (3, 1, 2, 0)
    locals_, twin_copies = {}, {}
    for k in order:
        if with_ep:
            twin_copies[k] = send(
                part_ref.at[rows_at(other + (t ^ k) * rows, rows)], twins.at[k], k, twin
            )
        locals_[k] = pltpu.make_async_copy(
            part_ref.at[rows_at(base + (t ^ k) * rows, rows)], mine.at[k], local_sem.at[k]
        )
        locals_[k].start()

    def ready(k):
        locals_[k].wait()
        if with_ep:
            twin_copies[k].wait_recv()
            mine[k] = (mine[k].astype(f32) + twins[k].astype(f32)).astype(mine.dtype)

    first, second = pl.ds(0, half), pl.ds(half, half)
    ready(3)
    a_on = send(mine.at[3, first], arrived.at[0, 0], 4, near)
    b_on = send(mine.at[3, second], arrived.at[1, 0], 5, far)
    ready(1)
    a_own = send(mine.at[1, first], arrived.at[0, 1], 6, near)
    ready(2)
    b_own = send(mine.at[2, second], arrived.at[1, 1], 7, far)
    ready(0)
    a_on.wait_recv()
    mine[2, first] = (mine[2, first].astype(f32) + arrived[0, 0].astype(f32)).astype(mine.dtype)
    a_last = send(mine.at[2, first], passed.at[0], 8, far)
    b_on.wait_recv()
    mine[1, second] = (mine[1, second].astype(f32) + arrived[1, 0].astype(f32)).astype(mine.dtype)
    b_last = send(mine.at[1, second], passed.at[1], 9, near)
    a_own.wait_recv()
    b_own.wait_recv()
    a_last.wait_recv()
    sum_ref[first] = (
        mine[0, first].astype(f32) + arrived[0, 1].astype(f32) + passed[0].astype(f32)
    ).astype(sum_ref.dtype)
    b_last.wait_recv()
    sum_ref[second] = (
        mine[0, second].astype(f32) + arrived[1, 1].astype(f32) + passed[1].astype(f32)
    ).astype(sum_ref.dtype)
    copies = [a_on, b_on, a_own, b_own, a_last, b_last]
    if with_ep:
        copies += list(twin_copies.values())
    for copy in copies:
        copy.wait_send()


def scatter_sum(parts, with_ep, collective_id, after=()):
    count = lax.axis_size("tp") * (lax.axis_size("ep") if with_ep else 1)
    rows, width = parts.shape[0] // count, parts.shape[1]
    return pl.pallas_call(
        functools.partial(scatter_kernel, with_ep),
        out_shape=jax.ShapeDtypeStruct((rows, width), f32),
        in_specs=[pl.BlockSpec(memory_space=pl.ANY)] * (1 + len(after)),
        out_specs=pl.BlockSpec(memory_space=pltpu.VMEM),
        scratch_shapes=[
            pltpu.VMEM((4, rows, width), bf16),
            pltpu.VMEM((4, rows, width) if with_ep else (4, 16, 128), bf16),
            pltpu.VMEM((2, 2, rows // 2, width), bf16),
            pltpu.VMEM((2, rows // 2, width), bf16),
            pltpu.SemaphoreType.DMA((4,)),
            pltpu.SemaphoreType.DMA((10,)),
            pltpu.SemaphoreType.DMA((10,)),
        ],
        name="scatter_plane" if with_ep else "scatter_tp",
        cost_estimate=pl.CostEstimate(flops=0, bytes_accessed=10**6, transcendentals=0),
        compiler_params=pltpu.CompilerParams(
            collective_id=collective_id, has_side_effects=True, vmem_limit_bytes=24 * 2**20
        ),
    )(parts, *after)


def halve(blocks, step):
    dp = lax.axis_size("dp")
    bit = (lax.axis_index("dp") // step) % 2
    pairs = blocks.reshape(-1, 2, *blocks.shape[1:])
    kept = lax.dynamic_index_in_dim(pairs, bit, 1, keepdims=False)
    given = lax.dynamic_index_in_dim(pairs, 1 - bit, 1, keepdims=False)
    got = lax.ppermute(given, "dp", [(i, i ^ step) for i in range(dp)])
    total = kept.astype(f32) + got.astype(f32)
    return total if 2 * step == dp else total.astype(bf16)


def halved_over_dp(blocks):
    dp = lax.axis_size("dp")
    if dp & (dp - 1):
        return lax.psum_scatter(blocks, "dp", scatter_dimension=0, tiled=False).astype(f32)
    step = 1
    while step < dp:
        blocks = halve(blocks, step)
        step *= 2
    return blocks[0].astype(f32)


def swapped(matrix, half):
    lane = lax.broadcasted_iota(jnp.int32, matrix.shape, 1)
    width = matrix.shape[1]
    return jnp.where(
        lane % (2 * half) < half,
        pltpu.roll(matrix, width - half, 1),
        pltpu.roll(matrix, half, 1),
    )


def rotated(matrix, tables, half, back):
    cosine, sine = tables
    times = matrix.shape[1] // cosine.shape[1]
    cosine, sine = (jnp.concatenate([t] * times, axis=1) for t in (cosine, sine))
    return matrix * cosine + swapped(matrix, half) * (-sine if back else sine)


def mask_into(bias_ref, row_ref):
    shape = bias_ref.shape
    key = lax.broadcasted_iota(jnp.int32, shape, 0)
    query = lax.broadcasted_iota(jnp.int32, shape, 1)
    column = jnp.broadcast_to(row_ref[:1], (128, shape[0])).T
    allowed = (column[:, :1] == row_ref[:1]) & (key <= query)
    bias_ref[...] = jnp.where(allowed, 0.0, neg_fill)


def head_cuts(head, kv_heads, q_heads, size):
    group = head // (q_heads // kv_heads)
    return (
        slice(head * size, (head + 1) * size),
        slice(2 * group * size, (2 * group + 1) * size),
        slice((2 * group + 1) * size, (2 * group + 2) * size),
    )


def attention_steps(
    size, scale, x_ref, gain_ref, query_ref, keyval_ref, tables, rows_ref, q_ref, kv_ref, total_ref, attended_ref,
    bias_ref, turned_ref,
):
    cos_ref, sin_ref, kcos_ref, ksin_ref = tables
    x = x_ref[...].astype(f32)
    factor = lax.rsqrt(jnp.mean(x * x, axis=-1, keepdims=True) + eps_norm)
    rows_ref[...] = (x * factor * gain_ref[:1]).astype(bf16)
    rows = rows_ref[...]
    q = jnp.dot(rows, query_ref[...], preferred_element_type=f32)
    q_ref[...] = rotated(q, (cos_ref[...], sin_ref[...]), size // 2, False).astype(bf16)
    kv = jnp.dot(rows, keyval_ref[...], preferred_element_type=f32)
    kv_ref[...] = rotated(kv, (kcos_ref[...], ksin_ref[...]), size // 2, False).astype(bf16)
    length = x.shape[0]
    tile = length // 2
    q_heads, kv_heads = q_ref.shape[1] // size, kv_ref.shape[1] // (2 * size)
    total_ref[...] = jnp.zeros_like(total_ref)
    for block in range(2):
        now, past = slice(block * tile, (block + 1) * tile), slice(0, (block + 1) * tile)
        for head in range(q_heads):
            at, key_at, value_at = head_cuts(head, kv_heads, q_heads, size)
            scores = dot(kv_ref[past, key_at], q_ref[now, at], (1, 1)) * scale + bias_ref[past, now]
            peak = jnp.max(scores, axis=0, keepdims=True)
            weight = jnp.exp(scores - peak)
            total = jnp.sum(weight, axis=0, keepdims=True)
            probs = (weight * (1.0 / total)).astype(bf16)
            total_ref[head : head + 1, now] = peak + jnp.log(total)
            turned_ref[at, now] = dot(kv_ref[past, value_at], probs, (0, 0))
    attended_ref[...] = turned_ref[...].T.astype(bf16)


def front_kernel(
    size, scale, x_ref, gain_ref, query_ref, keyval_ref, out_ref, row_ref, cos_ref, sin_ref,
    kcos_ref, ksin_ref, rows_out, q_out, kv_out, attended_out, total_ref, mid_ref, plane_ref, rows_ref, q_ref,
    kv_ref, attended_ref, x_whole, bias_ref, turned_ref, mine, arrived, passed, out_sem, x_s, x_r, h_s, h_r, p_s,
    p_r,
):
    t, e = lax.axis_index("tp"), lax.axis_index("ep")
    near, far, twin = {"tp": t ^ 1}, {"tp": t ^ 2}, {"ep": 1 - e}
    rows = x_ref.shape[0]
    half = rows // 2
    first, second = pl.ds(0, half), pl.ds(half, half)
    greet((near, far, twin))

    def link(send_sem, recv_sem):
        def send(src, dst, k, device):
            copy = pltpu.make_async_remote_copy(
                src, dst, send_sem.at[k], recv_sem.at[k], device_id=device, device_id_type=MESH
            )
            copy.start()
            return copy

        return send

    unsent = []

    def spread(send, whole, base, between, with_twin):
        def place(tt, part, count):
            return whole.at[rows_at(base + tt * rows + part * half, count)]

        def on(tt, part, count, k, device):
            copy = send(place(tt, part, count), place(tt, part, count), k, device)
            unsent.append(copy)
            return copy

        near_a, far_b = on(t, 0, half, 0, near), on(t, 1, half, 1, far)
        near_b, far_a = on(t, 1, half, 2, near), on(t, 0, half, 3, far)
        twins = [on(t, 0, rows, 6, twin)] if with_twin else []
        between()
        near_a.wait_recv()
        on_a = on(t ^ 1, 0, half, 4, far)
        far_b.wait_recv()
        on_b = on(t ^ 2, 1, half, 5, near)
        near_b.wait_recv()
        far_a.wait_recv()
        if with_twin:
            twins += [on(t ^ k, 0, rows, 6 + k, twin) for k in (1, 2)]
        on_a.wait_recv()
        on_b.wait_recv()
        if with_twin:
            twins.append(on(t ^ 3, 0, rows, 9, twin))
        for copy in twins:
            copy.wait_recv()

    x_whole[rows_at(t * rows, rows)] = x_ref[...]
    spread(link(x_s, x_r), x_whole, 0, lambda: mask_into(bias_ref, row_ref), False)
    attention_steps(
        size, scale, x_whole, gain_ref, query_ref, keyval_ref, (cos_ref, sin_ref, kcos_ref, ksin_ref),
        rows_ref, q_ref, kv_ref, total_ref, attended_ref, bias_ref, turned_ref,
    )
    late = ((rows_ref, rows_out), (q_ref, q_out), (kv_ref, kv_out), (attended_ref, attended_out))
    leaving = [pltpu.make_async_copy(a, b, out_sem.at[k]) for k, (a, b) in enumerate(late)]
    send = link(h_s, h_r)

    def bring(k):
        block = attended_ref[rows_at((t ^ k) * rows, rows)]
        mine[k] = jnp.dot(block, out_ref[...], preferred_element_type=f32).astype(bf16)

    def added(k, cut, *others):
        total = mine[k, cut].astype(f32)
        for other in others:
            total += other.astype(f32)
        return total

    bring(3)
    a_on = send(mine.at[3, first], arrived.at[0, 0], 0, near)
    b_on = send(mine.at[3, second], arrived.at[1, 0], 1, far)
    bring(1)
    a_own = send(mine.at[1, first], arrived.at[0, 1], 2, near)
    bring(2)
    b_own = send(mine.at[2, second], arrived.at[1, 1], 3, far)
    bring(0)
    for copy in leaving:
        copy.start()
    a_on.wait_recv()
    mine[2, first] = added(2, first, arrived[0, 0]).astype(bf16)
    a_last = send(mine.at[2, first], passed.at[0], 4, far)
    b_on.wait_recv()
    mine[1, second] = added(1, second, arrived[1, 0]).astype(bf16)
    b_last = send(mine.at[1, second], passed.at[1], 5, near)
    a_own.wait_recv()
    b_own.wait_recv()
    a_last.wait_recv()
    mid_ref[first] = x_ref[first].astype(f32) + added(0, first, arrived[0, 1], passed[0])
    b_last.wait_recv()
    mid_ref[second] = x_ref[second].astype(f32) + added(0, second, arrived[1, 1], passed[1])
    unsent.extend((a_on, b_on, a_own, b_own, a_last, b_last))
    x_mid = mid_ref[...]
    factor = lax.rsqrt(jnp.mean(x_mid * x_mid, axis=-1, keepdims=True) + eps_norm)
    base = e * (lax.axis_size("tp") * rows)
    plane_ref[rows_at(base + t * rows, rows)] = (x_mid * factor * gain_ref[1:2]).astype(bf16)
    spread(link(p_s, p_r), plane_ref, base, lambda: None, True)
    for copy in leaving:
        copy.wait()
    for copy in unsent:
        copy.wait_send()


def front(size, scale, x, gains, w_query, keyval, w_output, row, tables, collective_id):
    rows, width = x.shape
    length = row.shape[1]
    q_width, kv_width = w_query.shape[1], keyval.shape[1]
    shape, dma = jax.ShapeDtypeStruct, pltpu.SemaphoreType.DMA
    spec = pl.BlockSpec(memory_space=pltpu.VMEM)
    late = [
        shape((length, width), bf16),
        shape((length, q_width), bf16),
        shape((length, kv_width), bf16),
        shape((length, q_width), bf16),
    ]
    outs = late + [
        shape((-(-q_width // (8 * size)) * 8, length), f32),
        shape((rows, width), f32),
        shape((2 * length, width), bf16),
    ]
    return pl.pallas_call(
        functools.partial(front_kernel, size, scale),
        out_shape=outs,
        in_specs=[spec] * 10,
        out_specs=[pl.BlockSpec(memory_space=pl.ANY)] * 4 + [spec] * 3,
        scratch_shapes=[
            *(pltpu.VMEM(part.shape, part.dtype) for part in late),
            pltpu.VMEM((length, width), bf16),
            pltpu.VMEM((length, length), f32),
            pltpu.VMEM((q_width, length), f32),
            pltpu.VMEM((4, rows, width), bf16),
            pltpu.VMEM((2, 2, rows // 2, width), bf16),
            pltpu.VMEM((2, rows // 2, width), bf16),
            dma((4,)),
            *([dma((6,))] * 4),
            *([dma((10,))] * 2),
        ],
        name="front",
        cost_estimate=pl.CostEstimate(flops=10**9, bytes_accessed=10**6, transcendentals=0),
        compiler_params=pltpu.CompilerParams(
            collective_id=collective_id, has_side_effects=True, vmem_limit_bytes=58 * 2**20
        ),
    )(x, gains, w_query, keyval, w_output, row, *tables)


def attention_back_steps(
    size, scale, grad_ref, out_ref, q_ref, kv_ref, total_ref, tables, pre_ref, bias_ref, turned_ref,
    kv_grad_ref, heads_ref,
):
    heads_ref[...] = dot(grad_ref[...], out_ref[...], (1, 1)).astype(bf16)
    length = q_ref.shape[0]
    tile = length // 2
    q_heads, kv_heads = q_ref.shape[1] // size, kv_ref.shape[1] // (2 * size)
    for block in range(2):
        now, past = slice(block * tile, (block + 1) * tile), slice(0, (block + 1) * tile)
        for head in range(q_heads):
            at, key_at, value_at = head_cuts(head, kv_heads, q_heads, size)
            keys, query, grad = kv_ref[past, key_at], q_ref[now, at], heads_ref[now, at]
            scores = dot(keys, query, (1, 1)) * scale + bias_ref[past, now]
            probs = jnp.exp(scores - total_ref[head : head + 1, now])
            grad_probs = dot(kv_ref[past, value_at], grad, (1, 1))
            inner = jnp.sum(probs * grad_probs, axis=0, keepdims=True)
            grad_scores = (probs * (grad_probs - inner)).astype(bf16)
            turned_ref[at, now] = dot(keys, grad_scores, (0, 0)) * scale
            kv_grad_ref[past, key_at] += dot(grad_scores, query, (1, 0)) * scale
            kv_grad_ref[past, value_at] += dot(probs.astype(bf16), grad, (1, 0))
    width = q_ref.shape[1]
    cos_ref, sin_ref, kcos_ref, ksin_ref = tables
    pre_ref[:, :width] = rotated(
        turned_ref[...].T, (cos_ref[...], sin_ref[...]), size // 2, True
    ).astype(bf16)
    pre_ref[:, width:] = rotated(
        kv_grad_ref[...], (kcos_ref[...], ksin_ref[...]), size // 2, True
    ).astype(bf16)


def attention_back_kernel(
    size, scale, grad_ref, out_ref, q_ref, kv_ref, total_ref, query_ref, keyval_ref, row_ref,
    cos_ref, sin_ref, kcos_ref, ksin_ref, *refs,
):
    part_ref, pre_ref, bias_ref, turned_ref, kv_grad_ref, heads_ref = refs[-6:]
    mask_into(bias_ref, row_ref)
    kv_grad_ref[...] = jnp.zeros_like(kv_grad_ref)
    attention_back_steps(
        size, scale, grad_ref, out_ref, q_ref, kv_ref, total_ref, (cos_ref, sin_ref, kcos_ref, ksin_ref),
        pre_ref, bias_ref, turned_ref, kv_grad_ref, heads_ref,
    )
    width = q_ref.shape[1]
    part_ref[...] = (
        dot(pre_ref[:, :width], query_ref[...], (1, 1))
        + dot(pre_ref[:, width:], keyval_ref[...], (1, 1))
    ).astype(bf16)


def local_call(body, name, out_shape, scratch, args, after=(), limit=48):
    spec = pl.BlockSpec(memory_space=pltpu.VMEM)
    return pl.pallas_call(
        body,
        out_shape=out_shape,
        in_specs=[spec] * len(args) + [pl.BlockSpec(memory_space=pl.ANY)] * len(after),
        out_specs=jax.tree.map(lambda _: spec, out_shape),
        scratch_shapes=scratch,
        name=name,
        cost_estimate=pl.CostEstimate(flops=10**6, bytes_accessed=10**6, transcendentals=0),
        compiler_params=pltpu.CompilerParams(vmem_limit_bytes=limit * 2**20),
    )(*args, *after)


def attention_weights_kernel(rows_ref, pre_ref, grad_ref, attended_ref, *outs):
    width, pre = rows_ref.shape[1], pre_ref.shape[1]
    parts = outs[0].shape[0] if len(outs) == 2 else 4
    d, e = lax.axis_index("dp"), lax.axis_index("ep")
    step = width // parts
    for c in range(parts):
        cut = slice(c * step, (c + 1) * step)
        first = dot(rows_ref[:, cut], pre_ref[...], (0, 0)).astype(bf16)
        second = dot(grad_ref[:, cut], attended_ref[...], (0, 0)).astype(bf16)
        if len(outs) == 1:
            outs[0][cut, :pre] = first
            outs[0][cut, pre:] = second
            continue
        for half in range(2):
            some = slice(half * (step // 2), (half + 1) * (step // 2))
            for mine in range(2):

                @pl.when((half == e) == (mine == 1))
                def _():
                    out_ref = outs[0] if mine else outs[1]
                    out_ref[d ^ c, :, :pre] = first[some]
                    out_ref[d ^ c, :, pre:] = second[some]


def exchanged(blocks, step):
    return lax.ppermute(blocks, "dp", [(i, i ^ step) for i in range(lax.axis_size("dp"))])


def summed_everywhere(value):
    for axis in ("ep", "tp", "dp"):
        size, step = lax.axis_size(axis), 1
        if size & (size - 1):
            value = lax.psum(value, axis)
            continue
        while step < size:
            value = value + lax.ppermute(value, axis, [(i, i ^ step) for i in range(size)])
            step *= 2
    return value


def dot(a, b, dims):
    return lax.dot_general(a, b, ((dims[:1], dims[1:]), ((), ())), preferred_element_type=f32)


def experts_kernel(first, local_experts, is_last, held, *refs):
    if first == 0:
        rows_ref, grad_ref, router_ref, in_ref, out_ref = refs[:5]
        gates_ref, terms_ref, back_ref, mixed_ref, keep_ref, *give_refs = refs[5:]
    else:
        rows_ref, grad_ref, gates_ref, in_ref, out_ref = refs[:5]
        terms_in = refs[7]
        outs = refs[8 + held :]
        if is_last:
            logits_ref, router_grad_ref, *outs = outs
        terms_ref, back_ref, mixed_ref, keep_ref, *give_refs = outs
    tokens, width = rows_ref.shape
    pair, _, hidden, _ = in_ref.shape
    tile = 256 if tokens % 256 == 0 else tokens
    number = pl.program_id(0) + first

    if first == 0:
        logits = jnp.dot(rows_ref[...], router_ref[...], preferred_element_type=f32)
        used = grad_ref[:, width:].astype(f32) > 0.5
        peak = jnp.max(jnp.where(used, logits, -jnp.inf), axis=-1, keepdims=True)
        weight = jnp.where(used, jnp.exp(jnp.where(used, logits - peak, 0.0)), 0.0)
        gates = weight / jnp.sum(weight, axis=-1, keepdims=True)
        gates_ref[...] = gates.T[: gates_ref.shape[0]]
    if first == 0:
        terms_ref[...] = jnp.zeros_like(terms_ref)
    else:

        @pl.when(pl.program_id(0) == 0)
        def _():
            terms_ref[...] = terms_in[...]

    into = in_ref[...].reshape(pair * 2 * hidden, width)
    out_of = out_ref[...].reshape(pair * hidden, width)
    base = lax.axis_index("ep") * local_experts + number * pair

    @pl.loop(0, tokens // tile)
    def _(j):
        now = pl.ds(pl.multiple_of(j * tile, tile), tile)
        gate_up = dot(into, rows_ref[now, :], (1, 1))
        down = dot(out_of, grad_ref[now, :width], (1, 1))
        for k in range(pair):
            gate = gate_up[2 * k * hidden : (2 * k + 1) * hidden]
            up = gate_up[(2 * k + 1) * hidden : (2 * k + 2) * hidden]
            back = down[k * hidden : (k + 1) * hidden]
            g = gates_ref[pl.ds(base + k, 1), now]
            sig = 1.0 / (1.0 + jnp.exp(-gate))
            silu = gate * sig
            active = silu * up
            terms_ref[pl.ds(base + k, 1), now] = jnp.sum(active * back, axis=0, keepdims=True)
            mixed_ref[k * hidden : (k + 1) * hidden, now] = (g * active).astype(bf16)
            grad_active = g * back
            back_ref[2 * k * hidden : (2 * k + 1) * hidden, now] = (
                grad_active * up * (sig * (1.0 + gate * (1.0 - sig)))
            ).astype(bf16)
            back_ref[(2 * k + 1) * hidden : (2 * k + 2) * hidden, now] = (
                grad_active * silu
            ).astype(bf16)

    columns = keep_ref.shape[3]
    blocks = width // columns
    ins = pair * 2 * hidden
    for at in range(0, pair * 3 * hidden, pair * hidden):
        if at < ins:
            total = jnp.dot(
                back_ref[at : at + pair * hidden], rows_ref[...], preferred_element_type=f32
            )
        else:
            total = jnp.dot(mixed_ref[...], grad_ref[:, :width], preferred_element_type=f32)
        total = total.astype(bf16)
        if blocks == 1:
            keep_ref[0, 0, at : at + pair * hidden] = total
            continue
        for c in range(blocks):
            apart = c ^ lax.axis_index("dp")
            part = total[:, c * columns : (c + 1) * columns]

            @pl.when(apart % 2 == 0)
            def _():
                keep_ref[0, apart // 2, at : at + pair * hidden] = part

            @pl.when(apart % 2 == 1)
            def _():
                give_refs[0][0, apart // 2, at : at + pair * hidden] = part

    if is_last:

        @pl.when(pl.program_id(0) == pl.num_programs(0) - 1)
        def _():
            gates, terms = gates_ref[...], terms_ref[...]
            logits = gates * (terms - jnp.sum(gates * terms, axis=0, keepdims=True))
            high = logits.astype(bf16)
            rows = logits.shape[0]
            logits_ref[:rows] = high
            logits_ref[rows:] = (logits - high.astype(f32)).astype(bf16)
            both = jnp.dot(logits_ref[...], rows_ref[...], preferred_element_type=f32)
            router_grad_ref[...] = both[:rows] + both[rows:]


def experts(
    first, count, blocks, rows_two, plane_grad, gates_or_router, w_in, w_out, earlier=(), after=()
):
    local_experts, _, hidden, width = w_in.shape
    tokens = rows_two.shape[0]
    pair = 2 if local_experts % 2 == 0 else 1
    pairs = local_experts // pair
    gate_rows = -(-local_experts * lax.axis_size("ep") // 8) * 8
    is_last = first + count == pairs
    spread = (max(blocks // 2, 1), pair * 3 * hidden, width // blocks)
    given = 1 if blocks > 1 else 0

    def whole(array):
        return pl.BlockSpec(array.shape, lambda i: (0,) * array.ndim, pipeline_mode=pl.Buffered(1))

    in_specs = [
        whole(rows_two),
        whole(plane_grad),
        whole(gates_or_router),
        pl.BlockSpec((pair, 2, hidden, width), lambda i: (i + first, 0, 0, 0)),
        pl.BlockSpec((pair, hidden, width), lambda i: (i + first, 0, 0)),
    ]
    if earlier:
        in_specs += [pl.BlockSpec(memory_space=pl.ANY)] * 2 + [whole(earlier[2])]
    in_specs += [pl.BlockSpec(memory_space=pl.ANY)] * len(after)
    out_shape = [
        jax.ShapeDtypeStruct((gate_rows, tokens), f32),
        jax.ShapeDtypeStruct((local_experts * 2 * hidden, tokens), bf16),
        jax.ShapeDtypeStruct((local_experts * hidden, tokens), bf16),
        jax.ShapeDtypeStruct((count, *spread), bf16),
    ] + [jax.ShapeDtypeStruct((count, *spread), bf16)] * given
    out_specs = [
        pl.BlockSpec((gate_rows, tokens), lambda i: (0, 0)),
        pl.BlockSpec((pair * 2 * hidden, tokens), lambda i: (i + first, 0)),
        pl.BlockSpec((pair * hidden, tokens), lambda i: (i + first, 0)),
        pl.BlockSpec((1, *spread), lambda i: (i, 0, 0, 0)),
    ] + [pl.BlockSpec((1, *spread), lambda i: (i, 0, 0, 0))] * given
    aliases = {}
    if first == 0:
        out_shape.insert(0, jax.ShapeDtypeStruct((gate_rows, tokens), f32))
        out_specs.insert(0, pl.BlockSpec((gate_rows, tokens), lambda i: (0, 0)))
    else:
        aliases = {5: 1 + 2 * is_last, 6: 2 + 2 * is_last}
    if is_last:
        out_shape = [
            jax.ShapeDtypeStruct((2 * gate_rows, tokens), bf16),
            jax.ShapeDtypeStruct((gate_rows, width), f32),
        ] + out_shape
        out_specs = [
            pl.BlockSpec((2 * gate_rows, tokens), lambda i: (0, 0)),
            pl.BlockSpec((gate_rows, width), lambda i: (0, 0)),
        ] + out_specs
    return pl.pallas_call(
        functools.partial(experts_kernel, first, local_experts, is_last, len(after)),
        grid=(count,),
        out_shape=out_shape,
        in_specs=in_specs,
        out_specs=out_specs,
        input_output_aliases=aliases,
        name=f"experts_{first}",
        cost_estimate=pl.CostEstimate(
            flops=10**6, bytes_accessed=10**6, transcendentals=0
        ),
        compiler_params=pltpu.CompilerParams(vmem_limit_bytes=44 * 2**20),
    )(rows_two, plane_grad, gates_or_router, w_in, w_out, *earlier, *after)


def rope_tables(length, head_size):
    half_size = head_size // 2
    frequency = jnp.exp(
        jnp.arange(half_size, dtype=f32) * (-2.0 * math.log(rope_base) / head_size)
    )
    angles = jnp.arange(length, dtype=f32)[:, None] * frequency[None, :]
    cosine, sine = jnp.cos(angles), jnp.sin(angles)
    one_cos = jnp.concatenate([cosine, cosine], axis=1)
    one_sin = jnp.concatenate([-sine, sine], axis=1)
    return (
        jnp.concatenate([one_cos, one_cos], axis=1),
        jnp.concatenate([one_sin, one_sin], axis=1),
        jnp.concatenate([one_cos, jnp.ones_like(one_cos)], axis=1),
        jnp.concatenate([one_sin, jnp.zeros_like(one_sin)], axis=1),
    )


def normalize(matrix):
    factor = lax.rsqrt(jnp.mean(matrix * matrix, axis=-1, keepdims=True) + eps_norm)
    return (matrix * factor, factor)


def norm_back(grad_normed, normed_hat, factor, gain):
    grad_hat = grad_normed * gain
    grad_inner = jnp.mean(grad_hat * normed_hat, axis=-1, keepdims=True)
    return (
        factor * (grad_hat - normed_hat * grad_inner),
        jnp.sum(grad_normed * normed_hat, axis=0),
    )


tail_late = list(
    dict(
        got_a=0, got_b=0, w_output=0, q=0, kv=0, w_query=0, keyval=0, rows=0, attended=0
    )
)
tail_first = list(
    dict(
        back=0, w_up=0
    )
)
tail_last = list(
    dict(
        mixed=0, w_down=0
    )
)
tail_held = list(
    dict(
        keep_a=0, keep_b=0, keep_c=0, keep_rest=0, give_c=0, give_rest=0
    )
)
tail_near = list(
    dict(
        x_mid=0, grad=0, x=0, gains=0, router=0, router_rows=0, logits=0, total=0, row=0, cosine=0,
        sine=0, kcosine=0, ksine=0
    )
)
tail_out = list(
    dict(
        kept=0, got=0, attn_kept=0, attn_got=0, block_out=0, grad_input=0, small=0
    )
)
tail_scratch = list(
    dict(
        backs=0, ups=0, stage=0, came1=0, give2=0, mine=0, twins=0, arrived=0, passed=0, outbox=0,
        sums=0, bias=0, turned=0, kv_grad=0, heads=0, pre=0, own_w=0, twin_w=0, twin_came=0,
        w_came=0, w_give=0, quarters=0, small_came=0
    )
)
tail_sems = list(
    dict(
        late_sem=0, part_sem=0, stage_sem=0, z1_s=0, z1_r=0, z2_s=0, z2_r=0, p_s=0, p_r=0, g_s=0,
        g_r=0, o_s=0, o_r=0, h_s=0, h_r=0, w_s=0, w_r=0, s_s=0, s_r=0
    )
)


def tail_kernel(size, scale, *refs):
    names = tail_near + tail_late + tail_first + tail_last + tail_held + tail_out + ["l_" + n for n in tail_late]
    names = names + tail_scratch + tail_sems
    r = types.SimpleNamespace(**dict(zip(names, refs, strict=True)))
    d, e, t = lax.axis_index("dp"), lax.axis_index("ep"), lax.axis_index("tp")
    near, far, twin = {"tp": t ^ 1}, {"tp": t ^ 2}, {"ep": 1 - e}
    next_z, far_z = {"dp": d ^ 1}, {"dp": d ^ 2}
    rows, width = r.x_mid.shape
    half = rows // 2
    first, second = pl.ds(0, half), pl.ds(half, half)
    pairs = r.kept.shape[0]
    greet((near, far, twin, next_z, far_z))

    loads = {}
    for k, name in enumerate(tail_late):
        loads[name] = pltpu.make_async_copy(getattr(r, name), getattr(r, "l_" + name), r.late_sem.at[k])

    def late(name):
        if name in loads:
            loads.pop(name).wait()
        return getattr(r, "l_" + name)

    def link(name):
        send_sem, recv_sem = getattr(r, name + "_s"), getattr(r, name + "_r")

        def send(src, dst, k, device):
            copy = pltpu.make_async_remote_copy(
                src, dst, send_sem.at[k], recv_sem.at[k], device_id=device, device_id_type=MESH
            )
            copy.start()
            return copy

        return send

    unsent = []

    z1, z2 = link("z1"), link("z2")
    over1, over2, stages = {}, {}, {}

    units = r.kept.shape[1]
    pieces = [(n, pl.ds(0, units)) for n in range(pairs - 1)]
    pieces += [(pairs - 1, pl.ds(at, units // 2)) for at in (0, units // 2)]

    def start1(k):
        n, cut = pieces[k]
        over1[k] = [
            z1(
                (r.give_c.at[0] if n == 2 else r.give_rest.at[n - 3]).at[side, cut],
                r.came1.at[n - 2, side, cut],
                2 * (k - 2) + side,
                next_z,
            )
            for side in (1, 0)
        ]

    def prepare(k):
        n, cut = pieces[k]
        kept = (r.keep_a, r.keep_b, r.keep_c)[n].at[0] if n < 3 else r.keep_rest.at[n - 3]
        stages[k] = pltpu.make_async_copy(kept.at[:, cut], r.stage.at[:, cut], r.stage_sem)
        stages[k].start()

    def add1(k):
        n, cut = pieces[k]
        if n < 2:
            came = late(("got_a", "got_b")[n])
        else:
            for copy in over1[k]:
                copy.wait_recv()
            unsent.extend(over1[k])
            came = r.came1.at[n - 2]
        stages[k].wait()
        r.give2[n, cut] = (
            r.stage[1, cut].astype(f32) + came[1, cut].astype(f32)
        ).astype(bf16)
        over2[k] = z2(r.give2.at[n, cut], r.got.at[n, cut], k, far_z)
        r.kept[n, cut] = (r.stage[0, cut].astype(f32) + came[0, cut].astype(f32)).astype(bf16)
        if k + 1 < len(pieces):
            prepare(k + 1)

    def added(to, index, *others):
        total = to[index].astype(f32)
        for other in others:
            total += other.astype(f32)
        return total

    def scatter(send, bring, number, between):
        mine, arrived, passed = r.mine, r.arrived.at[number], r.passed.at[number]
        bring(3)
        a_on = send(mine.at[3, first], arrived.at[0, 0], 4, near)
        b_on = send(mine.at[3, second], arrived.at[1, 0], 5, far)
        bring(1)
        a_own = send(mine.at[1, first], arrived.at[0, 1], 6, near)
        bring(2)
        b_own = send(mine.at[2, second], arrived.at[1, 1], 7, far)
        bring(0)
        between()
        a_on.wait_recv()
        mine[2, first] = added(mine, (2, first), arrived[0, 0]).astype(bf16)
        a_last = send(mine.at[2, first], passed.at[0], 8, far)
        b_on.wait_recv()
        mine[1, second] = added(mine, (1, second), arrived[1, 0]).astype(bf16)
        b_last = send(mine.at[1, second], passed.at[1], 9, near)
        a_own.wait_recv()
        b_own.wait_recv()
        a_last.wait_recv()
        r.sums[first] = added(mine, (0, first), arrived[0, 1], passed[0])
        b_last.wait_recv()
        r.sums[second] = added(mine, (0, second), arrived[1, 1], passed[1])
        for copy in (a_on, b_on, a_own, b_own, a_last, b_last):
            copy.wait_send()

    def nothing():
        pass

    plane = rows * lax.axis_size("tp")

    def scatter_all(send, make, number, between):
        order = (3, 1, 2, 0)
        twins_sent = {}

        def compute(k):
            block = rows_at((1 - e) * plane + (t ^ k) * rows, rows)
            r.outbox[k] = make(block)
            twins_sent[k] = send(r.outbox.at[k], r.twins.at[number // 2, k], k, twin)
            r.mine[k] = make(rows_at(e * plane + (t ^ k) * rows, rows))

        def bring(k):
            at = order.index(k)
            if at + 1 < 4:
                compute(order[at + 1])
            twins_sent[k].wait_recv()
            r.mine[k] = added(r.mine, k, r.twins[number // 2, k]).astype(bf16)

        compute(order[0])
        scatter(send, bring, number, between)
        for copy in twins_sent.values():
            copy.wait_send()

    start1(2)
    backs, ups = r.backs, r.ups
    for copy in list(loads.values())[:2]:
        copy.start()
    prepare(0)
    firsts = [
        pltpu.make_async_copy(a, place, r.part_sem.at[k])
        for k, (a, place) in enumerate(((r.back, backs), (r.w_up, ups)))
    ]
    for copy in firsts + list(loads.values())[2:]:
        copy.start()
    add1(0)
    add1(1)
    for copy in firsts:
        copy.wait()

    def rows_back(block):
        return (
            dot(backs[:, block], ups[...], (0, 0))
            + dot(r.logits[:, block], r.router_rows[...], (0, 0))
        ).astype(bf16)

    scatter_all(link("p"), rows_back, 0, nothing)

    def norm_back_in(grad_normed, values, gain):
        factor = lax.rsqrt(jnp.mean(values * values, axis=-1, keepdims=True) + eps_norm)
        hat = values * factor
        grad_hat = grad_normed * gain
        inner = jnp.mean(grad_hat * hat, axis=-1, keepdims=True)
        return (
            factor * (grad_hat - hat * inner),
            jnp.sum(grad_normed * hat, axis=0, keepdims=True),
        )

    small, lanes = r.quarters, width // 4
    experts_all = r.router.shape[0] - 4

    def small_put(values, at):
        for k in range(4):
            small[k, at] = values[:, k * lanes : (k + 1) * lanes]

    small_put(r.router[...], slice(0, experts_all + 4))
    back, gain_grad = norm_back_in(r.sums[...], r.x_mid[...], r.gains[1:2])
    small_put(gain_grad, slice(experts_all, experts_all + 1))
    grad_mid = r.grad[...].astype(f32) + back
    r.grad_input[...] = grad_mid

    length = r.l_q.shape[0]
    whole = ups.at[:length]

    def place(tt, part, count):
        return ups.at[rows_at(tt * rows + part * half, count)]

    ups[rows_at(t * rows, rows), :] = grad_mid.astype(bf16)
    g = link("g")
    near_a = g(place(t, 0, half), place(t, 0, half), 0, near)
    far_b = g(place(t, 1, half), place(t, 1, half), 1, far)
    near_b = g(place(t, 1, half), place(t, 1, half), 2, near)
    far_a = g(place(t, 0, half), place(t, 0, half), 3, far)
    mixed = backs.at[: r.mixed.shape[0]]
    w_down = ups.at[length : length + r.w_down.shape[0]]
    lasts = [
        pltpu.make_async_copy(a, place_, r.part_sem.at[2 + k])
        for k, (a, place_) in enumerate(((r.mixed, mixed), (r.w_down, w_down)))
    ]
    for copy in lasts:
        copy.start()
    mask_into(r.bias, r.row)
    r.kv_grad[...] = jnp.zeros_like(r.kv_grad)
    near_a.wait_recv()
    on_a = g(place(t ^ 1, 0, half), place(t ^ 1, 0, half), 4, far)
    far_b.wait_recv()
    on_b = g(place(t ^ 2, 1, half), place(t ^ 2, 1, half), 5, near)
    for copy in (near_b, far_a, on_a, on_b):
        copy.wait_recv()
    unsent.extend((near_a, far_b, near_b, far_a, on_a, on_b))

    attention_back_steps(
        size,
        scale,
        whole,
        late("w_output"),
        late("q"),
        late("kv"),
        r.total,
        [r.cosine, r.sine, r.kcosine, r.ksine],
        r.pre, r.bias, r.turned, r.kv_grad, r.heads,
    )
    start1(3)
    q_width = r.l_q.shape[1]
    w_query, keyval = late("w_query"), late("keyval")

    def bring_heads(k):
        block = rows_at((t ^ k) * rows, rows)
        r.mine[k] = (
            dot(r.pre[block, :q_width], w_query[...], (1, 1))
            + dot(r.pre[block, q_width:], keyval[...], (1, 1))
        ).astype(bf16)

    w = link("w")
    twin_w = []

    def weights():
        attention_weights_kernel(
            late("rows"), r.pre, whole, late("attended"), r.own_w, r.twin_w
        )
        twin_w.append(w(r.twin_w, r.twin_came, 0, twin))
        add1(2)

    scatter(link("h"), bring_heads, 1, weights)
    back, gain_grad = norm_back_in(r.sums[...], r.x[...].astype(f32), r.gains[:1])
    small_put(gain_grad, slice(experts_all + 1, experts_all + 2))
    r.grad_input[...] = r.grad_input[...] + back

    twin_w[0].wait_recv()
    own_w = r.own_w
    w_copies = list(twin_w)
    for k in (1, 3):
        own_w[k] = added(own_w, k, r.twin_came[k]).astype(bf16)
        w_copies.append(w(own_w.at[k], r.w_came.at[k // 2], 1 + k // 2, next_z))
    for k in (0, 2):
        own_w[k] = added(own_w, k, r.twin_came[k]).astype(bf16)

    s = link("s")
    low, high = t % 2, t // 2 % 2
    two = [pl.ds((low ^ k) * 2, 2) for k in range(2)]
    one = [pl.ds(low * 2 + (high ^ k), 1) for k in range(2)]
    own, every = one[0], pl.ds(0, 4)
    small_plan = [
        (twin, every, every),
        (near, two[1], two[0]),
        (far, one[1], own),
        (next_z, own, own),
        (far_z, own, own),
        (far, own, one[1]),
        (near, two[0], two[1]),
    ]
    small_sent = {}

    def small_send(k):
        device, cut, _ = small_plan[k]
        small_sent[k] = s(small.at[cut], r.small_came.at[k, cut], k, device)

    def small_add(k):
        kept = small_plan[k][2]
        small_sent[k].wait()
        came = r.small_came[k, kept]
        small[kept] = small[kept] + came if k < 5 else came

    small_send(0)

    for copy in lasts:
        copy.wait()

    def mixed_rows(block):
        return dot(mixed[:, block], w_down[...], (0, 0)).astype(bf16)

    def third_sum():
        add1(3)
        start1(4)
        small_add(0)
        small_send(1)

    scatter_all(link("o"), mixed_rows, 2, third_sum)
    r.block_out[...] = (r.x_mid[...] + r.sums[...]).astype(bf16)

    small_add(1)
    small_send(2)
    small_add(2)
    small_send(3)
    for copy in w_copies[1:]:
        copy.wait_recv()
    r.w_give[...] = added(own_w, 2, r.w_came[1]).astype(bf16)
    w_copies.append(w(r.w_give, r.attn_got, 3, far_z))
    r.attn_kept[...] = added(own_w, 0, r.w_came[0]).astype(bf16)
    start1(5)
    small_add(3)
    small_send(4)
    add1(4)
    small_add(4)
    small_send(5)
    add1(5)
    small_add(5)
    small_send(6)
    small_add(6)
    for k in range(4):
        r.small[:, k * lanes : (k + 1) * lanes] = small[k]
    w_copies[-1].wait_recv()
    for k in range(len(pieces)):
        over2[k].wait()
    for copy in unsent + w_copies:
        copy.wait_send()


def tail(size, scale, named, collective_id):
    width = named.x_mid.shape[1]
    rows = named.x_mid.shape[0]
    length = named.q.shape[0]
    q_width, kv_width = named.q.shape[1], named.kv.shape[1]
    _, count, units, columns = named.keep_a.shape
    pairs = 3 + named.keep_rest.shape[0]
    block = (width // 8, 2 * q_width + kv_width)
    shape = jax.ShapeDtypeStruct
    outs = dict(
        kept=shape((pairs, units, columns), bf16),
        got=shape((pairs, units, columns), bf16),
        attn_kept=shape(block, bf16),
        attn_got=shape(block, bf16),
        block_out=shape((rows, width), bf16),
        grad_input=shape((rows, width), f32),
        small=shape(named.router.shape, f32),
    )
    scratch = dict(
        stage=((count, units, columns), bf16),
        came1=((pairs - 2, count, units, columns), bf16),
        give2=((pairs, units, columns), bf16),
        mine=((4, rows, width), bf16),
        twins=((2, 4, rows, width), bf16),
        arrived=((3, 2, 2, rows // 2, width), bf16),
        passed=((3, 2, rows // 2, width), bf16),
        outbox=((4, rows, width), bf16),
        sums=((rows, width), f32),
        backs=(named.back.shape, bf16),
        ups=(named.w_up.shape, bf16),
        bias=((length, length), f32),
        turned=((q_width, length), f32),
        kv_grad=((length, kv_width), f32),
        heads=((length, q_width), bf16),
        pre=((length, q_width + kv_width), bf16),
        own_w=((4, *block), bf16),
        twin_w=((4, *block), bf16),
        twin_came=((4, *block), bf16),
        w_came=((2, *block), bf16),
        w_give=(block, bf16),
        quarters=((4, named.router.shape[0], width // 4), f32),
        small_came=((7, 4, named.router.shape[0], width // 4), f32),
    )
    sems = dict(late_sem=len(tail_late), part_sem=4, z1=2 * (pairs - 1), z2=pairs + 1, p=10, g=6, o=10, h=10, w=4, s=7)
    dma = pltpu.SemaphoreType.DMA
    scratch_shapes = (
        [pltpu.VMEM(getattr(named, n).shape, getattr(named, n).dtype) for n in tail_late]
        + [pltpu.VMEM(*scratch[n]) for n in tail_scratch]
        + [dma((sems["late_sem"],)), dma((4,)), dma]
        + [dma((sems[n[:-2]],)) for n in tail_sems[3:]]
    )
    elsewhere, here = pl.BlockSpec(memory_space=pl.ANY), pl.BlockSpec(memory_space=pltpu.VMEM)
    ins = tail_near + tail_late + tail_first + tail_last + tail_held
    results = pl.pallas_call(
        functools.partial(tail_kernel, size, scale),
        out_shape=[outs[n] for n in tail_out],
        in_specs=[here] * len(tail_near) + [elsewhere] * (len(ins) - len(tail_near)),
        out_specs=[elsewhere if n in ("got", "attn_got") else here for n in tail_out],
        scratch_shapes=scratch_shapes,
        name="tail",
        cost_estimate=pl.CostEstimate(flops=10**9, bytes_accessed=10**6, transcendentals=0),
        compiler_params=pltpu.CompilerParams(
            collective_id=collective_id, has_side_effects=True, vmem_limit_bytes=60 * 2**20
        ),
    )(*(getattr(named, n) for n in ins))
    return types.SimpleNamespace(**dict(zip(tail_out, results)))


def place_pairs(kept, got, shapes):
    (_, _, hidden, columns), _ = shapes
    pairs, units, _ = kept.shape
    pair = units // (3 * hidden)
    ins = 2 * pair * hidden

    def body(kept_ref, got_ref, into_ref, out_ref):
        total = kept_ref[0].astype(f32) + got_ref[0].astype(f32)
        into_ref[...] = total[:ins].reshape(pair, 2, hidden, columns)
        out_ref[...] = total[ins:].reshape(pair, hidden, columns)

    block = pl.BlockSpec((1, units, columns), lambda i: (i, 0, 0))
    return pl.pallas_call(
        body,
        grid=(pairs,),
        out_shape=[jax.ShapeDtypeStruct(s, f32) for s in shapes],
        in_specs=[block, block],
        out_specs=[
            pl.BlockSpec((pair, 2, hidden, columns), lambda i: (i, 0, 0, 0)),
            pl.BlockSpec((pair, hidden, columns), lambda i: (i, 0, 0)),
        ],
        name="place_pairs",
        compiler_params=pltpu.CompilerParams(vmem_limit_bytes=24 * 2**20),
    )(kept, got)


def per_device(
    activations,
    segments,
    routes,
    attn_gain,
    w_query,
    key_value_weight,
    w_output,
    moe_gain,
    w_router,
    w_in,
    w_out,
    out_cotangent,
):
    row_count, width = activations.shape
    tp_count = lax.axis_size("tp")
    ep_count = lax.axis_size("ep")
    dp_count = lax.axis_size("dp")
    e_index = lax.axis_index("ep")
    seq_len = row_count * tp_count
    head_size = key_value_weight.shape[2] // 2
    kv_heads = key_value_weight.shape[1]
    q_heads = w_query.shape[1] // head_size
    heads_per_group = q_heads // kv_heads
    top_count = routes.shape[1]
    expert_count = w_router.shape[1]
    local_experts = w_in.shape[0]
    hidden = w_in.shape[2]
    score_scale = 1.0 / math.sqrt(head_size)

    lanes = jnp.arange(128, dtype=jnp.int32)
    used = jnp.any(routes[:, :, None] == lanes[None, None, :], axis=1).astype(bf16)
    plane_grad = lax.all_gather(
        jnp.concatenate([out_cotangent, used], axis=1), ("ep", "tp"), axis=0, tiled=True
    )

    tables = rope_tables(seq_len, head_size)
    keyval_flat = key_value_weight.reshape(width, kv_heads * 2 * head_size)
    doc_row = segments.astype(f32)
    q_width, kv_width = q_heads * head_size, 2 * kv_heads * head_size
    gains = jnp.concatenate([attn_gain[None], moe_gain[None], jnp.zeros((6, width), f32)])
    full_rows, query_rows, keyval_rows, attended, log_total, x_mid, rows_two = front(
        head_size,
        score_scale,
        activations,
        gains,
        w_query,
        keyval_flat,
        w_output,
        doc_row,
        tables,
        0,
    )

    pair = 2 if local_experts % 2 == 0 else 1
    pairs = local_experts // pair
    columns = width // dp_count
    in_order = dp_count == 4 and ep_count == 2 and tp_count == 4 and columns % 128 == 0 and pairs == 5
    blocks = dp_count if in_order else 1
    gates = jnp.pad(w_router, ((0, 0), (0, 128 - expert_count)))
    keeps, gives, came, earlier = [], [], [], ()
    calls = ((0, 1), (1, 1), (2, 1), (3, pairs - 3)) if in_order else ((0, 1), (1, pairs - 1))
    for start, count in calls:
        after = (came[0],) if start == 3 else ()
        results = experts(
            start, count, blocks, rows_two, plane_grad, gates, w_in, w_out, earlier, after
        )
        if start == 0:
            gates, *results = results
        if start + count == pairs:
            logits, grad_w_router, *results = results
        terms, back, mixed, keep, *give = results
        earlier = (back, mixed, terms)
        keeps.append(keep)
        gives += give
        if in_order and start < 2:
            came.append(exchanged(give[0][0], 1))

    gate_rows = gates.shape[0]
    router_rows = jnp.pad(w_router.T, ((0, gate_rows - expert_count), (0, 0)))
    router_rows = jnp.concatenate([router_rows] * 2)
    all_width = 2 * q_width + kv_width
    shapes = [(local_experts, 2, hidden, columns), (local_experts, hidden, columns)]
    if in_order:
        done = tail(
            head_size,
            score_scale,
            types.SimpleNamespace(
                back=back,
                w_up=w_in.reshape(-1, width),
                logits=logits,
                router_rows=router_rows,
                keep_a=keeps[0],
                keep_b=keeps[1],
                keep_c=keeps[2],
                give_c=gives[2],
                keep_rest=keeps[3],
                give_rest=gives[3],
                got_a=came[0],
                got_b=came[1],
                x_mid=x_mid,
                grad=out_cotangent,
                x=activations,
                gains=gains,
                router=grad_w_router,
                total=log_total,
                row=doc_row,
                cosine=tables[0],
                sine=tables[1],
                kcosine=tables[2],
                ksine=tables[3],
                w_output=w_output,
                q=query_rows,
                kv=keyval_rows,
                w_query=w_query,
                keyval=keyval_flat,
                rows=full_rows,
                attended=attended,
                mixed=mixed,
                w_down=w_out.reshape(-1, width),
            ),
            3,
        )
        block_out, grad_input, small = done.block_out, done.grad_input, done.small
        grad_w_in, grad_w_out = place_pairs(done.kept, done.got, shapes)
        attn_sum = done.attn_kept.astype(f32) + done.attn_got.astype(f32)
    else:
        grad_rows_two = dot(back, w_in.reshape(-1, width), (0, 0)) + dot(logits, router_rows, (0, 0))
        grad_normed_two = scatter_sum(grad_rows_two.astype(bf16), True, 3)
        hat_two, factor_two = normalize(x_mid)
        grad_from_moe, grad_moe_gain = norm_back(grad_normed_two, hat_two, factor_two, moe_gain)
        grad_mid = out_cotangent.astype(f32) + grad_from_moe
        grad_full = gather(grad_mid.astype(bf16), False, 4)

        heads_part, grad_pre = local_call(
            functools.partial(attention_back_kernel, head_size, score_scale),
            "attention_back",
            [
                jax.ShapeDtypeStruct((seq_len, width), bf16),
                jax.ShapeDtypeStruct((seq_len, q_width + kv_width), bf16),
            ],
            [
                pltpu.VMEM((seq_len, seq_len), f32),
                pltpu.VMEM((q_width, seq_len), f32),
                pltpu.VMEM((seq_len, kv_width), f32),
                pltpu.VMEM((seq_len, q_width), bf16),
            ],
            (
                grad_full,
                w_output,
                query_rows,
                keyval_rows,
                log_total,
                w_query,
                keyval_flat,
                        doc_row,
                *tables,
            ),
        )
        attn_weights = local_call(
            attention_weights_kernel,
            "attention_weights",
            [jax.ShapeDtypeStruct((width, all_width), bf16)],
            [],
            (full_rows, grad_pre, grad_full, attended),
        )
        grad_normed_one = scatter_sum(heads_part, False, 6)
        hat_one, factor_one = normalize(activations.astype(f32))
        grad_from_attn, grad_attn_gain = norm_back(grad_normed_one, hat_one, factor_one, attn_gain)
        grad_input = grad_mid + grad_from_attn

        expert_part = dot(mixed, w_out.reshape(-1, width), (0, 0)).astype(bf16)
        block_out = (x_mid + scatter_sum(expert_part, True, 5)).astype(bf16)

        halves = attn_weights[0].reshape(dp_count, ep_count, -1, all_width)
        kept = lax.dynamic_index_in_dim(halves, e_index, 1, keepdims=False)
        given = lax.dynamic_index_in_dim(halves, 1 - e_index, 1, keepdims=False)
        got = lax.ppermute(given, "ep", [(0, 1), (1, 0)])
        attn_sum = halved_over_dp((kept.astype(f32) + got.astype(f32)).astype(bf16))
        summed = []
        for keep in keeps:
            for k in range(keep.shape[0]):
                parts = jnp.moveaxis(keep[k].reshape(-1, dp_count, columns), 1, 0)
                summed.append(halved_over_dp(parts))
        summed = jnp.stack(summed)
        ins = pair * 2 * hidden
        grad_w_in = summed[:, :ins].reshape(shapes[0])
        grad_w_out = summed[:, ins:].reshape(shapes[1])
        small = summed_everywhere(
            jnp.concatenate(
                [grad_w_router[:expert_count], grad_moe_gain[None], grad_attn_gain[None]]
            )
        )
    grad_w_query = attn_sum[:, :q_width]
    grad_w_keyval = attn_sum[:, q_width : q_width + kv_width].reshape(-1, kv_heads, 2 * head_size)
    grad_w_output = attn_sum[:, q_width + kv_width :].T
    grad_w_router = small[:expert_count].T
    grad_moe_gain, grad_attn_gain = small[expert_count], small[expert_count + 1]
    return (
        block_out,
        grad_input,
        grad_attn_gain,
        grad_w_query,
        grad_w_keyval,
        grad_w_output,
        grad_moe_gain,
        grad_w_router,
        grad_w_in,
        grad_w_out,
    )


def solution(mesh):
    return jax.shard_map(
        per_device,
        mesh=mesh,
        in_specs=(
            P(("dp", "ep", "tp"), None),
            P(("dp", "ep"), None),
            P(("dp", "ep", "tp"), None),
            P(),
            P(None, "tp"),
            P(None, "tp", None),
            P("tp", None),
            P(),
            P(),
            P("ep", None, "tp", None),
            P("ep", "tp", None),
            P(("dp", "ep", "tp"), None),
        ),
        out_specs=(
            P(("dp", "ep", "tp"), None),
            P(("dp", "ep", "tp"), None),
            P(),
            P(("dp", "ep"), "tp"),
            P(("dp", "ep"), "tp", None),
            P("tp", ("dp", "ep")),
            P(),
            P(),
            P("ep", None, "tp", "dp"),
            P("ep", "tp", "dp"),
        ),
        check_vma=False,
    )
```

```python
import functools
import math
import types

import jax
import jax.numpy as jnp
from jax import lax
from jax.experimental import pallas as pl
from jax.experimental.pallas import tpu as pltpu
from jax.sharding import PartitionSpec as P

eps_norm = 1e-05
rope_base = 10000.0
neg_fill = -1000000000.0
MESH = pl.DeviceIdType.MESH
bf16 = jnp.bfloat16
f32 = jnp.float32


def greet(partners):
    barrier = pltpu.get_barrier_semaphore()
    for partner in partners:
        pl.semaphore_signal(barrier, inc=1, device_id=partner, device_id_type=MESH)
    pl.semaphore_wait(barrier, len(partners))


def rows_at(start, count):
    return pl.ds(pl.multiple_of(start, count), count)


def gather_kernel(with_ep, block_ref, *refs):
    whole_ref, local_sem, send_sem, recv_sem = refs[-4:]
    rows = block_ref.shape[0]
    half = rows // 2
    t, e = lax.axis_index("tp"), lax.axis_index("ep")
    near, far = {"tp": t ^ 1}, {"tp": t ^ 2}
    twin = {"ep": 1 - e}
    greet((near, far, twin) if with_ep else (near, far))
    tp = lax.axis_size("tp")
    base = e * (tp * rows) if with_ep else 0

    def place(tt, part, count):
        return whole_ref.at[rows_at(base + tt * rows + part * half, count)]

    def send(src, dst, k, device):
        copy = pltpu.make_async_remote_copy(
            src, dst, send_sem.at[k], recv_sem.at[k], device_id=device, device_id_type=MESH
        )
        copy.start()
        return copy

    def own(part):
        return block_ref.at[pl.ds(part * half, half)]

    local = pltpu.make_async_copy(block_ref, place(t, 0, rows), local_sem)
    near_a = send(own(0), place(t, 0, half), 0, near)
    far_b = send(own(1), place(t, 1, half), 1, far)
    near_b = send(own(1), place(t, 1, half), 2, near)
    far_a = send(own(0), place(t, 0, half), 3, far)
    local.start()
    copies = [near_a, far_b, near_b, far_a]
    if with_ep:
        twin_own = send(block_ref, place(t, 0, rows), 6, twin)
        copies.append(twin_own)
    near_a.wait_recv()
    on_a = send(place(t ^ 1, 0, half), place(t ^ 1, 0, half), 4, far)
    far_b.wait_recv()
    on_b = send(place(t ^ 2, 1, half), place(t ^ 2, 1, half), 5, near)
    near_b.wait_recv()
    far_a.wait_recv()
    if with_ep:
        twin_near = send(place(t ^ 1, 0, rows), place(t ^ 1, 0, rows), 7, twin)
        twin_far = send(place(t ^ 2, 0, rows), place(t ^ 2, 0, rows), 8, twin)
    on_a.wait_recv()
    on_b.wait_recv()
    if with_ep:
        twin_diag = send(place(t ^ 3, 0, rows), place(t ^ 3, 0, rows), 9, twin)
        for copy in (twin_own, twin_near, twin_far, twin_diag):
            copy.wait_recv()
        copies += [twin_near, twin_far, twin_diag]
    local.wait()
    for copy in copies + [on_a, on_b]:
        copy.wait_send()


def gather(block, with_ep, collective_id, after=()):
    rows, width = block.shape
    count = lax.axis_size("tp") * (lax.axis_size("ep") if with_ep else 1)
    return pl.pallas_call(
        functools.partial(gather_kernel, with_ep),
        out_shape=jax.ShapeDtypeStruct((count * rows, width), block.dtype),
        in_specs=[pl.BlockSpec(memory_space=pl.ANY)] * (1 + len(after)),
        out_specs=pl.BlockSpec(memory_space=pl.ANY),
        scratch_shapes=[
            pltpu.SemaphoreType.DMA,
            pltpu.SemaphoreType.DMA((10,)),
            pltpu.SemaphoreType.DMA((10,)),
        ],
        name="gather_plane" if with_ep else "gather_tp",
        cost_estimate=pl.CostEstimate(flops=0, bytes_accessed=10**6, transcendentals=0),
        compiler_params=pltpu.CompilerParams(
            collective_id=collective_id, has_side_effects=True, vmem_limit_bytes=16 * 2**20
        ),
    )(block, *after)


def scatter_kernel(with_ep, part_ref, *refs):
    sum_ref, mine, twins, arrived, passed, local_sem, send_sem, recv_sem = refs[-8:]
    rows = sum_ref.shape[0]
    half = rows // 2
    t, e = lax.axis_index("tp"), lax.axis_index("ep")
    tp = lax.axis_size("tp")
    near, far = {"tp": t ^ 1}, {"tp": t ^ 2}
    twin = {"ep": 1 - e}
    greet((near, far, twin) if with_ep else (near, far))
    base = e * (tp * rows) if with_ep else 0
    other = (1 - e) * (tp * rows)

    def send(src, dst, k, device):
        copy = pltpu.make_async_remote_copy(
            src, dst, send_sem.at[k], recv_sem.at[k], device_id=device, device_id_type=MESH
        )
        copy.start()
        return copy

    order = (3, 1, 2, 0)
    locals_, twin_copies = {}, {}
    for k in order:
        if with_ep:
            twin_copies[k] = send(
                part_ref.at[rows_at(other + (t ^ k) * rows, rows)], twins.at[k], k, twin
            )
        locals_[k] = pltpu.make_async_copy(
            part_ref.at[rows_at(base + (t ^ k) * rows, rows)], mine.at[k], local_sem.at[k]
        )
        locals_[k].start()

    def ready(k):
        locals_[k].wait()
        if with_ep:
            twin_copies[k].wait_recv()
            mine[k] = (mine[k].astype(f32) + twins[k].astype(f32)).astype(mine.dtype)

    first, second = pl.ds(0, half), pl.ds(half, half)
    ready(3)
    a_on = send(mine.at[3, first], arrived.at[0, 0], 4, near)
    b_on = send(mine.at[3, second], arrived.at[1, 0], 5, far)
    ready(1)
    a_own = send(mine.at[1, first], arrived.at[0, 1], 6, near)
    ready(2)
    b_own = send(mine.at[2, second], arrived.at[1, 1], 7, far)
    ready(0)
    a_on.wait_recv()
    mine[2, first] = (mine[2, first].astype(f32) + arrived[0, 0].astype(f32)).astype(mine.dtype)
    a_last = send(mine.at[2, first], passed.at[0], 8, far)
    b_on.wait_recv()
    mine[1, second] = (mine[1, second].astype(f32) + arrived[1, 0].astype(f32)).astype(mine.dtype)
    b_last = send(mine.at[1, second], passed.at[1], 9, near)
    a_own.wait_recv()
    b_own.wait_recv()
    a_last.wait_recv()
    sum_ref[first] = (
        mine[0, first].astype(f32) + arrived[0, 1].astype(f32) + passed[0].astype(f32)
    ).astype(sum_ref.dtype)
    b_last.wait_recv()
    sum_ref[second] = (
        mine[0, second].astype(f32) + arrived[1, 1].astype(f32) + passed[1].astype(f32)
    ).astype(sum_ref.dtype)
    copies = [a_on, b_on, a_own, b_own, a_last, b_last]
    if with_ep:
        copies += list(twin_copies.values())
    for copy in copies:
        copy.wait_send()


def scatter_sum(parts, with_ep, collective_id, after=()):
    count = lax.axis_size("tp") * (lax.axis_size("ep") if with_ep else 1)
    rows, width = parts.shape[0] // count, parts.shape[1]
    return pl.pallas_call(
        functools.partial(scatter_kernel, with_ep),
        out_shape=jax.ShapeDtypeStruct((rows, width), f32),
        in_specs=[pl.BlockSpec(memory_space=pl.ANY)] * (1 + len(after)),
        out_specs=pl.BlockSpec(memory_space=pltpu.VMEM),
        scratch_shapes=[
            pltpu.VMEM((4, rows, width), bf16),
            pltpu.VMEM((4, rows, width) if with_ep else (4, 16, 128), bf16),
            pltpu.VMEM((2, 2, rows // 2, width), bf16),
            pltpu.VMEM((2, rows // 2, width), bf16),
            pltpu.SemaphoreType.DMA((4,)),
            pltpu.SemaphoreType.DMA((10,)),
            pltpu.SemaphoreType.DMA((10,)),
        ],
        name="scatter_plane" if with_ep else "scatter_tp",
        cost_estimate=pl.CostEstimate(flops=0, bytes_accessed=10**6, transcendentals=0),
        compiler_params=pltpu.CompilerParams(
            collective_id=collective_id, has_side_effects=True, vmem_limit_bytes=24 * 2**20
        ),
    )(parts, *after)


def halve(blocks, step):
    dp = lax.axis_size("dp")
    bit = (lax.axis_index("dp") // step) % 2
    pairs = blocks.reshape(-1, 2, *blocks.shape[1:])
    kept = lax.dynamic_index_in_dim(pairs, bit, 1, keepdims=False)
    given = lax.dynamic_index_in_dim(pairs, 1 - bit, 1, keepdims=False)
    got = lax.ppermute(given, "dp", [(i, i ^ step) for i in range(dp)])
    total = kept.astype(f32) + got.astype(f32)
    return total if 2 * step == dp else total.astype(bf16)


def halved_over_dp(blocks):
    dp = lax.axis_size("dp")
    if dp & (dp - 1):
        return lax.psum_scatter(blocks, "dp", scatter_dimension=0, tiled=False).astype(f32)
    step = 1
    while step < dp:
        blocks = halve(blocks, step)
        step *= 2
    return blocks[0].astype(f32)


def swapped(matrix, half):
    lane = lax.broadcasted_iota(jnp.int32, matrix.shape, 1)
    width = matrix.shape[1]
    return jnp.where(
        lane % (2 * half) < half,
        pltpu.roll(matrix, width - half, 1),
        pltpu.roll(matrix, half, 1),
    )


def rotated(matrix, tables, half, back):
    cosine, sine = tables
    times = matrix.shape[1] // cosine.shape[1]
    cosine, sine = (jnp.concatenate([t] * times, axis=1) for t in (cosine, sine))
    return matrix * cosine + swapped(matrix, half) * (-sine if back else sine)


def mask_into(bias_ref, row_ref):
    shape = bias_ref.shape
    key = lax.broadcasted_iota(jnp.int32, shape, 0)
    query = lax.broadcasted_iota(jnp.int32, shape, 1)
    column = jnp.broadcast_to(row_ref[:1], (128, shape[0])).T
    allowed = (column[:, :1] == row_ref[:1]) & (key <= query)
    bias_ref[...] = jnp.where(allowed, 0.0, neg_fill)


def head_cuts(head, kv_heads, q_heads, size):
    group = head // (q_heads // kv_heads)
    return (
        slice(head * size, (head + 1) * size),
        slice(2 * group * size, (2 * group + 1) * size),
        slice((2 * group + 1) * size, (2 * group + 2) * size),
    )


def attention_steps(
    size, scale, x_ref, gain_ref, query_ref, keyval_ref, tables, rows_ref, q_ref, kv_ref, total_ref, attended_ref,
    bias_ref, turned_ref,
):
    cos_ref, sin_ref, kcos_ref, ksin_ref = tables
    x = x_ref[...].astype(f32)
    factor = lax.rsqrt(jnp.mean(x * x, axis=-1, keepdims=True) + eps_norm)
    rows_ref[...] = (x * factor * gain_ref[:1]).astype(bf16)
    rows = rows_ref[...]
    q = jnp.dot(rows, query_ref[...], preferred_element_type=f32)
    q_ref[...] = rotated(q, (cos_ref[...], sin_ref[...]), size // 2, False).astype(bf16)
    kv = jnp.dot(rows, keyval_ref[...], preferred_element_type=f32)
    kv_ref[...] = rotated(kv, (kcos_ref[...], ksin_ref[...]), size // 2, False).astype(bf16)
    length = x.shape[0]
    tile = length // 2
    q_heads, kv_heads = q_ref.shape[1] // size, kv_ref.shape[1] // (2 * size)
    total_ref[...] = jnp.zeros_like(total_ref)
    for block in range(2):
        now, past = slice(block * tile, (block + 1) * tile), slice(0, (block + 1) * tile)
        for head in range(q_heads):
            at, key_at, value_at = head_cuts(head, kv_heads, q_heads, size)
            scores = dot(kv_ref[past, key_at], q_ref[now, at], (1, 1)) * scale + bias_ref[past, now]
            peak = jnp.max(scores, axis=0, keepdims=True)
            weight = jnp.exp(scores - peak)
            total = jnp.sum(weight, axis=0, keepdims=True)
            probs = (weight * (1.0 / total)).astype(bf16)
            total_ref[head : head + 1, now] = peak + jnp.log(total)
            turned_ref[at, now] = dot(kv_ref[past, value_at], probs, (0, 0))
    attended_ref[...] = turned_ref[...].T.astype(bf16)


def front_kernel(
    size, scale, x_ref, gain_ref, query_ref, keyval_ref, out_ref, row_ref, cos_ref, sin_ref,
    kcos_ref, ksin_ref, rows_out, q_out, kv_out, attended_out, total_ref, mid_ref, plane_ref, rows_ref, q_ref,
    kv_ref, attended_ref, x_whole, bias_ref, turned_ref, mine, arrived, passed, out_sem, x_s, x_r, h_s, h_r, p_s,
    p_r,
):
    t, e = lax.axis_index("tp"), lax.axis_index("ep")
    near, far, twin = {"tp": t ^ 1}, {"tp": t ^ 2}, {"ep": 1 - e}
    rows = x_ref.shape[0]
    half = rows // 2
    first, second = pl.ds(0, half), pl.ds(half, half)
    greet((near, far, twin))

    def link(send_sem, recv_sem):
        def send(src, dst, k, device):
            copy = pltpu.make_async_remote_copy(
                src, dst, send_sem.at[k], recv_sem.at[k], device_id=device, device_id_type=MESH
            )
            copy.start()
            return copy

        return send

    unsent = []

    def spread(send, whole, base, between, with_twin):
        def place(tt, part, count):
            return whole.at[rows_at(base + tt * rows + part * half, count)]

        def on(tt, part, count, k, device):
            copy = send(place(tt, part, count), place(tt, part, count), k, device)
            unsent.append(copy)
            return copy

        near_a, far_b = on(t, 0, half, 0, near), on(t, 1, half, 1, far)
        near_b, far_a = on(t, 1, half, 2, near), on(t, 0, half, 3, far)
        twins = [on(t, 0, rows, 6, twin)] if with_twin else []
        between()
        near_a.wait_recv()
        on_a = on(t ^ 1, 0, half, 4, far)
        far_b.wait_recv()
        on_b = on(t ^ 2, 1, half, 5, near)
        near_b.wait_recv()
        far_a.wait_recv()
        if with_twin:
            twins += [on(t ^ k, 0, rows, 6 + k, twin) for k in (1, 2)]
        on_a.wait_recv()
        on_b.wait_recv()
        if with_twin:
            twins.append(on(t ^ 3, 0, rows, 9, twin))
        for copy in twins:
            copy.wait_recv()

    x_whole[rows_at(t * rows, rows)] = x_ref[...]
    spread(link(x_s, x_r), x_whole, 0, lambda: mask_into(bias_ref, row_ref), False)
    attention_steps(
        size, scale, x_whole, gain_ref, query_ref, keyval_ref, (cos_ref, sin_ref, kcos_ref, ksin_ref),
        rows_ref, q_ref, kv_ref, total_ref, attended_ref, bias_ref, turned_ref,
    )
    late = ((rows_ref, rows_out), (q_ref, q_out), (kv_ref, kv_out), (attended_ref, attended_out))
    leaving = [pltpu.make_async_copy(a, b, out_sem.at[k]) for k, (a, b) in enumerate(late)]
    send = link(h_s, h_r)

    def bring(k):
        block = attended_ref[rows_at((t ^ k) * rows, rows)]
        mine[k] = jnp.dot(block, out_ref[...], preferred_element_type=f32).astype(bf16)

    def added(k, cut, *others):
        total = mine[k, cut].astype(f32)
        for other in others:
            total += other.astype(f32)
        return total

    bring(3)
    a_on = send(mine.at[3, first], arrived.at[0, 0], 0, near)
    b_on = send(mine.at[3, second], arrived.at[1, 0], 1, far)
    bring(1)
    a_own = send(mine.at[1, first], arrived.at[0, 1], 2, near)
    bring(2)
    b_own = send(mine.at[2, second], arrived.at[1, 1], 3, far)
    bring(0)
    for copy in leaving:
        copy.start()
    a_on.wait_recv()
    mine[2, first] = added(2, first, arrived[0, 0]).astype(bf16)
    a_last = send(mine.at[2, first], passed.at[0], 4, far)
    b_on.wait_recv()
    mine[1, second] = added(1, second, arrived[1, 0]).astype(bf16)
    b_last = send(mine.at[1, second], passed.at[1], 5, near)
    a_own.wait_recv()
    b_own.wait_recv()
    a_last.wait_recv()
    mid_ref[first] = x_ref[first].astype(f32) + added(0, first, arrived[0, 1], passed[0])
    b_last.wait_recv()
    mid_ref[second] = x_ref[second].astype(f32) + added(0, second, arrived[1, 1], passed[1])
    unsent.extend((a_on, b_on, a_own, b_own, a_last, b_last))
    x_mid = mid_ref[...]
    factor = lax.rsqrt(jnp.mean(x_mid * x_mid, axis=-1, keepdims=True) + eps_norm)
    base = e * (lax.axis_size("tp") * rows)
    plane_ref[rows_at(base + t * rows, rows)] = (x_mid * factor * gain_ref[1:2]).astype(bf16)
    spread(link(p_s, p_r), plane_ref, base, lambda: None, True)
    for copy in leaving:
        copy.wait()
    for copy in unsent:
        copy.wait_send()


def front(size, scale, x, gains, w_query, keyval, w_output, row, tables, collective_id):
    rows, width = x.shape
    length = row.shape[1]
    q_width, kv_width = w_query.shape[1], keyval.shape[1]
    shape, dma = jax.ShapeDtypeStruct, pltpu.SemaphoreType.DMA
    spec = pl.BlockSpec(memory_space=pltpu.VMEM)
    late = [
        shape((length, width), bf16),
        shape((length, q_width), bf16),
        shape((length, kv_width), bf16),
        shape((length, q_width), bf16),
    ]
    outs = late + [
        shape((-(-q_width // (8 * size)) * 8, length), f32),
        shape((rows, width), f32),
        shape((2 * length, width), bf16),
    ]
    return pl.pallas_call(
        functools.partial(front_kernel, size, scale),
        out_shape=outs,
        in_specs=[spec] * 10,
        out_specs=[pl.BlockSpec(memory_space=pl.ANY)] * 4 + [spec] * 3,
        scratch_shapes=[
            *(pltpu.VMEM(part.shape, part.dtype) for part in late),
            pltpu.VMEM((length, width), bf16),
            pltpu.VMEM((length, length), f32),
            pltpu.VMEM((q_width, length), f32),
            pltpu.VMEM((4, rows, width), bf16),
            pltpu.VMEM((2, 2, rows // 2, width), bf16),
            pltpu.VMEM((2, rows // 2, width), bf16),
            dma((4,)),
            *([dma((6,))] * 4),
            *([dma((10,))] * 2),
        ],
        name="front",
        cost_estimate=pl.CostEstimate(flops=10**9, bytes_accessed=10**6, transcendentals=0),
        compiler_params=pltpu.CompilerParams(
            collective_id=collective_id, has_side_effects=True, vmem_limit_bytes=58 * 2**20
        ),
    )(x, gains, w_query, keyval, w_output, row, *tables)


def attention_back_steps(
    size, scale, grad_ref, out_ref, q_ref, kv_ref, total_ref, tables, pre_ref, bias_ref, turned_ref,
    kv_grad_ref, heads_ref,
):
    heads_ref[...] = dot(grad_ref[...], out_ref[...], (1, 1)).astype(bf16)
    length = q_ref.shape[0]
    tile = length // 2
    q_heads, kv_heads = q_ref.shape[1] // size, kv_ref.shape[1] // (2 * size)
    for block in range(2):
        now, past = slice(block * tile, (block + 1) * tile), slice(0, (block + 1) * tile)
        for head in range(q_heads):
            at, key_at, value_at = head_cuts(head, kv_heads, q_heads, size)
            keys, query, grad = kv_ref[past, key_at], q_ref[now, at], heads_ref[now, at]
            scores = dot(keys, query, (1, 1)) * scale + bias_ref[past, now]
            probs = jnp.exp(scores - total_ref[head : head + 1, now])
            grad_probs = dot(kv_ref[past, value_at], grad, (1, 1))
            inner = jnp.sum(probs * grad_probs, axis=0, keepdims=True)
            grad_scores = (probs * (grad_probs - inner)).astype(bf16)
            turned_ref[at, now] = dot(keys, grad_scores, (0, 0)) * scale
            kv_grad_ref[past, key_at] += dot(grad_scores, query, (1, 0)) * scale
            kv_grad_ref[past, value_at] += dot(probs.astype(bf16), grad, (1, 0))
    width = q_ref.shape[1]
    cos_ref, sin_ref, kcos_ref, ksin_ref = tables
    pre_ref[:, :width] = rotated(
        turned_ref[...].T, (cos_ref[...], sin_ref[...]), size // 2, True
    ).astype(bf16)
    pre_ref[:, width:] = rotated(
        kv_grad_ref[...], (kcos_ref[...], ksin_ref[...]), size // 2, True
    ).astype(bf16)


def attention_back_kernel(
    size, scale, grad_ref, out_ref, q_ref, kv_ref, total_ref, query_ref, keyval_ref, row_ref,
    cos_ref, sin_ref, kcos_ref, ksin_ref, *refs,
):
    part_ref, pre_ref, bias_ref, turned_ref, kv_grad_ref, heads_ref = refs[-6:]
    mask_into(bias_ref, row_ref)
    kv_grad_ref[...] = jnp.zeros_like(kv_grad_ref)
    attention_back_steps(
        size, scale, grad_ref, out_ref, q_ref, kv_ref, total_ref, (cos_ref, sin_ref, kcos_ref, ksin_ref),
        pre_ref, bias_ref, turned_ref, kv_grad_ref, heads_ref,
    )
    width = q_ref.shape[1]
    part_ref[...] = (
        dot(pre_ref[:, :width], query_ref[...], (1, 1))
        + dot(pre_ref[:, width:], keyval_ref[...], (1, 1))
    ).astype(bf16)


def local_call(body, name, out_shape, scratch, args, after=(), limit=48):
    spec = pl.BlockSpec(memory_space=pltpu.VMEM)
    return pl.pallas_call(
        body,
        out_shape=out_shape,
        in_specs=[spec] * len(args) + [pl.BlockSpec(memory_space=pl.ANY)] * len(after),
        out_specs=jax.tree.map(lambda _: spec, out_shape),
        scratch_shapes=scratch,
        name=name,
        cost_estimate=pl.CostEstimate(flops=10**6, bytes_accessed=10**6, transcendentals=0),
        compiler_params=pltpu.CompilerParams(vmem_limit_bytes=limit * 2**20),
    )(*args, *after)


def attention_weights_kernel(rows_ref, pre_ref, grad_ref, attended_ref, *outs):
    width, pre = rows_ref.shape[1], pre_ref.shape[1]
    parts = outs[0].shape[0] if len(outs) == 2 else 4
    d, e = lax.axis_index("dp"), lax.axis_index("ep")
    step = width // parts
    for c in range(parts):
        cut = slice(c * step, (c + 1) * step)
        first = dot(rows_ref[:, cut], pre_ref[...], (0, 0)).astype(bf16)
        second = dot(grad_ref[:, cut], attended_ref[...], (0, 0)).astype(bf16)
        if len(outs) == 1:
            outs[0][cut, :pre] = first
            outs[0][cut, pre:] = second
            continue
        for half in range(2):
            some = slice(half * (step // 2), (half + 1) * (step // 2))
            for mine in range(2):

                @pl.when((half == e) == (mine == 1))
                def _():
                    out_ref = outs[0] if mine else outs[1]
                    out_ref[d ^ c, :, :pre] = first[some]
                    out_ref[d ^ c, :, pre:] = second[some]


def exchanged(blocks, step):
    return lax.ppermute(blocks, "dp", [(i, i ^ step) for i in range(lax.axis_size("dp"))])


def summed_everywhere(value):
    for axis in ("ep", "tp", "dp"):
        size, step = lax.axis_size(axis), 1
        if size & (size - 1):
            value = lax.psum(value, axis)
            continue
        while step < size:
            value = value + lax.ppermute(value, axis, [(i, i ^ step) for i in range(size)])
            step *= 2
    return value


def dot(a, b, dims):
    return lax.dot_general(a, b, ((dims[:1], dims[1:]), ((), ())), preferred_element_type=f32)


def experts_kernel(first, local_experts, is_last, held, *refs):
    if first == 0:
        rows_ref, grad_ref, router_ref, in_ref, out_ref = refs[:5]
        gates_ref, terms_ref, back_ref, mixed_ref, keep_ref, *give_refs = refs[5:]
    else:
        rows_ref, grad_ref, gates_ref, in_ref, out_ref = refs[:5]
        terms_in = refs[7]
        outs = refs[8 + held :]
        if is_last:
            logits_ref, router_grad_ref, *outs = outs
        terms_ref, back_ref, mixed_ref, keep_ref, *give_refs = outs
    tokens, width = rows_ref.shape
    pair, _, hidden, _ = in_ref.shape
    tile = 256 if tokens % 256 == 0 else tokens
    number = pl.program_id(0) + first

    if first == 0:
        logits = jnp.dot(rows_ref[...], router_ref[...], preferred_element_type=f32)
        used = grad_ref[:, width:].astype(f32) > 0.5
        peak = jnp.max(jnp.where(used, logits, -jnp.inf), axis=-1, keepdims=True)
        weight = jnp.where(used, jnp.exp(jnp.where(used, logits - peak, 0.0)), 0.0)
        gates = weight / jnp.sum(weight, axis=-1, keepdims=True)
        gates_ref[...] = gates.T[: gates_ref.shape[0]]
    if first == 0:
        terms_ref[...] = jnp.zeros_like(terms_ref)
    else:

        @pl.when(pl.program_id(0) == 0)
        def _():
            terms_ref[...] = terms_in[...]

    into = in_ref[...].reshape(pair * 2 * hidden, width)
    out_of = out_ref[...].reshape(pair * hidden, width)
    base = lax.axis_index("ep") * local_experts + number * pair

    @pl.loop(0, tokens // tile)
    def _(j):
        now = pl.ds(pl.multiple_of(j * tile, tile), tile)
        gate_up = dot(into, rows_ref[now, :], (1, 1))
        down = dot(out_of, grad_ref[now, :width], (1, 1))
        for k in range(pair):
            gate = gate_up[2 * k * hidden : (2 * k + 1) * hidden]
            up = gate_up[(2 * k + 1) * hidden : (2 * k + 2) * hidden]
            back = down[k * hidden : (k + 1) * hidden]
            g = gates_ref[pl.ds(base + k, 1), now]
            sig = 1.0 / (1.0 + jnp.exp(-gate))
            silu = gate * sig
            active = silu * up
            terms_ref[pl.ds(base + k, 1), now] = jnp.sum(active * back, axis=0, keepdims=True)
            mixed_ref[k * hidden : (k + 1) * hidden, now] = (g * active).astype(bf16)
            grad_active = g * back
            back_ref[2 * k * hidden : (2 * k + 1) * hidden, now] = (
                grad_active * up * (sig * (1.0 + gate * (1.0 - sig)))
            ).astype(bf16)
            back_ref[(2 * k + 1) * hidden : (2 * k + 2) * hidden, now] = (
                grad_active * silu
            ).astype(bf16)

    columns = keep_ref.shape[3]
    blocks = width // columns
    ins = pair * 2 * hidden
    for at in range(0, pair * 3 * hidden, pair * hidden):
        if at < ins:
            total = jnp.dot(
                back_ref[at : at + pair * hidden], rows_ref[...], preferred_element_type=f32
            )
        else:
            total = jnp.dot(mixed_ref[...], grad_ref[:, :width], preferred_element_type=f32)
        total = total.astype(bf16)
        if blocks == 1:
            keep_ref[0, 0, at : at + pair * hidden] = total
            continue
        for c in range(blocks):
            apart = c ^ lax.axis_index("dp")
            part = total[:, c * columns : (c + 1) * columns]

            @pl.when(apart % 2 == 0)
            def _():
                keep_ref[0, apart // 2, at : at + pair * hidden] = part

            @pl.when(apart % 2 == 1)
            def _():
                give_refs[0][0, apart // 2, at : at + pair * hidden] = part

    if is_last:

        @pl.when(pl.program_id(0) == pl.num_programs(0) - 1)
        def _():
            gates, terms = gates_ref[...], terms_ref[...]
            logits = gates * (terms - jnp.sum(gates * terms, axis=0, keepdims=True))
            high = logits.astype(bf16)
            rows = logits.shape[0]
            logits_ref[:rows] = high
            logits_ref[rows:] = (logits - high.astype(f32)).astype(bf16)
            both = jnp.dot(logits_ref[...], rows_ref[...], preferred_element_type=f32)
            router_grad_ref[...] = both[:rows] + both[rows:]


def experts(
    first, count, blocks, rows_two, plane_grad, gates_or_router, w_in, w_out, earlier=(), after=()
):
    local_experts, _, hidden, width = w_in.shape
    tokens = rows_two.shape[0]
    pair = 2 if local_experts % 2 == 0 else 1
    pairs = local_experts // pair
    gate_rows = -(-local_experts * lax.axis_size("ep") // 8) * 8
    is_last = first + count == pairs
    spread = (max(blocks // 2, 1), pair * 3 * hidden, width // blocks)
    given = 1 if blocks > 1 else 0

    def whole(array):
        return pl.BlockSpec(array.shape, lambda i: (0,) * array.ndim, pipeline_mode=pl.Buffered(1))

    in_specs = [
        whole(rows_two),
        whole(plane_grad),
        whole(gates_or_router),
        pl.BlockSpec((pair, 2, hidden, width), lambda i: (i + first, 0, 0, 0)),
        pl.BlockSpec((pair, hidden, width), lambda i: (i + first, 0, 0)),
    ]
    if earlier:
        in_specs += [pl.BlockSpec(memory_space=pl.ANY)] * 2 + [whole(earlier[2])]
    in_specs += [pl.BlockSpec(memory_space=pl.ANY)] * len(after)
    out_shape = [
        jax.ShapeDtypeStruct((gate_rows, tokens), f32),
        jax.ShapeDtypeStruct((local_experts * 2 * hidden, tokens), bf16),
        jax.ShapeDtypeStruct((local_experts * hidden, tokens), bf16),
        jax.ShapeDtypeStruct((count, *spread), bf16),
    ] + [jax.ShapeDtypeStruct((count, *spread), bf16)] * given
    out_specs = [
        pl.BlockSpec((gate_rows, tokens), lambda i: (0, 0)),
        pl.BlockSpec((pair * 2 * hidden, tokens), lambda i: (i + first, 0)),
        pl.BlockSpec((pair * hidden, tokens), lambda i: (i + first, 0)),
        pl.BlockSpec((1, *spread), lambda i: (i, 0, 0, 0)),
    ] + [pl.BlockSpec((1, *spread), lambda i: (i, 0, 0, 0))] * given
    aliases = {}
    if first == 0:
        out_shape.insert(0, jax.ShapeDtypeStruct((gate_rows, tokens), f32))
        out_specs.insert(0, pl.BlockSpec((gate_rows, tokens), lambda i: (0, 0)))
    else:
        aliases = {5: 1 + 2 * is_last, 6: 2 + 2 * is_last}
    if is_last:
        out_shape = [
            jax.ShapeDtypeStruct((2 * gate_rows, tokens), bf16),
            jax.ShapeDtypeStruct((gate_rows, width), f32),
        ] + out_shape
        out_specs = [
            pl.BlockSpec((2 * gate_rows, tokens), lambda i: (0, 0)),
            pl.BlockSpec((gate_rows, width), lambda i: (0, 0)),
        ] + out_specs
    return pl.pallas_call(
        functools.partial(experts_kernel, first, local_experts, is_last, len(after)),
        grid=(count,),
        out_shape=out_shape,
        in_specs=in_specs,
        out_specs=out_specs,
        input_output_aliases=aliases,
        name=f"experts_{first}",
        cost_estimate=pl.CostEstimate(
            flops=10**6, bytes_accessed=10**6, transcendentals=0
        ),
        compiler_params=pltpu.CompilerParams(vmem_limit_bytes=44 * 2**20),
    )(rows_two, plane_grad, gates_or_router, w_in, w_out, *earlier, *after)


def rope_tables(length, head_size):
    half_size = head_size // 2
    frequency = jnp.exp(
        jnp.arange(half_size, dtype=f32) * (-2.0 * math.log(rope_base) / head_size)
    )
    angles = jnp.arange(length, dtype=f32)[:, None] * frequency[None, :]
    cosine, sine = jnp.cos(angles), jnp.sin(angles)
    one_cos = jnp.concatenate([cosine, cosine], axis=1)
    one_sin = jnp.concatenate([-sine, sine], axis=1)
    return (
        jnp.concatenate([one_cos, one_cos], axis=1),
        jnp.concatenate([one_sin, one_sin], axis=1),
        jnp.concatenate([one_cos, jnp.ones_like(one_cos)], axis=1),
        jnp.concatenate([one_sin, jnp.zeros_like(one_sin)], axis=1),
    )


def normalize(matrix):
    factor = lax.rsqrt(jnp.mean(matrix * matrix, axis=-1, keepdims=True) + eps_norm)
    return (matrix * factor, factor)


def norm_back(grad_normed, normed_hat, factor, gain):
    grad_hat = grad_normed * gain
    grad_inner = jnp.mean(grad_hat * normed_hat, axis=-1, keepdims=True)
    return (
        factor * (grad_hat - normed_hat * grad_inner),
        jnp.sum(grad_normed * normed_hat, axis=0),
    )


tail_late = list(
    dict(
        got_a=0, got_b=0, w_output=0, q=0, kv=0, w_query=0, keyval=0, rows=0, attended=0
    )
)
tail_first = list(
    dict(
        back=0, w_up=0
    )
)
tail_last = list(
    dict(
        mixed=0, w_down=0
    )
)
tail_held = list(
    dict(
        keep_a=0, keep_b=0, keep_c=0, keep_rest=0, give_c=0, give_rest=0
    )
)
tail_near = list(
    dict(
        x_mid=0, grad=0, x=0, gains=0, router=0, router_rows=0, logits=0, total=0, row=0, cosine=0,
        sine=0, kcosine=0, ksine=0
    )
)
tail_out = list(
    dict(
        kept=0, got=0, attn_kept=0, attn_got=0, block_out=0, grad_input=0, small=0
    )
)
tail_scratch = list(
    dict(
        backs=0, ups=0, stage=0, came1=0, give2=0, mine=0, twins=0, arrived=0, passed=0, outbox=0,
        sums=0, bias=0, turned=0, kv_grad=0, heads=0, pre=0, own_w=0, twin_w=0, twin_came=0,
        w_came=0, w_give=0, quarters=0, small_came=0
    )
)
tail_sems = list(
    dict(
        late_sem=0, part_sem=0, stage_sem=0, z1_s=0, z1_r=0, z2_s=0, z2_r=0, p_s=0, p_r=0, g_s=0,
        g_r=0, o_s=0, o_r=0, h_s=0, h_r=0, w_s=0, w_r=0, s_s=0, s_r=0
    )
)


def tail_kernel(size, scale, *refs):
    names = tail_near + tail_late + tail_first + tail_last + tail_held + tail_out + ["l_" + n for n in tail_late]
    names = names + tail_scratch + tail_sems
    r = types.SimpleNamespace(**dict(zip(names, refs, strict=True)))
    d, e, t = lax.axis_index("dp"), lax.axis_index("ep"), lax.axis_index("tp")
    near, far, twin = {"tp": t ^ 1}, {"tp": t ^ 2}, {"ep": 1 - e}
    next_z, far_z = {"dp": d ^ 1}, {"dp": d ^ 2}
    rows, width = r.x_mid.shape
    half = rows // 2
    first, second = pl.ds(0, half), pl.ds(half, half)
    pairs = r.kept.shape[0]
    greet((near, far, twin, next_z, far_z))

    loads = {}
    for k, name in enumerate(tail_late):
        loads[name] = pltpu.make_async_copy(getattr(r, name), getattr(r, "l_" + name), r.late_sem.at[k])

    def late(name):
        if name in loads:
            loads.pop(name).wait()
        return getattr(r, "l_" + name)

    def link(name):
        send_sem, recv_sem = getattr(r, name + "_s"), getattr(r, name + "_r")

        def send(src, dst, k, device):
            copy = pltpu.make_async_remote_copy(
                src, dst, send_sem.at[k], recv_sem.at[k], device_id=device, device_id_type=MESH
            )
            copy.start()
            return copy

        return send

    unsent = []

    z1, z2 = link("z1"), link("z2")
    over1, over2, stages = {}, {}, {}

    units = r.kept.shape[1]
    pieces = [(n, pl.ds(0, units)) for n in range(pairs - 1)]
    pieces += [(pairs - 1, pl.ds(at, units // 2)) for at in (0, units // 2)]

    def start1(k):
        n, cut = pieces[k]
        over1[k] = [
            z1(
                (r.give_c.at[0] if n == 2 else r.give_rest.at[n - 3]).at[side, cut],
                r.came1.at[n - 2, side, cut],
                2 * (k - 2) + side,
                next_z,
            )
            for side in (1, 0)
        ]

    def prepare(k):
        n, cut = pieces[k]
        kept = (r.keep_a, r.keep_b, r.keep_c)[n].at[0] if n < 3 else r.keep_rest.at[n - 3]
        stages[k] = pltpu.make_async_copy(kept.at[:, cut], r.stage.at[:, cut], r.stage_sem)
        stages[k].start()

    def add1(k):
        n, cut = pieces[k]
        if n < 2:
            came = late(("got_a", "got_b")[n])
        else:
            for copy in over1[k]:
                copy.wait_recv()
            unsent.extend(over1[k])
            came = r.came1.at[n - 2]
        stages[k].wait()
        r.give2[n, cut] = (
            r.stage[1, cut].astype(f32) + came[1, cut].astype(f32)
        ).astype(bf16)
        over2[k] = z2(r.give2.at[n, cut], r.got.at[n, cut], k, far_z)
        r.kept[n, cut] = (r.stage[0, cut].astype(f32) + came[0, cut].astype(f32)).astype(bf16)
        if k + 1 < len(pieces):
            prepare(k + 1)

    def added(to, index, *others):
        total = to[index].astype(f32)
        for other in others:
            total += other.astype(f32)
        return total

    def scatter(send, bring, number, between):
        mine, arrived, passed = r.mine, r.arrived.at[number], r.passed.at[number]
        bring(3)
        a_on = send(mine.at[3, first], arrived.at[0, 0], 4, near)
        b_on = send(mine.at[3, second], arrived.at[1, 0], 5, far)
        bring(1)
        a_own = send(mine.at[1, first], arrived.at[0, 1], 6, near)
        bring(2)
        b_own = send(mine.at[2, second], arrived.at[1, 1], 7, far)
        bring(0)
        between()
        a_on.wait_recv()
        mine[2, first] = added(mine, (2, first), arrived[0, 0]).astype(bf16)
        a_last = send(mine.at[2, first], passed.at[0], 8, far)
        b_on.wait_recv()
        mine[1, second] = added(mine, (1, second), arrived[1, 0]).astype(bf16)
        b_last = send(mine.at[1, second], passed.at[1], 9, near)
        a_own.wait_recv()
        b_own.wait_recv()
        a_last.wait_recv()
        r.sums[first] = added(mine, (0, first), arrived[0, 1], passed[0])
        b_last.wait_recv()
        r.sums[second] = added(mine, (0, second), arrived[1, 1], passed[1])
        for copy in (a_on, b_on, a_own, b_own, a_last, b_last):
            copy.wait_send()

    def nothing():
        pass

    plane = rows * lax.axis_size("tp")

    def scatter_all(send, make, number, between):
        order = (3, 1, 2, 0)
        twins_sent = {}

        def compute(k):
            block = rows_at((1 - e) * plane + (t ^ k) * rows, rows)
            r.outbox[k] = make(block)
            twins_sent[k] = send(r.outbox.at[k], r.twins.at[number // 2, k], k, twin)
            r.mine[k] = make(rows_at(e * plane + (t ^ k) * rows, rows))

        def bring(k):
            at = order.index(k)
            if at + 1 < 4:
                compute(order[at + 1])
            twins_sent[k].wait_recv()
            r.mine[k] = added(r.mine, k, r.twins[number // 2, k]).astype(bf16)

        compute(order[0])
        scatter(send, bring, number, between)
        for copy in twins_sent.values():
            copy.wait_send()

    start1(2)
    backs, ups = r.backs, r.ups
    for copy in list(loads.values())[:2]:
        copy.start()
    prepare(0)
    firsts = [
        pltpu.make_async_copy(a, place, r.part_sem.at[k])
        for k, (a, place) in enumerate(((r.back, backs), (r.w_up, ups)))
    ]
    for copy in firsts + list(loads.values())[2:]:
        copy.start()
    add1(0)
    add1(1)
    for copy in firsts:
        copy.wait()

    def rows_back(block):
        return (
            dot(backs[:, block], ups[...], (0, 0))
            + dot(r.logits[:, block], r.router_rows[...], (0, 0))
        ).astype(bf16)

    scatter_all(link("p"), rows_back, 0, nothing)

    def norm_back_in(grad_normed, values, gain):
        factor = lax.rsqrt(jnp.mean(values * values, axis=-1, keepdims=True) + eps_norm)
        hat = values * factor
        grad_hat = grad_normed * gain
        inner = jnp.mean(grad_hat * hat, axis=-1, keepdims=True)
        return (
            factor * (grad_hat - hat * inner),
            jnp.sum(grad_normed * hat, axis=0, keepdims=True),
        )

    small, lanes = r.quarters, width // 4
    experts_all = r.router.shape[0] - 4

    def small_put(values, at):
        for k in range(4):
            small[k, at] = values[:, k * lanes : (k + 1) * lanes]

    small_put(r.router[...], slice(0, experts_all + 4))
    back, gain_grad = norm_back_in(r.sums[...], r.x_mid[...], r.gains[1:2])
    small_put(gain_grad, slice(experts_all, experts_all + 1))
    grad_mid = r.grad[...].astype(f32) + back
    r.grad_input[...] = grad_mid

    length = r.l_q.shape[0]
    whole = ups.at[:length]

    def place(tt, part, count):
        return ups.at[rows_at(tt * rows + part * half, count)]

    ups[rows_at(t * rows, rows), :] = grad_mid.astype(bf16)
    g = link("g")
    near_a = g(place(t, 0, half), place(t, 0, half), 0, near)
    far_b = g(place(t, 1, half), place(t, 1, half), 1, far)
    near_b = g(place(t, 1, half), place(t, 1, half), 2, near)
    far_a = g(place(t, 0, half), place(t, 0, half), 3, far)
    mixed = backs.at[: r.mixed.shape[0]]
    w_down = ups.at[length : length + r.w_down.shape[0]]
    lasts = [
        pltpu.make_async_copy(a, place_, r.part_sem.at[2 + k])
        for k, (a, place_) in enumerate(((r.mixed, mixed), (r.w_down, w_down)))
    ]
    for copy in lasts:
        copy.start()
    mask_into(r.bias, r.row)
    r.kv_grad[...] = jnp.zeros_like(r.kv_grad)
    near_a.wait_recv()
    on_a = g(place(t ^ 1, 0, half), place(t ^ 1, 0, half), 4, far)
    far_b.wait_recv()
    on_b = g(place(t ^ 2, 1, half), place(t ^ 2, 1, half), 5, near)
    for copy in (near_b, far_a, on_a, on_b):
        copy.wait_recv()
    unsent.extend((near_a, far_b, near_b, far_a, on_a, on_b))

    attention_back_steps(
        size,
        scale,
        whole,
        late("w_output"),
        late("q"),
        late("kv"),
        r.total,
        [r.cosine, r.sine, r.kcosine, r.ksine],
        r.pre, r.bias, r.turned, r.kv_grad, r.heads,
    )
    start1(3)
    q_width = r.l_q.shape[1]
    w_query, keyval = late("w_query"), late("keyval")

    def bring_heads(k):
        block = rows_at((t ^ k) * rows, rows)
        r.mine[k] = (
            dot(r.pre[block, :q_width], w_query[...], (1, 1))
            + dot(r.pre[block, q_width:], keyval[...], (1, 1))
        ).astype(bf16)

    w = link("w")
    twin_w = []

    def weights():
        attention_weights_kernel(
            late("rows"), r.pre, whole, late("attended"), r.own_w, r.twin_w
        )
        twin_w.append(w(r.twin_w, r.twin_came, 0, twin))
        add1(2)

    scatter(link("h"), bring_heads, 1, weights)
    back, gain_grad = norm_back_in(r.sums[...], r.x[...].astype(f32), r.gains[:1])
    small_put(gain_grad, slice(experts_all + 1, experts_all + 2))
    r.grad_input[...] = r.grad_input[...] + back

    twin_w[0].wait_recv()
    own_w = r.own_w
    w_copies = list(twin_w)
    for k in (1, 3):
        own_w[k] = added(own_w, k, r.twin_came[k]).astype(bf16)
        w_copies.append(w(own_w.at[k], r.w_came.at[k // 2], 1 + k // 2, next_z))
    for k in (0, 2):
        own_w[k] = added(own_w, k, r.twin_came[k]).astype(bf16)

    s = link("s")
    low, high = t % 2, t // 2 % 2
    two = [pl.ds((low ^ k) * 2, 2) for k in range(2)]
    one = [pl.ds(low * 2 + (high ^ k), 1) for k in range(2)]
    own, every = one[0], pl.ds(0, 4)
    small_plan = [
        (twin, every, every),
        (near, two[1], two[0]),
        (far, one[1], own),
        (next_z, own, own),
        (far_z, own, own),
        (far, own, one[1]),
        (near, two[0], two[1]),
    ]
    small_sent = {}

    def small_send(k):
        device, cut, _ = small_plan[k]
        small_sent[k] = s(small.at[cut], r.small_came.at[k, cut], k, device)

    def small_add(k):
        kept = small_plan[k][2]
        small_sent[k].wait()
        came = r.small_came[k, kept]
        small[kept] = small[kept] + came if k < 5 else came

    small_send(0)

    for copy in lasts:
        copy.wait()

    def mixed_rows(block):
        return dot(mixed[:, block], w_down[...], (0, 0)).astype(bf16)

    def third_sum():
        add1(3)
        start1(4)
        small_add(0)
        small_send(1)

    scatter_all(link("o"), mixed_rows, 2, third_sum)
    r.block_out[...] = (r.x_mid[...] + r.sums[...]).astype(bf16)

    small_add(1)
    small_send(2)
    small_add(2)
    small_send(3)
    for copy in w_copies[1:]:
        copy.wait_recv()
    r.w_give[...] = added(own_w, 2, r.w_came[1]).astype(bf16)
    w_copies.append(w(r.w_give, r.attn_got, 3, far_z))
    r.attn_kept[...] = added(own_w, 0, r.w_came[0]).astype(bf16)
    start1(5)
    small_add(3)
    small_send(4)
    add1(4)
    small_add(4)
    small_send(5)
    add1(5)
    small_add(5)
    small_send(6)
    small_add(6)
    for k in range(4):
        r.small[:, k * lanes : (k + 1) * lanes] = small[k]
    w_copies[-1].wait_recv()
    for k in range(len(pieces)):
        over2[k].wait()
    for copy in unsent + w_copies:
        copy.wait_send()


def tail(size, scale, named, collective_id):
    width = named.x_mid.shape[1]
    rows = named.x_mid.shape[0]
    length = named.q.shape[0]
    q_width, kv_width = named.q.shape[1], named.kv.shape[1]
    _, count, units, columns = named.keep_a.shape
    pairs = 3 + named.keep_rest.shape[0]
    block = (width // 8, 2 * q_width + kv_width)
    shape = jax.ShapeDtypeStruct
    outs = dict(
        kept=shape((pairs, units, columns), bf16),
        got=shape((pairs, units, columns), bf16),
        attn_kept=shape(block, bf16),
        attn_got=shape(block, bf16),
        block_out=shape((rows, width), bf16),
        grad_input=shape((rows, width), f32),
        small=shape(named.router.shape, f32),
    )
    scratch = dict(
        stage=((count, units, columns), bf16),
        came1=((pairs - 2, count, units, columns), bf16),
        give2=((pairs, units, columns), bf16),
        mine=((4, rows, width), bf16),
        twins=((2, 4, rows, width), bf16),
        arrived=((3, 2, 2, rows // 2, width), bf16),
        passed=((3, 2, rows // 2, width), bf16),
        outbox=((4, rows, width), bf16),
        sums=((rows, width), f32),
        backs=(named.back.shape, bf16),
        ups=(named.w_up.shape, bf16),
        bias=((length, length), f32),
        turned=((q_width, length), f32),
        kv_grad=((length, kv_width), f32),
        heads=((length, q_width), bf16),
        pre=((length, q_width + kv_width), bf16),
        own_w=((4, *block), bf16),
        twin_w=((4, *block), bf16),
        twin_came=((4, *block), bf16),
        w_came=((2, *block), bf16),
        w_give=(block, bf16),
        quarters=((4, named.router.shape[0], width // 4), f32),
        small_came=((7, 4, named.router.shape[0], width // 4), f32),
    )
    sems = dict(late_sem=len(tail_late), part_sem=4, z1=2 * (pairs - 1), z2=pairs + 1, p=10, g=6, o=10, h=10, w=4, s=7)
    dma = pltpu.SemaphoreType.DMA
    scratch_shapes = (
        [pltpu.VMEM(getattr(named, n).shape, getattr(named, n).dtype) for n in tail_late]
        + [pltpu.VMEM(*scratch[n]) for n in tail_scratch]
        + [dma((sems["late_sem"],)), dma((4,)), dma]
        + [dma((sems[n[:-2]],)) for n in tail_sems[3:]]
    )
    elsewhere, here = pl.BlockSpec(memory_space=pl.ANY), pl.BlockSpec(memory_space=pltpu.VMEM)
    ins = tail_near + tail_late + tail_first + tail_last + tail_held
    results = pl.pallas_call(
        functools.partial(tail_kernel, size, scale),
        out_shape=[outs[n] for n in tail_out],
        in_specs=[here] * len(tail_near) + [elsewhere] * (len(ins) - len(tail_near)),
        out_specs=[elsewhere if n in ("got", "attn_got") else here for n in tail_out],
        scratch_shapes=scratch_shapes,
        name="tail",
        cost_estimate=pl.CostEstimate(flops=10**9, bytes_accessed=10**6, transcendentals=0),
        compiler_params=pltpu.CompilerParams(
            collective_id=collective_id, has_side_effects=True, vmem_limit_bytes=60 * 2**20
        ),
    )(*(getattr(named, n) for n in ins))
    return types.SimpleNamespace(**dict(zip(tail_out, results)))


def place_pairs(kept, got, shapes):
    (_, _, hidden, columns), _ = shapes
    pairs, units, _ = kept.shape
    pair = units // (3 * hidden)
    ins = 2 * pair * hidden

    def body(kept_ref, got_ref, into_ref, out_ref):
        total = kept_ref[0].astype(f32) + got_ref[0].astype(f32)
        into_ref[...] = total[:ins].reshape(pair, 2, hidden, columns)
        out_ref[...] = total[ins:].reshape(pair, hidden, columns)

    block = pl.BlockSpec((1, units, columns), lambda i: (i, 0, 0))
    return pl.pallas_call(
        body,
        grid=(pairs,),
        out_shape=[jax.ShapeDtypeStruct(s, f32) for s in shapes],
        in_specs=[block, block],
        out_specs=[
            pl.BlockSpec((pair, 2, hidden, columns), lambda i: (i, 0, 0, 0)),
            pl.BlockSpec((pair, hidden, columns), lambda i: (i, 0, 0)),
        ],
        name="place_pairs",
        compiler_params=pltpu.CompilerParams(vmem_limit_bytes=24 * 2**20),
    )(kept, got)


def per_device(
    activations,
    segments,
    routes,
    attn_gain,
    w_query,
    key_value_weight,
    w_output,
    moe_gain,
    w_router,
    w_in,
    w_out,
    out_cotangent,
):
    row_count, width = activations.shape
    tp_count = lax.axis_size("tp")
    ep_count = lax.axis_size("ep")
    dp_count = lax.axis_size("dp")
    e_index = lax.axis_index("ep")
    seq_len = row_count * tp_count
    head_size = key_value_weight.shape[2] // 2
    kv_heads = key_value_weight.shape[1]
    q_heads = w_query.shape[1] // head_size
    heads_per_group = q_heads // kv_heads
    top_count = routes.shape[1]
    expert_count = w_router.shape[1]
    local_experts = w_in.shape[0]
    hidden = w_in.shape[2]
    score_scale = 1.0 / math.sqrt(head_size)

    lanes = jnp.arange(128, dtype=jnp.int32)
    used = functools.reduce(
        jnp.logical_or, [routes[:, k : k + 1] == lanes[None, :] for k in range(routes.shape[1])]
    ).astype(bf16)
    plane_grad = lax.all_gather(
        jnp.concatenate([out_cotangent, used], axis=1), ("ep", "tp"), axis=0, tiled=True
    )

    tables = rope_tables(seq_len, head_size)
    keyval_flat = key_value_weight.reshape(width, kv_heads * 2 * head_size)
    doc_row = segments.astype(f32)
    q_width, kv_width = q_heads * head_size, 2 * kv_heads * head_size
    gains = jnp.concatenate([attn_gain[None], moe_gain[None], jnp.zeros((6, width), f32)])
    full_rows, query_rows, keyval_rows, attended, log_total, x_mid, rows_two = front(
        head_size,
        score_scale,
        activations,
        gains,
        w_query,
        keyval_flat,
        w_output,
        doc_row,
        tables,
        0,
    )

    pair = 2 if local_experts % 2 == 0 else 1
    pairs = local_experts // pair
    columns = width // dp_count
    in_order = dp_count == 4 and ep_count == 2 and tp_count == 4 and columns % 128 == 0 and pairs == 5
    blocks = dp_count if in_order else 1
    gates = jnp.pad(w_router, ((0, 0), (0, 128 - expert_count)))
    keeps, gives, came, earlier = [], [], [], ()
    calls = ((0, 1), (1, 1), (2, 1), (3, pairs - 3)) if in_order else ((0, 1), (1, pairs - 1))
    for start, count in calls:
        after = (came[0],) if start == 3 else ()
        results = experts(
            start, count, blocks, rows_two, plane_grad, gates, w_in, w_out, earlier, after
        )
        if start == 0:
            gates, *results = results
        if start + count == pairs:
            logits, grad_w_router, *results = results
        terms, back, mixed, keep, *give = results
        earlier = (back, mixed, terms)
        keeps.append(keep)
        gives += give
        if in_order and start < 2:
            came.append(exchanged(give[0][0], 1))

    gate_rows = gates.shape[0]
    router_rows = jnp.pad(w_router.T, ((0, gate_rows - expert_count), (0, 0)))
    router_rows = jnp.concatenate([router_rows] * 2)
    all_width = 2 * q_width + kv_width
    shapes = [(local_experts, 2, hidden, columns), (local_experts, hidden, columns)]
    if in_order:
        done = tail(
            head_size,
            score_scale,
            types.SimpleNamespace(
                back=back,
                w_up=w_in.reshape(-1, width),
                logits=logits,
                router_rows=router_rows,
                keep_a=keeps[0],
                keep_b=keeps[1],
                keep_c=keeps[2],
                give_c=gives[2],
                keep_rest=keeps[3],
                give_rest=gives[3],
                got_a=came[0],
                got_b=came[1],
                x_mid=x_mid,
                grad=out_cotangent,
                x=activations,
                gains=gains,
                router=grad_w_router,
                total=log_total,
                row=doc_row,
                cosine=tables[0],
                sine=tables[1],
                kcosine=tables[2],
                ksine=tables[3],
                w_output=w_output,
                q=query_rows,
                kv=keyval_rows,
                w_query=w_query,
                keyval=keyval_flat,
                rows=full_rows,
                attended=attended,
                mixed=mixed,
                w_down=w_out.reshape(-1, width),
            ),
            3,
        )
        block_out, grad_input, small = done.block_out, done.grad_input, done.small
        grad_w_in, grad_w_out = place_pairs(done.kept, done.got, shapes)
        attn_sum = done.attn_kept.astype(f32) + done.attn_got.astype(f32)
    else:
        grad_rows_two = dot(back, w_in.reshape(-1, width), (0, 0)) + dot(logits, router_rows, (0, 0))
        grad_normed_two = scatter_sum(grad_rows_two.astype(bf16), True, 3)
        hat_two, factor_two = normalize(x_mid)
        grad_from_moe, grad_moe_gain = norm_back(grad_normed_two, hat_two, factor_two, moe_gain)
        grad_mid = out_cotangent.astype(f32) + grad_from_moe
        grad_full = gather(grad_mid.astype(bf16), False, 4)

        heads_part, grad_pre = local_call(
            functools.partial(attention_back_kernel, head_size, score_scale),
            "attention_back",
            [
                jax.ShapeDtypeStruct((seq_len, width), bf16),
                jax.ShapeDtypeStruct((seq_len, q_width + kv_width), bf16),
            ],
            [
                pltpu.VMEM((seq_len, seq_len), f32),
                pltpu.VMEM((q_width, seq_len), f32),
                pltpu.VMEM((seq_len, kv_width), f32),
                pltpu.VMEM((seq_len, q_width), bf16),
            ],
            (
                grad_full,
                w_output,
                query_rows,
                keyval_rows,
                log_total,
                w_query,
                keyval_flat,
                        doc_row,
                *tables,
            ),
        )
        attn_weights = local_call(
            attention_weights_kernel,
            "attention_weights",
            [jax.ShapeDtypeStruct((width, all_width), bf16)],
            [],
            (full_rows, grad_pre, grad_full, attended),
        )
        grad_normed_one = scatter_sum(heads_part, False, 6)
        hat_one, factor_one = normalize(activations.astype(f32))
        grad_from_attn, grad_attn_gain = norm_back(grad_normed_one, hat_one, factor_one, attn_gain)
        grad_input = grad_mid + grad_from_attn

        expert_part = dot(mixed, w_out.reshape(-1, width), (0, 0)).astype(bf16)
        block_out = (x_mid + scatter_sum(expert_part, True, 5)).astype(bf16)

        halves = attn_weights[0].reshape(dp_count, ep_count, -1, all_width)
        kept = lax.dynamic_index_in_dim(halves, e_index, 1, keepdims=False)
        given = lax.dynamic_index_in_dim(halves, 1 - e_index, 1, keepdims=False)
        got = lax.ppermute(given, "ep", [(0, 1), (1, 0)])
        attn_sum = halved_over_dp((kept.astype(f32) + got.astype(f32)).astype(bf16))
        summed = []
        for keep in keeps:
            for k in range(keep.shape[0]):
                parts = jnp.moveaxis(keep[k].reshape(-1, dp_count, columns), 1, 0)
                summed.append(halved_over_dp(parts))
        summed = jnp.stack(summed)
        ins = pair * 2 * hidden
        grad_w_in = summed[:, :ins].reshape(shapes[0])
        grad_w_out = summed[:, ins:].reshape(shapes[1])
        small = summed_everywhere(
            jnp.concatenate(
                [grad_w_router[:expert_count], grad_moe_gain[None], grad_attn_gain[None]]
            )
        )
    grad_w_query = attn_sum[:, :q_width]
    grad_w_keyval = attn_sum[:, q_width : q_width + kv_width].reshape(-1, kv_heads, 2 * head_size)
    grad_w_output = attn_sum[:, q_width + kv_width :].T
    grad_w_router = small[:expert_count].T
    grad_moe_gain, grad_attn_gain = small[expert_count], small[expert_count + 1]
    return (
        block_out,
        grad_input,
        grad_attn_gain,
        grad_w_query,
        grad_w_keyval,
        grad_w_output,
        grad_moe_gain,
        grad_w_router,
        grad_w_in,
        grad_w_out,
    )


def solution(mesh):
    return jax.shard_map(
        per_device,
        mesh=mesh,
        in_specs=(
            P(("dp", "ep", "tp"), None),
            P(("dp", "ep"), None),
            P(("dp", "ep", "tp"), None),
            P(),
            P(None, "tp"),
            P(None, "tp", None),
            P("tp", None),
            P(),
            P(),
            P("ep", None, "tp", None),
            P("ep", "tp", None),
            P(("dp", "ep", "tp"), None),
        ),
        out_specs=(
            P(("dp", "ep", "tp"), None),
            P(("dp", "ep", "tp"), None),
            P(),
            P(("dp", "ep"), "tp"),
            P(("dp", "ep"), "tp", None),
            P("tp", ("dp", "ep")),
            P(),
            P(),
            P("ep", None, "tp", "dp"),
            P("ep", "tp", "dp"),
        ),
        check_vma=False,
    )
```
